256 devices in a mesh: section: 8 (over z_hi, core), row: 4 (over x), col: 8 (over y, z_lo).
Axes of the slice: x: 4, y: 4, z: 8 (z_hi: 4, z_lo: 2; z = z_hi * 2 + z_lo), core: 2. Of those that a mesh axis runs over, the one named last changes fastest.
Arguments:
- boundary_grad: bfloat16 [8, 1024, 12288], P('section', 'col', 'row'), may hold values from -6 to 6
- w_out: bfloat16 [8, 6144, 12288], P('section', 'col', 'row'), may hold values from -0.078125 to 0.078125
- context: bfloat16 [8, 1024, 6144], P('section', 'row', 'col'), may hold values from -6 to 6
- queries: bfloat16 [8, 1024, 6144], P('section', 'row', 'col'), may hold values from -24 to 24
- keys: bfloat16 [8, 1024, 6144], P('section', 'row', 'col'), may hold values from -24 to 24
- values: bfloat16 [8, 1024, 6144], P('section', 'row', 'col'), may hold values from -6 to 6
Outputs:
- grad_w_out: bfloat16 [8, 6144, 12288], P('section', 'col', 'row')
- grad_queries: bfloat16 [8, 1024, 6144], P('section', 'row', 'col')
- grad_keys: bfloat16 [8, 1024, 6144], P('section', 'row', 'col')
- grad_values: bfloat16 [8, 1024, 6144], P('section', 'row', 'col')
The draws below stay inside these ranges and needn't reach their ends.
All inputs are finite; a program needn't handle non-finite values.
Results may differ from the reference program's by a relative error of at most 0.007.
Values may be sent and summed in bfloat16 or wider, within the bound.
A program may use at most 128 MiB of HBM per device.

```python
import jax
import jax.numpy as jnp

D = 12288
HEAD_DIM = 128
HEADS = 48
TOKENS = 1024
SECTIONS = 8
INNER = 6144


def draw_queries(key, part):
    key = jax.random.fold_in(key, 11)
    shape = (SECTIONS, TOKENS, HEADS, HEAD_DIM)
    result = jnp.clip(jax.random.normal(key, shape, jnp.float32), -6.0, 6.0)
    return result.reshape(SECTIONS, TOKENS, HEADS * HEAD_DIM).astype(jnp.bfloat16)


def draw_keys(key, part):
    key = jax.random.fold_in(key, 23)
    shape = (SECTIONS, TOKENS, HEADS, HEAD_DIM)
    result = jnp.clip(jax.random.normal(key, shape, jnp.float32), -6.0, 6.0)
    return result.reshape(SECTIONS, TOKENS, HEADS * HEAD_DIM).astype(jnp.bfloat16)


def steps_of(rng, extent, pieces, smallest, largest):
    def one(dim, blocks):
        heights = jax.random.uniform(jax.random.fold_in(jax.random.fold_in(rng, 6), dim), (blocks,), jnp.float32, smallest / len(pieces), largest / len(pieces))
        return jnp.repeat(jnp.exp(heights), extent[dim] // blocks).reshape((-1,) + (1,) * (len(extent) - dim - 1))

    gain = one(*pieces[0])
    for cut in pieces[1:]:
        gain = gain * one(*cut)
    return gain


def scatter_about(own_key, extent, scale, most, cuts=(), held_as=jnp.bfloat16):
    loudness = steps_of(own_key, extent, cuts, -0.22, 0.18) if cuts else 1.0
    values = jax.random.normal(own_key, extent, jnp.float32) * scale * loudness
    return jnp.minimum(jnp.maximum(values, -most), most).astype(held_as)


def setup_inputs(seed: int = 0) -> dict:
    seeds = jax.random.split(jax.random.key(seed), 7)
    boundary_grad = scatter_about(seeds[0], (SECTIONS, TOKENS, D), 1.0, 6.0, ((0, 8), (1, 8), (2, 4)))
    w_out = scatter_about(seeds[1], (SECTIONS, INNER, D), INNER ** -0.5, 0.078125, ((0, 8), (1, 8), (2, 4)))
    context = scatter_about(seeds[2], (SECTIONS, TOKENS, INNER), 1.0, 6.0, ((0, 8), (1, 4), (2, 8)))
    queries = draw_queries(jax.random.fold_in(seeds[6], 71), 0)
    keys = draw_keys(jax.random.fold_in(seeds[6], 71), 0)
    values = scatter_about(seeds[5], (SECTIONS, TOKENS, INNER), 1.0, 6.0, ((0, 8), (1, 4), (2, 8)))
    return {"boundary_grad": boundary_grad, "w_out": w_out, "context": context, "queries": queries, "keys": keys, "values": values}


def attend_backward(query, key_rows, value_rows, output, grad_out):
    count = query.shape[0]
    heads = query.shape[1] // HEAD_DIM
    scale = HEAD_DIM ** -0.5
    qh = query.astype(jnp.float32).reshape(count, heads, HEAD_DIM)
    kh = key_rows.astype(jnp.float32).reshape(count, heads, HEAD_DIM)
    vh = value_rows.astype(jnp.float32).reshape(count, heads, HEAD_DIM)
    oh = output.astype(jnp.float32).reshape(count, heads, HEAD_DIM)
    gh = grad_out.astype(jnp.float32).reshape(count, heads, HEAD_DIM)
    scores = jnp.einsum("qhd,khd->hqk", qh, kh) * scale
    positions = jnp.arange(count, dtype=jnp.int32)
    allowed = positions[:, None] >= positions[None, :]
    scores = jnp.where(allowed[None], scores, -jnp.inf)
    top = jnp.max(scores, axis=2, keepdims=True)
    weights = jnp.exp(scores - top)
    probs = weights / jnp.sum(weights, axis=2, keepdims=True)
    delta = jnp.einsum("qhd,qhd->hq", gh, oh)
    dprobs = jnp.einsum("qhd,khd->hqk", gh, vh)
    dscores = probs * (dprobs - delta[:, :, None])
    probs_b = probs.astype(jnp.bfloat16).astype(jnp.float32)
    dscores_b = dscores.astype(jnp.bfloat16).astype(jnp.float32)
    grad_v = jnp.einsum("hqk,qhd->khd", probs_b, gh)
    grad_q = jnp.einsum("hqk,khd->qhd", dscores_b, kh) * scale
    grad_k = jnp.einsum("hqk,qhd->khd", dscores_b, qh) * scale
    width = heads * HEAD_DIM
    return (grad_q.reshape(count, width).astype(jnp.bfloat16),
            grad_k.reshape(count, width).astype(jnp.bfloat16),
            grad_v.reshape(count, width).astype(jnp.bfloat16))


def reference(boundary_grad, w_out, context, queries, keys, values):
    incoming = jnp.concatenate([boundary_grad[1:], boundary_grad[-1:]], axis=0)
    weight_grads, query_grads, key_grads, value_grads = [], [], [], []
    for section in range(SECTIONS):
        arriving = incoming[section]
        grad_context = jnp.dot(arriving, w_out[section].T, preferred_element_type=jnp.float32).astype(jnp.bfloat16)
        weight_grads.append(jnp.dot(context[section].T, arriving, preferred_element_type=jnp.float32).astype(jnp.bfloat16))
        grad_q, grad_k, grad_v = attend_backward(queries[section], keys[section], values[section], context[section], grad_context)
        query_grads.append(grad_q)
        key_grads.append(grad_k)
        value_grads.append(grad_v)
    return (jnp.stack(weight_grads), jnp.stack(query_grads), jnp.stack(key_grads), jnp.stack(value_grads))
```

```python
import jax
import jax.numpy as jnp
from jax import lax
from jax.experimental import pallas as pl
from jax.experimental.pallas import tpu as pltpu
from jax.sharding import PartitionSpec as P

HEAD = 128
SCALE = HEAD ** (-0.5)
MESH = pl.DeviceIdType.MESH
BF16 = jnp.bfloat16
F32 = jnp.float32

ROWS = 256
PIECE = 128
HALF = 64
KEYS = 512
FEAT = 3072
WIDTH = 768
PAIR = 384
SLAB = 256
TILE = 512

ORDER0 = [
    "E1", "E0", "e0l", "q", "e0r", "k", "e1l", "cB", "e1r", "cA", "kf", "f0", "f1", "qf", "cfB", "zs1", "P0", "P1",
    "cfA", "zs0", "t0", "p0", "g0a", "zr1", "t1", "zr1r", "P2", "v", "zr0l", "t2", "s0", "g0b", "f3", "vf", "zr0",
    "p1", "f2", "t3", "P3", "a0", "s1", "p2", "g1a", "p3", "g1b", "s2", "a1", "g2a", "g2b", "dq", "s3", "a2", "g3a",
    "dqf", "g3b", "a3", "dk", "dv", "dql",
]
ORDER1 = [
    "E1", "q", "cB", "E0", "e0l", "e0r", "k", "cA", "e1l", "e1r", "kf", "f0", "f1", "qf", "zs1", "P0", "cfB", "P1",
    "cfA", "zs0", "t0", "p0", "zr1r", "g0a", "zr1", "t1", "v", "P2", "zr0l", "s0", "g0b", "f3", "zr0", "p1", "t2",
    "f2", "vf", "P3", "a0", "s1", "p2", "g1a", "p3", "g1b", "s2", "t3", "a1", "g2a", "g2b", "dq", "s3", "a2", "g3a",
    "dqf", "g3b", "a3", "dk", "dv", "dql",
]


def dot(a, b, ca, cb):
    return lax.dot_general(a, b, (((ca,), (cb,)), ((), ())), preferred_element_type=F32)


def kernel(
    bg, wo, cx, qs, ks, vs,
    gw, gq, gk, gv,
    inc, wv, ctx, ctxt, acc, q2, k2, v2, qg, part, partb, got_a, got_b, sumb, pt, linv, dout,
    dqa, dka, dva, dqb, dkb, dvb, stage,
    send, recv, lsem, esem, osem,
):
    s = lax.axis_index("section")
    x = lax.axis_index("row")
    c = lax.axis_index("col")
    y = c // 2
    z = c - 2 * y
    core = s - 2 * (s // 2)
    y_r = lax.rem(y + 1 + 2 * core, 4)
    y_l = lax.rem(y + 3 + 2 * core, 4)
    y_o = lax.rem(y + 2, 4)
    zp = 1 - z
    pair = x // 2
    par = x - 2 * pair
    par_b = 1 - par
    x_a = 3 - x
    x_b = 2 * pair + par_b
    x_c = lax.rem(x + 2, 4)
    dev_r = (s, x, 2 * y_r + z)
    dev_l = (s, x, 2 * y_l + z)
    dev_z = (s, x, 2 * y + zp)
    dev_a = (s, x_a, c)
    dev_b = (s, x_b, c)
    has_prev = s > 0
    has_next = s < 7
    dev_prev = (jnp.maximum(s - 1, 0), x, c)
    dev_next = (jnp.minimum(s + 1, 7), x, c)

    barrier = pltpu.get_barrier_semaphore()
    for dev in (dev_r, dev_l, dev_z, dev_a, dev_b):
        pl.semaphore_signal(barrier, inc=1, device_id=dev, device_id_type=MESH)

    @pl.when(has_prev)
    def _():
        pl.semaphore_signal(barrier, inc=1, device_id=dev_prev, device_id_type=MESH)

    @pl.when(has_next)
    def _():
        pl.semaphore_signal(barrier, inc=1, device_id=dev_next, device_id_type=MESH)

    pl.semaphore_wait(barrier, 5 + has_prev.astype(jnp.int32) + has_next.astype(jnp.int32))

    def m128(v):
        return pl.multiple_of(v, 128)

    def slab_of(xx):
        p = xx // 2
        return pl.ds(m128(PAIR * p + HEAD * (xx - 2 * p)), SLAB)

    def full_of(xx):
        p = xx // 2
        return pl.ds(m128(PAIR * p + 2 * HEAD * (xx - 2 * p)), HEAD)

    def pair_of(xx):
        return pl.ds(m128(PAIR * (xx // 2)), PAIR)

    own_slab = slab_of(x)
    in_pair = pl.ds(m128(HEAD * par), SLAB)
    in_pair_b = pl.ds(m128(HEAD * par_b), SLAB)
    own_full = pl.ds(m128(HEAD * par), HEAD)

    def slot(yy, zz, h):
        half = yy // 2
        return inc.at[2 * zz + half, pl.ds(pl.multiple_of(PIECE * (yy - 2 * half) + HALF * h, HALF), HALF)]

    groups = [2 * z + y // 2, 2 * z + 1 - y // 2, 2 * zp + y // 2, 2 * zp + 1 - y // 2]

    moves = {}

    def move(tag, src, there, here, dev):
        moves[tag] = (len(moves), src, there, here, dev)

    for h in range(2):
        move("E%d" % h, bg.at[0, pl.ds(HALF * h, HALF)], slot(y, z, h), slot(y, z, h), dev_prev)
        move("z%d" % h, slot(y, z, h), slot(y, z, h), slot(y, zp, h), dev_z)
        move("l_own%d" % h, slot(y, z, h), slot(y, z, h), slot(y_l, z, h), dev_r)
        move("r_own%d" % h, slot(y, z, h), slot(y, z, h), slot(y_r, z, h), dev_l)
        move("l_oth%d" % h, slot(y, zp, h), slot(y, zp, h), slot(y_l, zp, h), dev_r)
        move("r_oth%d" % h, slot(y, zp, h), slot(y, zp, h), slot(y_r, zp, h), dev_l)
    move("o_own0", slot(y_l, z, 0), slot(y_l, z, 0), slot(y_o, z, 0), dev_r)
    move("o_own1", slot(y_r, z, 1), slot(y_r, z, 1), slot(y_o, z, 1), dev_l)
    move("o_oth1", slot(y_r, zp, 1), slot(y_r, zp, 1), slot(y_o, zp, 1), dev_l)
    move("o_oth0", slot(y_o, z, 0), slot(y_o, z, 0), slot(y_o, zp, 0), dev_z)
    def block(xx, start=0, size=ROWS):
        half = xx // 2
        return half, pl.ds(m128(ROWS * (xx - 2 * half) + start), size)

    for n, a, b in (("k", ks, k2), ("q", qs, q2), ("v", vs, v2)):
        to, from_a, from_b, from_c = block(x), block(x_a), block(x_b), block(x_c)
        move(n + "A", a.at[0, :, pair_of(x_a)], b.at[to], b.at[from_a], dev_a)
        move(n + "B", a.at[0, :, slab_of(x_b)], b.at[(*to, in_pair_b)], b.at[(*from_b, in_pair)], dev_b)
        move(n + "C", b.at[(*from_a, in_pair_b)], b.at[(*from_a, in_pair_b)], b.at[(*from_c, in_pair)], dev_b)
    move("cA", cx.at[0], ctx.at[x], ctx.at[x_a], dev_a)
    move("cB", cx.at[0], ctx.at[x], ctx.at[x_b], dev_b)
    lo, hi = pl.ds(0, ROWS // 2), pl.ds(ROWS // 2, ROWS // 2)
    move("cC0", ctx.at[x_a, lo], ctx.at[x_a, lo], ctx.at[x_c, lo], dev_b)
    move("cC1", ctx.at[x_b, hi], ctx.at[x_b, hi], ctx.at[x_c, hi], dev_a)
    for k in range(4):
        move("rsA%d" % k, partb.at[k, :, pair_of(x_a)], got_a.at[k], got_a.at[k], dev_a)
        move("rsB%d" % k, sumb.at[k], got_b.at[k], got_b.at[k], dev_b)

    def move_out(n, src, dst, start, size, where):
        rows = pl.ds(start, size)
        hop = stage.at[where, pl.ds(0, size)]
        to_a, to_b, to_c = (block(xx, start, size) for xx in (x_a, x_b, x_c))
        move(n + "1", src.at[(*to_c, own_full)], hop, hop, dev_b)
        move(n + "A", src.at[to_a], dst.at[0, rows, own_slab], dst.at[0, rows, slab_of(x_a)], dev_a)
        move(n + "B", src.at[(*to_b, own_full)], dst.at[0, rows, full_of(x)], dst.at[0, rows, full_of(x_b)], dev_b)
        move(n + "C", hop, dst.at[0, rows, full_of(x_b)], dst.at[0, rows, full_of(x_c)], dev_a)

    move_out("dk", dkb, gk, 0, ROWS, 0)
    move_out("dv", dvb, gv, 0, ROWS, 1)
    move_out("dqe", dqb, gq, m128(PIECE * z), PIECE, 2)
    move_out("dql", dqb, gq, m128(PIECE * zp), PIECE, 3)

    def outgoing(tag):
        i, src, there, _, dev = moves[tag]
        return pltpu.make_async_remote_copy(src, there, send.at[i], recv.at[i], device_id=dev, device_id_type=MESH)

    def arriving(tag):
        i, _, _, here, dev = moves[tag]
        return pltpu.make_async_remote_copy(here, here, send.at[i], recv.at[i], device_id=dev, device_id_type=MESH)

    def entry_kept(h):
        return pltpu.make_async_copy(bg.at[0, pl.ds(HALF * h, HALF)], slot(y, z, h), esem.at[h])

    loads = []
    for src, dst in (
        (ks.at[0, :, own_slab], k2.at[(*block(x), in_pair)]),
        (qs.at[0, :, own_slab], q2.at[(*block(x), in_pair)]),
        (vs.at[0, :, own_slab], v2.at[(*block(x), in_pair)]),
        (cx.at[0], ctx.at[x]),
        (wo.at[0], wv),
    ):
        loads.append(pltpu.make_async_copy(src, dst, lsem.at[len(loads)]))

    def emit_send(tag):
        if tag[0] == "E":
            h = int(tag[1])

            @pl.when(has_prev)
            def _():
                outgoing(tag).start()

            @pl.when(jnp.logical_not(has_next))
            def _():
                entry_kept(h).start()
        else:
            outgoing(tag).start()

    def emit_wait(tag):
        if tag[0] == "E":
            h = int(tag[1])

            @pl.when(has_next)
            def _():
                arriving(tag).wait_recv()

            @pl.when(jnp.logical_not(has_next))
            def _():
                entry_kept(h).wait()
        elif tag[0] == "@":
            loads[int(tag[1])].wait()
        else:
            arriving(tag).wait_recv()

    def group_rows(g):
        zz = g // 2
        return g - 2 * zz, zz, pl.ds(m128(PIECE * zz), PIECE), pl.ds(m128(ROWS + PIECE * zz), PIECE)

    def partial_grad(k):
        g = groups[k]

        @pl.loop(0, 3)
        def _(n):
            rows = pl.ds(pl.multiple_of(n * 256, 256), 256)
            r = dot(inc[g], wv[rows], 1, 1)
            part[k, :, rows] = r
            partb[k, :, rows] = r.astype(BF16)

    def pass_on(k):
        r = part[k, :, slab_of(x_b)] + got_a[k, :, in_pair_b].astype(F32)
        sumb[k] = r.astype(BF16)

    heads = [pl.ds(HEAD * h, HEAD) for h in range(2)]
    pheads = [pl.ds(m128(HEAD * (par + h)), HEAD) for h in range(2)]

    def softmax(k):
        p, zz, rows0, rows1 = group_rows(groups[k])
        row = lax.broadcasted_iota(jnp.int32, (KEYS, ROWS), 0)
        lane = lax.broadcasted_iota(jnp.int32, (KEYS, ROWS), 1)
        ahead = jnp.where(lane < PIECE, lane, lane + PIECE) - row
        for h in range(2):
            qg[k, 0:PIECE, heads[h]] = q2[p, rows0, pheads[h]]
            qg[k, PIECE:ROWS, heads[h]] = q2[p, rows1, pheads[h]]

        def scores(j, tops):
            result = []
            ok = ahead >= KEYS * (j - p) - PIECE * zz
            for h in range(2):
                sc = dot(k2[j, :, pheads[h]], qg[k, :, heads[h]], 1, 1) * SCALE
                sc = jnp.where(ok, sc, -jnp.inf)
                pt[h, k, j] = sc
                result.append(jnp.maximum(tops[h], jnp.max(sc, axis=0, keepdims=True)))
            return tuple(result)

        low = jnp.full((1, ROWS), -jnp.inf, F32)
        tops = lax.fori_loop(0, p + 1, scores, (low, low))

        def weights(j, sums):
            result = []
            for h in range(2):
                e = jnp.exp(pt[h, k, j] - tops[h])
                pt[h, k, j] = e
                result.append(sums[h] + jnp.sum(e, axis=0, keepdims=True))
            return tuple(result)

        none = jnp.zeros((1, ROWS), F32)
        sums = lax.fori_loop(0, p + 1, weights, (none, none))
        for h in range(2):
            linv[k, h : h + 1] = 1.0 / sums[h]

    def turn(k):
        p, _, rows, _ = group_rows(groups[k])
        ctxt[k, :, 0:PIECE] = ctx[2 * p, rows].T
        ctxt[k, :, PIECE:ROWS] = ctx[2 * p + 1, rows].T

    def weight_grad(k, half, first):
        g = groups[k]

        @pl.loop(0, FEAT // TILE // 2)
        def _(n):
            cols = pl.ds(pl.multiple_of(half * (FEAT // 2) + n * TILE, TILE), TILE)
            r = dot(ctxt[k], inc[g, :, cols], 1, 0)
            if not first:
                r = r + acc[:, cols]
            if k == 3:
                gw[0, :, cols] = r.astype(BF16)
            else:
                acc[:, cols] = r

    def attend(k):
        p, _, rows0, rows1 = group_rows(groups[k])
        if k == 0:
            dka[...] = jnp.zeros_like(dka)
            dva[...] = jnp.zeros_like(dva)
        grad = part[k, :, own_slab] + got_a[k, :, in_pair].astype(F32) + got_b[k].astype(F32)
        gb = grad.astype(BF16)
        dout[...] = gb
        rounded = gb.astype(F32)
        top = (rounded[0:PIECE] * ctx[2 * p, rows0, own_slab].astype(F32)).T
        low = (rounded[PIECE:ROWS] * ctx[2 * p + 1, rows0, own_slab].astype(F32)).T
        deltas = []
        for h in range(2):
            sel = slice(HEAD * h, HEAD * (h + 1))
            deltas.append(
                jnp.concatenate(
                    [jnp.sum(top[sel], axis=0, keepdims=True), jnp.sum(low[sel], axis=0, keepdims=True)], axis=1
                )
            )
        inv = [linv[k, h : h + 1] for h in range(2)]
        dqa[...] = jnp.zeros_like(dqa)

        @pl.loop(0, p + 1)
        def _(j):
            for h in range(2):
                gh = dout[:, heads[h]]
                w = pt[h, k, j] * inv[h]
                dp = dot(v2[j, :, pheads[h]], gh, 1, 1)
                ds = (w * (dp - deltas[h])).astype(BF16)
                dva[j, :, heads[h]] += dot(w.astype(BF16), gh, 1, 0)
                dka[j, :, heads[h]] += dot(ds, qg[k, :, heads[h]], 1, 0)
                dqa[:, heads[h]] += dot(ds, k2[j, :, pheads[h]], 0, 0)

        dqb[p, rows0] = (dqa[0:PIECE] * SCALE).astype(BF16)
        dqb[p, rows1] = (dqa[PIECE:ROWS] * SCALE).astype(BF16)

    def cast_keys():
        dkb[...] = (dka[...] * SCALE).astype(BF16)

    def cast_values():
        dvb[...] = dva[...].astype(BF16)

    table = {
        "E0": ([], None, ["E0"]),
        "E1": ([], None, ["E1"]),
        "cA": ([], None, ["cA"]),
        "cB": ([], None, ["cB"]),
        "cfA": (["cA"], None, ["cC0"]),
        "cfB": (["cB"], None, ["cC1"]),
        "e0r": (["E0"], None, ["l_own0"]),
        "e0l": (["E0"], None, ["r_own0"]),
        "e1l": (["E1"], None, ["r_own1"]),
        "e1r": (["E1"], None, ["l_own1"]),
        "zs0": (["E0"], None, ["z0"]),
        "zs1": (["E1"], None, ["z1"]),
        "f0": (["l_own0"], None, ["o_own0"]),
        "f1": (["r_own1"], None, ["o_own1"]),
        "f2": (["r_oth1"], None, ["o_oth1"]),
        "f3": (["o_own0"], None, ["o_oth0"]),
        "zr0": (["z0"], None, ["l_oth0"]),
        "zr0l": (["z0"], None, ["r_oth0"]),
        "zr1": (["z1"], None, ["r_oth1"]),
        "zr1r": (["z1"], None, ["l_oth1"]),
        "dq": ([], None, ["dqe1", "dqeA", "dqeB"]),
        "dqf": (["dqe1"], None, ["dqeC"]),
        "dk": ([], cast_keys, ["dk1", "dkA", "dkB"]),
        "dv": ([], cast_values, ["dv1", "dvA", "dvB"]),
        "dql": ([], None, ["dql1", "dqlA", "dqlB"]),
    }
    own = ["E0", "E1"]
    near = ["l_own0", "l_own1", "r_own0", "r_own1"]
    far = ["o_own0", "o_own1"]
    near_z = ["z0", "z1", "l_oth0", "l_oth1", "r_oth0", "r_oth1"]
    far_z = ["o_oth0", "o_oth1"]
    for n in "kqv":
        table[n] = ([], None, [n + "A", n + "B"])
        table[n + "f"] = ([n + "A"], None, [n + "C"])
    for k, need in enumerate((["@4"] + own + near, far, near_z, far_z)):
        table["p%d" % k] = (need, lambda k=k: partial_grad(k), ["rsA%d" % k])
        table["s%d" % k] = (["rsA%d" % k], lambda k=k: pass_on(k), ["rsB%d" % k])
        table["P%d" % k] = (["@0", "@1", "kA", "kB", "kC", "qA", "qB", "qC"], lambda k=k: softmax(k), [])
        table["t%d" % k] = (["@3", "cA", "cB", "cC0", "cC1"], lambda k=k: turn(k), [])
        table["a%d" % k] = (["@2", "vA", "vB", "vC", "rsB%d" % k], lambda k=k: attend(k), [])

    def perform(order):
        seen = set()
        touched = set()
        for name in order:
            if name[0] == "g":
                k, half = int(name[1]), "ab".index(name[2])
                weight_grad(k, half, half not in touched)
                touched.add(half)
                continue
            waits, work, sends = table[name]
            for tag in waits:
                if tag not in seen:
                    seen.add(tag)
                    emit_wait(tag)
            if work is not None:
                work()
            for tag in sends:
                emit_send(tag)
        for n, (b, g) in enumerate(((dqb, gq), (dkb, gk), (dvb, gv))):
            pltpu.make_async_copy(b.at[block(x)], g.at[0, :, own_slab], osem.at[n]).start()
        for n in ("dk", "dv", "dql"):
            emit_wait(n + "1")
            emit_send(n + "C")

    for copy in loads:
        copy.start()
    for n, order in enumerate((ORDER0, ORDER1)):
        pl.when(core == n)(lambda order=order: perform(order))

    for n in ("dqe", "dk", "dv", "dql"):
        for tail in "ABC":
            emit_wait(n + tail)
    for n, (b, g) in enumerate(((dqb, gq), (dkb, gk), (dvb, gv))):
        pltpu.make_async_copy(b.at[block(x)], g.at[0, :, own_slab], osem.at[n]).wait()
    for tag in moves:
        if tag[0] == "E":

            @pl.when(has_prev)
            def _():
                outgoing(tag).wait_send()
        else:
            outgoing(tag).wait_send()


N_MOVES = 2 * 6 + 4 + 9 + 4 + 8 + 16


def write_out(gw, gq, gk, gv, gw_out, gq_out, gk_out, gv_out, sems):
    copies = []
    for n in range(6):
        rows = pl.ds(n * (WIDTH // 6), WIDTH // 6)
        copies.append(pltpu.make_async_copy(gw.at[0, rows], gw_out.at[0, rows], sems.at[n]))
    for n, (src, dst) in enumerate(((gq, gq_out), (gk, gk_out), (gv, gv_out))):
        copies.append(pltpu.make_async_copy(src, dst, sems.at[6 + n]))
    for copy in copies:
        copy.start()
    for copy in copies:
        copy.wait()


def local(boundary_grad, w_out, context, queries, keys, values):
    any_spec = pl.BlockSpec(memory_space=pl.ANY)
    vmem_spec = pl.BlockSpec(memory_space=pltpu.VMEM)
    shapes = [(1, WIDTH, FEAT), (1, ROWS, WIDTH), (1, ROWS, WIDTH), (1, ROWS, WIDTH)]
    grads = pl.pallas_call(
        kernel,
        out_shape=[pltpu.VMEM(shape, BF16) for shape in shapes],
        in_specs=[any_spec] * 6,
        out_specs=[vmem_spec] * 4,
        scratch_shapes=[
            pltpu.VMEM((4, ROWS, FEAT), BF16),
            pltpu.VMEM((WIDTH, FEAT), BF16),
            pltpu.VMEM((4, ROWS, WIDTH), BF16),
            pltpu.VMEM((4, WIDTH, ROWS), BF16),
            pltpu.VMEM((WIDTH, FEAT), F32),
            pltpu.VMEM((2, KEYS, PAIR), BF16),
            pltpu.VMEM((2, KEYS, PAIR), BF16),
            pltpu.VMEM((2, KEYS, PAIR), BF16),
            pltpu.VMEM((4, ROWS, SLAB), BF16),
            pltpu.VMEM((4, ROWS, WIDTH), F32),
            pltpu.VMEM((4, ROWS, WIDTH), BF16),
            pltpu.VMEM((4, ROWS, PAIR), BF16),
            pltpu.VMEM((4, ROWS, SLAB), BF16),
            pltpu.VMEM((4, ROWS, SLAB), BF16),
            pltpu.VMEM((2, 4, 2, KEYS, ROWS), F32),
            pltpu.VMEM((4, 8, ROWS), F32),
            pltpu.VMEM((ROWS, SLAB), BF16),
            pltpu.VMEM((ROWS, SLAB), F32),
            pltpu.VMEM((2, KEYS, SLAB), F32),
            pltpu.VMEM((2, KEYS, SLAB), F32),
            pltpu.VMEM((2, KEYS, SLAB), BF16),
            pltpu.VMEM((2, KEYS, SLAB), BF16),
            pltpu.VMEM((2, KEYS, SLAB), BF16),
            pltpu.VMEM((4, ROWS, HEAD), BF16),
            pltpu.SemaphoreType.DMA((N_MOVES,)),
            pltpu.SemaphoreType.DMA((N_MOVES,)),
            pltpu.SemaphoreType.DMA((5,)),
            pltpu.SemaphoreType.DMA((2,)),
            pltpu.SemaphoreType.DMA((3,)),
        ],
        compiler_params=pltpu.CompilerParams(
            collective_id=0, has_side_effects=True, vmem_limit_bytes=54 * 1024 * 1024
        ),
    )(boundary_grad, w_out, context, queries, keys, values)
    return pl.pallas_call(
        write_out,
        out_shape=[jax.ShapeDtypeStruct(shape, BF16) for shape in shapes],
        in_specs=[vmem_spec] * 4,
        out_specs=[any_spec] * 4,
        scratch_shapes=[pltpu.SemaphoreType.DMA((9,))],
    )(*grads)


def solution(mesh):
    in_specs = (
        P("section", "col", "row"),
        P("section", "col", "row"),
        P("section", "row", "col"),
        P("section", "row", "col"),
        P("section", "row", "col"),
        P("section", "row", "col"),
    )
    out_specs = (
        P("section", "col", "row"),
        P("section", "row", "col"),
        P("section", "row", "col"),
        P("section", "row", "col"),
    )
    return jax.shard_map(local, mesh=mesh, in_specs=in_specs, out_specs=out_specs, check_vma=False)
```

```python
import jax
import jax.numpy as jnp
from jax import lax
from jax.experimental import pallas as pl
from jax.experimental.pallas import tpu as pltpu
from jax.sharding import PartitionSpec as P

HEAD = 128
SCALE = HEAD ** (-0.5)
MESH = pl.DeviceIdType.MESH
BF16 = jnp.bfloat16
F32 = jnp.float32

ROWS = 256
PIECE = 128
HALF = 64
KEYS = 512
FEAT = 3072
WIDTH = 768
PAIR = 384
SLAB = 256
TILE = 512

ORDER0 = [
    "E0", "cA", "e1l", "e0r", "k", "f1", "q", "E1", "cB", "f0", "kf", "zs1", "e0l", "e1r", "qf", "v", "cfA", "cfB",
    "p0", "zr1r", "zs0", "t0", "g0a", "vf", "f3", "s0", "zr1", "P0", "t1", "p1", "zr0l", "a0", "P1", "zr0", "f2",
    "t2", "g0b", "t3", "s1", "g1a", "P2", "a1", "P3", "dq", "p2", "p3", "dqf", "g1b", "g2a", "s2", "s3", "a2",
    "g2b", "g3a", "a3", "g3b", "dk", "dv", "dql",
]
ORDER1 = [
    "cB", "E1", "cA", "E0", "k", "kf", "e0l", "e0r", "q", "qf", "f0", "zs1", "cfA", "e1l", "cfB", "e1r", "P0", "P1",
    "f1", "v", "t0", "zs0", "t1", "p0", "zr1", "f3", "s0", "vf", "g0a", "t2", "zr1r", "p1", "zr0l", "g0b", "zr0",
    "s1", "a0", "P2", "f2", "g1a", "a1", "g1b", "dq", "p2", "p3", "t3", "P3", "s2", "g2a", "s3", "dqf", "g2b", "a2",
    "a3", "g3a", "g3b", "dk", "dv", "dql",
]


def dot(a, b, ca, cb):
    return lax.dot_general(a, b, (((ca,), (cb,)), ((), ())), preferred_element_type=F32)


def kernel(
    bg, wo, cx, qs, ks, vs,
    gw, gq, gk, gv,
    inc, wv, ctx, ctxt, acc, q2, k2, v2, qg, part, partb, got_a, got_b, sumb, pt, linv, dout,
    dqa, dka, dva, dqb, dkb, dvb, stage,
    send, recv, lsem, esem, osem,
):
    s = lax.axis_index("section")
    x = lax.axis_index("row")
    c = lax.axis_index("col")
    y = c // 2
    z = c - 2 * y
    core = s - 2 * (s // 2)
    y_r = lax.rem(y + 1 + 2 * core, 4)
    y_l = lax.rem(y + 3 + 2 * core, 4)
    y_o = lax.rem(y + 2, 4)
    zp = 1 - z
    pair = x // 2
    par = x - 2 * pair
    par_b = 1 - par
    x_a = 3 - x
    x_b = 2 * pair + par_b
    x_c = lax.rem(x + 2, 4)
    dev_r = (s, x, 2 * y_r + z)
    dev_l = (s, x, 2 * y_l + z)
    dev_z = (s, x, 2 * y + zp)
    dev_a = (s, x_a, c)
    dev_b = (s, x_b, c)
    has_prev = s > 0
    has_next = s < 7
    dev_prev = (jnp.maximum(s - 1, 0), x, c)
    dev_next = (jnp.minimum(s + 1, 7), x, c)

    barrier = pltpu.get_barrier_semaphore()
    for dev in (dev_r, dev_l, dev_z, dev_a, dev_b):
        pl.semaphore_signal(barrier, inc=1, device_id=dev, device_id_type=MESH)

    @pl.when(has_prev)
    def _():
        pl.semaphore_signal(barrier, inc=1, device_id=dev_prev, device_id_type=MESH)

    @pl.when(has_next)
    def _():
        pl.semaphore_signal(barrier, inc=1, device_id=dev_next, device_id_type=MESH)

    pl.semaphore_wait(barrier, 5 + has_prev.astype(jnp.int32) + has_next.astype(jnp.int32))

    def m128(v):
        return pl.multiple_of(v, 128)

    def slab_of(xx):
        p = xx // 2
        return pl.ds(m128(PAIR * p + HEAD * (xx - 2 * p)), SLAB)

    def full_of(xx):
        p = xx // 2
        return pl.ds(m128(PAIR * p + 2 * HEAD * (xx - 2 * p)), HEAD)

    def pair_of(xx):
        return pl.ds(m128(PAIR * (xx // 2)), PAIR)

    own_slab = slab_of(x)
    in_pair = pl.ds(m128(HEAD * par), SLAB)
    in_pair_b = pl.ds(m128(HEAD * par_b), SLAB)
    own_full = pl.ds(m128(HEAD * par), HEAD)

    def slot(yy, zz, h):
        half = yy // 2
        return inc.at[2 * zz + half, pl.ds(pl.multiple_of(PIECE * (yy - 2 * half) + HALF * h, HALF), HALF)]

    groups = [2 * z + y // 2, 2 * z + 1 - y // 2, 2 * zp + y // 2, 2 * zp + 1 - y // 2]

    moves = {}

    def move(tag, src, there, here, dev):
        moves[tag] = (len(moves), src, there, here, dev)

    for h in range(2):
        move("E%d" % h, bg.at[0, pl.ds(HALF * h, HALF)], slot(y, z, h), slot(y, z, h), dev_prev)
        move("z%d" % h, slot(y, z, h), slot(y, z, h), slot(y, zp, h), dev_z)
        move("l_own%d" % h, slot(y, z, h), slot(y, z, h), slot(y_l, z, h), dev_r)
        move("r_own%d" % h, slot(y, z, h), slot(y, z, h), slot(y_r, z, h), dev_l)
        move("l_oth%d" % h, slot(y, zp, h), slot(y, zp, h), slot(y_l, zp, h), dev_r)
        move("r_oth%d" % h, slot(y, zp, h), slot(y, zp, h), slot(y_r, zp, h), dev_l)
    move("o_own0", slot(y_l, z, 0), slot(y_l, z, 0), slot(y_o, z, 0), dev_r)
    move("o_own1", slot(y_r, z, 1), slot(y_r, z, 1), slot(y_o, z, 1), dev_l)
    move("o_oth1", slot(y_r, zp, 1), slot(y_r, zp, 1), slot(y_o, zp, 1), dev_l)
    move("o_oth0", slot(y_o, z, 0), slot(y_o, z, 0), slot(y_o, zp, 0), dev_z)
    def block(xx, start=0, size=ROWS):
        half = xx // 2
        return half, pl.ds(m128(ROWS * (xx - 2 * half) + start), size)

    for n, a, b in (("k", ks, k2), ("q", qs, q2), ("v", vs, v2)):
        to, from_a, from_b, from_c = block(x), block(x_a), block(x_b), block(x_c)
        move(n + "A", a.at[0, :, pair_of(x_a)], b.at[to], b.at[from_a], dev_a)
        move(n + "B", a.at[0, :, slab_of(x_b)], b.at[(*to, in_pair_b)], b.at[(*from_b, in_pair)], dev_b)
        move(n + "C", b.at[(*from_a, in_pair_b)], b.at[(*from_a, in_pair_b)], b.at[(*from_c, in_pair)], dev_b)
    move("cA", cx.at[0], ctx.at[x], ctx.at[x_a], dev_a)
    move("cB", cx.at[0], ctx.at[x], ctx.at[x_b], dev_b)
    lo, hi = pl.ds(0, ROWS // 2), pl.ds(ROWS // 2, ROWS // 2)
    move("cC0", ctx.at[x_a, lo], ctx.at[x_a, lo], ctx.at[x_c, lo], dev_b)
    move("cC1", ctx.at[x_b, hi], ctx.at[x_b, hi], ctx.at[x_c, hi], dev_a)
    for k in range(4):
        move("rsA%d" % k, partb.at[k, :, pair_of(x_a)], got_a.at[k], got_a.at[k], dev_a)
        move("rsB%d" % k, sumb.at[k], got_b.at[k], got_b.at[k], dev_b)

    def move_out(n, src, dst, start, size, where):
        rows = pl.ds(start, size)
        hop = stage.at[where, pl.ds(0, size)]
        to_a, to_b, to_c = (block(xx, start, size) for xx in (x_a, x_b, x_c))
        move(n + "1", src.at[(*to_c, own_full)], hop, hop, dev_b)
        move(n + "A", src.at[to_a], dst.at[0, rows, own_slab], dst.at[0, rows, slab_of(x_a)], dev_a)
        move(n + "B", src.at[(*to_b, own_full)], dst.at[0, rows, full_of(x)], dst.at[0, rows, full_of(x_b)], dev_b)
        move(n + "C", hop, dst.at[0, rows, full_of(x_b)], dst.at[0, rows, full_of(x_c)], dev_a)

    move_out("dk", dkb, gk, 0, ROWS, 0)
    move_out("dv", dvb, gv, 0, ROWS, 1)
    move_out("dqe", dqb, gq, m128(PIECE * z), PIECE, 2)
    move_out("dql", dqb, gq, m128(PIECE * zp), PIECE, 3)

    def outgoing(tag):
        i, src, there, _, dev = moves[tag]
        return pltpu.make_async_remote_copy(src, there, send.at[i], recv.at[i], device_id=dev, device_id_type=MESH)

    def arriving(tag):
        i, _, _, here, dev = moves[tag]
        return pltpu.make_async_remote_copy(here, here, send.at[i], recv.at[i], device_id=dev, device_id_type=MESH)

    def entry_kept(h):
        return pltpu.make_async_copy(bg.at[0, pl.ds(HALF * h, HALF)], slot(y, z, h), esem.at[h])

    loads = []
    for src, dst in (
        (ks.at[0, :, own_slab], k2.at[(*block(x), in_pair)]),
        (qs.at[0, :, own_slab], q2.at[(*block(x), in_pair)]),
        (vs.at[0, :, own_slab], v2.at[(*block(x), in_pair)]),
        (cx.at[0], ctx.at[x]),
        (wo.at[0], wv),
    ):
        loads.append(pltpu.make_async_copy(src, dst, lsem.at[len(loads)]))

    def emit_send(tag):
        if tag[0] == "E":
            h = int(tag[1])

            @pl.when(has_prev)
            def _():
                outgoing(tag).start()

            @pl.when(jnp.logical_not(has_next))
            def _():
                entry_kept(h).start()
        else:
            outgoing(tag).start()

    def emit_wait(tag):
        if tag[0] == "E":
            h = int(tag[1])

            @pl.when(has_next)
            def _():
                arriving(tag).wait_recv()

            @pl.when(jnp.logical_not(has_next))
            def _():
                entry_kept(h).wait()
        elif tag[0] == "@":
            loads[int(tag[1])].wait()
        else:
            arriving(tag).wait_recv()

    def group_rows(g):
        zz = g // 2
        return g - 2 * zz, zz, pl.ds(m128(PIECE * zz), PIECE), pl.ds(m128(ROWS + PIECE * zz), PIECE)

    def partial_grad(k):
        g = groups[k]

        @pl.loop(0, 3)
        def _(n):
            rows = pl.ds(pl.multiple_of(n * 256, 256), 256)
            r = dot(inc[g], wv[rows], 1, 1)
            part[k, :, rows] = r
            partb[k, :, rows] = r.astype(BF16)

    def pass_on(k):
        r = part[k, :, slab_of(x_b)] + got_a[k, :, in_pair_b].astype(F32)
        sumb[k] = r.astype(BF16)

    heads = [pl.ds(HEAD * h, HEAD) for h in range(2)]
    pheads = [pl.ds(m128(HEAD * (par + h)), HEAD) for h in range(2)]

    def softmax(k):
        p, zz, rows0, rows1 = group_rows(groups[k])
        row = lax.broadcasted_iota(jnp.int32, (KEYS, ROWS), 0)
        lane = lax.broadcasted_iota(jnp.int32, (KEYS, ROWS), 1)
        ahead = jnp.where(lane < PIECE, lane, lane + PIECE) - row
        for h in range(2):
            qg[k, 0:PIECE, heads[h]] = q2[p, rows0, pheads[h]]
            qg[k, PIECE:ROWS, heads[h]] = q2[p, rows1, pheads[h]]

        def scores(j, tops):
            result = []
            ok = ahead >= KEYS * (j - p) - PIECE * zz
            for h in range(2):
                sc = dot(k2[j, :, pheads[h]], qg[k, :, heads[h]], 1, 1) * SCALE
                sc = jnp.where(ok, sc, -jnp.inf)
                pt[h, k, j] = sc
                result.append(jnp.maximum(tops[h], jnp.max(sc, axis=0, keepdims=True)))
            return tuple(result)

        low = jnp.full((1, ROWS), -jnp.inf, F32)
        tops = lax.fori_loop(0, p + 1, scores, (low, low))

        def weights(j, sums):
            result = []
            for h in range(2):
                e = jnp.exp(pt[h, k, j] - tops[h])
                pt[h, k, j] = e
                result.append(sums[h] + jnp.sum(e, axis=0, keepdims=True))
            return tuple(result)

        none = jnp.zeros((1, ROWS), F32)
        sums = lax.fori_loop(0, p + 1, weights, (none, none))
        for h in range(2):
            linv[k, h : h + 1] = 1.0 / sums[h]

    def turn(k):
        p, _, rows, _ = group_rows(groups[k])
        ctxt[k, :, 0:PIECE] = ctx[2 * p, rows].T
        ctxt[k, :, PIECE:ROWS] = ctx[2 * p + 1, rows].T

    def weight_grad(k, half, first):
        g = groups[k]

        @pl.loop(0, FEAT // TILE // 2)
        def _(n):
            cols = pl.ds(pl.multiple_of(half * (FEAT // 2) + n * TILE, TILE), TILE)
            r = dot(ctxt[k], inc[g, :, cols], 1, 0)
            if not first:
                r = r + acc[:, cols]
            if k == 3:
                gw[0, :, cols] = r.astype(BF16)
            else:
                acc[:, cols] = r

    def attend(k):
        p, _, rows0, rows1 = group_rows(groups[k])
        if k == 0:
            dka[...] = jnp.zeros_like(dka)
            dva[...] = jnp.zeros_like(dva)
        grad = part[k, :, own_slab] + got_a[k, :, in_pair].astype(F32) + got_b[k].astype(F32)
        gb = grad.astype(BF16)
        dout[...] = gb
        rounded = gb.astype(F32)
        top = (rounded[0:PIECE] * ctx[2 * p, rows0, own_slab].astype(F32)).T
        low = (rounded[PIECE:ROWS] * ctx[2 * p + 1, rows0, own_slab].astype(F32)).T
        deltas = []
        for h in range(2):
            sel = slice(HEAD * h, HEAD * (h + 1))
            deltas.append(
                jnp.concatenate(
                    [jnp.sum(top[sel], axis=0, keepdims=True), jnp.sum(low[sel], axis=0, keepdims=True)], axis=1
                )
            )
        inv = [linv[k, h : h + 1] for h in range(2)]
        dqa[...] = jnp.zeros_like(dqa)

        @pl.loop(0, p + 1)
        def _(j):
            for h in range(2):
                gh = dout[:, heads[h]]
                w = pt[h, k, j] * inv[h]
                dp = dot(v2[j, :, pheads[h]], gh, 1, 1)
                ds = (w * (dp - deltas[h])).astype(BF16)
                dva[j, :, heads[h]] += dot(w.astype(BF16), gh, 1, 0)
                dka[j, :, heads[h]] += dot(ds, qg[k, :, heads[h]], 1, 0)
                dqa[:, heads[h]] += dot(ds, k2[j, :, pheads[h]], 0, 0)

        dqb[p, rows0] = (dqa[0:PIECE] * SCALE).astype(BF16)
        dqb[p, rows1] = (dqa[PIECE:ROWS] * SCALE).astype(BF16)

    def cast_keys():
        dkb[...] = (dka[...] * SCALE).astype(BF16)

    def cast_values():
        dvb[...] = dva[...].astype(BF16)

    table = {
        "E0": ([], None, ["E0"]),
        "E1": ([], None, ["E1"]),
        "cA": ([], None, ["cA"]),
        "cB": ([], None, ["cB"]),
        "cfA": (["cA"], None, ["cC0"]),
        "cfB": (["cB"], None, ["cC1"]),
        "e0r": (["E0"], None, ["l_own0"]),
        "e0l": (["E0"], None, ["r_own0"]),
        "e1l": (["E1"], None, ["r_own1"]),
        "e1r": (["E1"], None, ["l_own1"]),
        "zs0": (["E0"], None, ["z0"]),
        "zs1": (["E1"], None, ["z1"]),
        "f0": (["l_own0"], None, ["o_own0"]),
        "f1": (["r_own1"], None, ["o_own1"]),
        "f2": (["r_oth1"], None, ["o_oth1"]),
        "f3": (["o_own0"], None, ["o_oth0"]),
        "zr0": (["z0"], None, ["l_oth0"]),
        "zr0l": (["z0"], None, ["r_oth0"]),
        "zr1": (["z1"], None, ["r_oth1"]),
        "zr1r": (["z1"], None, ["l_oth1"]),
        "dq": ([], None, ["dqe1", "dqeA", "dqeB"]),
        "dqf": (["dqe1"], None, ["dqeC"]),
        "dk": ([], cast_keys, ["dk1", "dkA", "dkB"]),
        "dv": ([], cast_values, ["dv1", "dvA", "dvB"]),
        "dql": ([], None, ["dql1", "dqlA", "dqlB"]),
    }
    own = ["E0", "E1"]
    near = ["l_own0", "l_own1", "r_own0", "r_own1"]
    far = ["o_own0", "o_own1"]
    near_z = ["z0", "z1", "l_oth0", "l_oth1", "r_oth0", "r_oth1"]
    far_z = ["o_oth0", "o_oth1"]
    for n in "kqv":
        table[n] = ([], None, [n + "A", n + "B"])
        table[n + "f"] = ([n + "A"], None, [n + "C"])
    for k, need in enumerate((["@4"] + own + near, far, near_z, far_z)):
        table["p%d" % k] = (need, lambda k=k: partial_grad(k), ["rsA%d" % k])
        table["s%d" % k] = (["rsA%d" % k], lambda k=k: pass_on(k), ["rsB%d" % k])
        table["P%d" % k] = (["@0", "@1", "kA", "kB", "kC", "qA", "qB", "qC"], lambda k=k: softmax(k), [])
        table["t%d" % k] = (["@3", "cA", "cB", "cC0", "cC1"], lambda k=k: turn(k), [])
        table["a%d" % k] = (["@2", "vA", "vB", "vC", "rsB%d" % k], lambda k=k: attend(k), [])

    def perform(order):
        seen = set()
        touched = set()
        for name in order:
            if name[0] == "g":
                k, half = int(name[1]), "ab".index(name[2])
                weight_grad(k, half, half not in touched)
                touched.add(half)
                continue
            waits, work, sends = table[name]
            for tag in waits:
                if tag not in seen:
                    seen.add(tag)
                    emit_wait(tag)
            if work is not None:
                work()
            for tag in sends:
                emit_send(tag)
        for n, (b, g) in enumerate(((dqb, gq), (dkb, gk), (dvb, gv))):
            pltpu.make_async_copy(b.at[block(x)], g.at[0, :, own_slab], osem.at[n]).start()
        for n in ("dk", "dv", "dql"):
            emit_wait(n + "1")
            emit_send(n + "C")

    for copy in loads:
        copy.start()
    for n, order in enumerate((ORDER0, ORDER1)):
        pl.when(core == n)(lambda order=order: perform(order))

    for n in ("dqe", "dk", "dv", "dql"):
        for tail in "ABC":
            emit_wait(n + tail)
    for n, (b, g) in enumerate(((dqb, gq), (dkb, gk), (dvb, gv))):
        pltpu.make_async_copy(b.at[block(x)], g.at[0, :, own_slab], osem.at[n]).wait()
    for tag in moves:
        if tag[0] == "E":

            @pl.when(has_prev)
            def _():
                outgoing(tag).wait_send()
        else:
            outgoing(tag).wait_send()


N_MOVES = 2 * 6 + 4 + 9 + 4 + 8 + 16


def write_out(gw, gq, gk, gv, gw_out, gq_out, gk_out, gv_out, sems):
    copies = []
    for n in range(6):
        rows = pl.ds(n * (WIDTH // 6), WIDTH // 6)
        copies.append(pltpu.make_async_copy(gw.at[0, rows], gw_out.at[0, rows], sems.at[n]))
    for n, (src, dst) in enumerate(((gq, gq_out), (gk, gk_out), (gv, gv_out))):
        copies.append(pltpu.make_async_copy(src, dst, sems.at[6 + n]))
    for copy in copies:
        copy.start()
    for copy in copies:
        copy.wait()


def local(boundary_grad, w_out, context, queries, keys, values):
    any_spec = pl.BlockSpec(memory_space=pl.ANY)
    vmem_spec = pl.BlockSpec(memory_space=pltpu.VMEM)
    shapes = [(1, WIDTH, FEAT), (1, ROWS, WIDTH), (1, ROWS, WIDTH), (1, ROWS, WIDTH)]
    grads = pl.pallas_call(
        kernel,
        out_shape=[pltpu.VMEM(shape, BF16) for shape in shapes],
        in_specs=[any_spec] * 6,
        out_specs=[vmem_spec] * 4,
        scratch_shapes=[
            pltpu.VMEM((4, ROWS, FEAT), BF16),
            pltpu.VMEM((WIDTH, FEAT), BF16),
            pltpu.VMEM((4, ROWS, WIDTH), BF16),
            pltpu.VMEM((4, WIDTH, ROWS), BF16),
            pltpu.VMEM((WIDTH, FEAT), F32),
            pltpu.VMEM((2, KEYS, PAIR), BF16),
            pltpu.VMEM((2, KEYS, PAIR), BF16),
            pltpu.VMEM((2, KEYS, PAIR), BF16),
            pltpu.VMEM((4, ROWS, SLAB), BF16),
            pltpu.VMEM((4, ROWS, WIDTH), F32),
            pltpu.VMEM((4, ROWS, WIDTH), BF16),
            pltpu.VMEM((4, ROWS, PAIR), BF16),
            pltpu.VMEM((4, ROWS, SLAB), BF16),
            pltpu.VMEM((4, ROWS, SLAB), BF16),
            pltpu.VMEM((2, 4, 2, KEYS, ROWS), F32),
            pltpu.VMEM((4, 8, ROWS), F32),
            pltpu.VMEM((ROWS, SLAB), BF16),
            pltpu.VMEM((ROWS, SLAB), F32),
            pltpu.VMEM((2, KEYS, SLAB), F32),
            pltpu.VMEM((2, KEYS, SLAB), F32),
            pltpu.VMEM((2, KEYS, SLAB), BF16),
            pltpu.VMEM((2, KEYS, SLAB), BF16),
            pltpu.VMEM((2, KEYS, SLAB), BF16),
            pltpu.VMEM((4, ROWS, HEAD), BF16),
            pltpu.SemaphoreType.DMA((N_MOVES,)),
            pltpu.SemaphoreType.DMA((N_MOVES,)),
            pltpu.SemaphoreType.DMA((5,)),
            pltpu.SemaphoreType.DMA((2,)),
            pltpu.SemaphoreType.DMA((3,)),
        ],
        compiler_params=pltpu.CompilerParams(
            collective_id=0, has_side_effects=True, vmem_limit_bytes=54 * 1024 * 1024
        ),
    )(boundary_grad, w_out, context, queries, keys, values)
    return pl.pallas_call(
        write_out,
        out_shape=[jax.ShapeDtypeStruct(shape, BF16) for shape in shapes],
        in_specs=[any_spec] * 4,
        out_specs=[any_spec] * 4,
        scratch_shapes=[pltpu.SemaphoreType.DMA((9,))],
        compiler_params=pltpu.CompilerParams(vmem_limit_bytes=1024 * 1024),
    )(*grads)


def solution(mesh):
    in_specs = (
        P("section", "col", "row"),
        P("section", "col", "row"),
        P("section", "row", "col"),
        P("section", "row", "col"),
        P("section", "row", "col"),
        P("section", "row", "col"),
    )
    out_specs = (
        P("section", "col", "row"),
        P("section", "row", "col"),
        P("section", "row", "col"),
        P("section", "row", "col"),
    )
    return jax.shard_map(local, mesh=mesh, in_specs=in_specs, out_specs=out_specs, check_vma=False)
```

```python
import jax
import jax.numpy as jnp
from jax import lax
from jax.experimental import pallas as pl
from jax.experimental.pallas import tpu as pltpu
from jax.sharding import PartitionSpec as P

HEAD = 128
SCALE = HEAD ** (-0.5)
MESH = pl.DeviceIdType.MESH
BF16 = jnp.bfloat16
F32 = jnp.float32

ROWS = 256
PIECE = 128
CHUNKS = 2
CHUNK = PIECE // CHUNKS
LOW = 192
KEYS = 512
FEAT = 3072
WIDTH = 768
PAIR = 384
SLAB = 256
TILE = 512

ORDER0 = [
    "E0", "l0", "r0", "q", "cA", "l1", "f0", "E1", "qf", "k", "f1", "cB", "r1", "z1", "kf", "F0", "R1", "z0", "cfB",
    "L1", "p0", "cfA", "v", "p1", "R0", "L0", "P0", "s0", "t0", "P1", "t1", "F1", "t2", "P2", "vf", "gA", "s1",
    "p2", "gB", "a0", "p3", "s2", "a1", "t3", "dq", "s3", "a2", "gC", "P3", "a3", "gD", "dqf", "dk", "dv", "dql",
]
ORDER1 = [
    "E0", "cB", "k", "q", "cA", "E1", "cfB", "qf", "v", "l0", "r0", "f0", "cfA", "kf", "l1", "r1", "t0", "f1", "t1",
    "z1", "P0", "vf", "P1", "p0", "t2", "L1", "z0", "P2", "s0", "R1", "F0", "p1", "gA", "R0", "L0", "t3", "gB",
    "s1", "F1", "P3", "a0", "a1", "dq", "p2", "p3", "s2", "gC", "dqf", "s3", "gD", "a2", "a3", "dk", "dv", "dql",
]


def dot(a, b, ca, cb):
    return lax.dot_general(a, b, (((ca,), (cb,)), ((), ())), preferred_element_type=F32)


def kernel(
    bg, wo, cx, qs, ks, vs,
    gw, gq, gk, gv,
    inc, wv, ctx, ctxt, acc, q2, k2, v2, qg, part, partb, got_a, got_b, sumb, kt, pt, linv, dout,
    dqa, dka, dva, dqb, dkb, dvb, stage,
    send, recv, lsem, esem, osem,
):
    s = lax.axis_index("section")
    x = lax.axis_index("row")
    c = lax.axis_index("col")
    y = c // 2
    z = c - 2 * y
    core = s - 2 * (s // 2)
    y_r = lax.rem(y + 1 + 2 * core, 4)
    y_l = lax.rem(y + 3 + 2 * core, 4)
    y_o = lax.rem(y + 2, 4)
    zp = 1 - z
    pair = x // 2
    par = x - 2 * pair
    par_b = 1 - par
    x_a = 3 - x
    x_b = 2 * pair + par_b
    x_c = lax.rem(x + 2, 4)
    dev_r = (s, x, 2 * y_r + z)
    dev_l = (s, x, 2 * y_l + z)
    dev_z = (s, x, 2 * y + zp)
    dev_a = (s, x_a, c)
    dev_b = (s, x_b, c)
    has_prev = s > 0
    has_next = s < 7
    dev_prev = (jnp.maximum(s - 1, 0), x, c)
    dev_next = (jnp.minimum(s + 1, 7), x, c)

    barrier = pltpu.get_barrier_semaphore()
    for dev in (dev_r, dev_l, dev_z, dev_a, dev_b):
        pl.semaphore_signal(barrier, inc=1, device_id=dev, device_id_type=MESH)

    @pl.when(has_prev)
    def _():
        pl.semaphore_signal(barrier, inc=1, device_id=dev_prev, device_id_type=MESH)

    @pl.when(has_next)
    def _():
        pl.semaphore_signal(barrier, inc=1, device_id=dev_next, device_id_type=MESH)

    pl.semaphore_wait(barrier, 5 + has_prev.astype(jnp.int32) + has_next.astype(jnp.int32))

    def m128(v):
        return pl.multiple_of(v, 128)

    def slab_of(xx):
        p = xx // 2
        return pl.ds(m128(PAIR * p + HEAD * (xx - 2 * p)), SLAB)

    def full_of(xx):
        p = xx // 2
        return pl.ds(m128(PAIR * p + 2 * HEAD * (xx - 2 * p)), HEAD)

    def pair_of(xx):
        return pl.ds(m128(PAIR * (xx // 2)), PAIR)

    own_slab = slab_of(x)
    in_pair = pl.ds(m128(HEAD * par), SLAB)
    in_pair_b = pl.ds(m128(HEAD * par_b), SLAB)
    own_full = pl.ds(m128(HEAD * par), HEAD)

    def slot(yy, zz, q):
        return inc.at[zz, pl.ds(pl.multiple_of(PIECE * yy + CHUNK * q, CHUNK), CHUNK)]

    groups = [(z, y // 2), (z, 1 - y // 2), (zp, y // 2), (zp, 1 - y // 2)]

    moves = {}

    def move(tag, src, there, here, dev):
        moves[tag] = (len(moves), src, there, here, dev)

    for q in range(CHUNKS):
        move("E%d" % q, bg.at[0, pl.ds(CHUNK * q, CHUNK)], slot(y, z, q), slot(y, z, q), dev_prev)
        move("z%d" % q, slot(y, z, q), slot(y, z, q), slot(y, zp, q), dev_z)
        move("l_own%d" % q, slot(y, z, q), slot(y, z, q), slot(y_l, z, q), dev_r)
        move("r_own%d" % q, slot(y, z, q), slot(y, z, q), slot(y_r, z, q), dev_l)
        move("l_oth%d" % q, slot(y, zp, q), slot(y, zp, q), slot(y_l, zp, q), dev_r)
        move("r_oth%d" % q, slot(y, zp, q), slot(y, zp, q), slot(y_r, zp, q), dev_l)
        if q < CHUNKS // 2:
            move("o_own%d" % q, slot(y_l, z, q), slot(y_l, z, q), slot(y_o, z, q), dev_r)
            move("o_oth%d" % q, slot(y_o, z, q), slot(y_o, z, q), slot(y_o, zp, q), dev_z)
        else:
            move("o_own%d" % q, slot(y_r, z, q), slot(y_r, z, q), slot(y_o, z, q), dev_l)
            move("o_oth%d" % q, slot(y_r, zp, q), slot(y_r, zp, q), slot(y_o, zp, q), dev_l)

    def block(xx, start=0, size=ROWS):
        half = xx // 2
        return half, pl.ds(m128(ROWS * (xx - 2 * half) + start), size)

    for n, a, b in (("k", ks, k2), ("q", qs, q2), ("v", vs, v2)):
        to, from_a, from_b, from_c = block(x), block(x_a), block(x_b), block(x_c)
        move(n + "A", a.at[0, :, pair_of(x_a)], b.at[to], b.at[from_a], dev_a)
        move(n + "B", a.at[0, :, slab_of(x_b)], b.at[(*to, in_pair_b)], b.at[(*from_b, in_pair)], dev_b)
        move(n + "C", b.at[(*from_a, in_pair_b)], b.at[(*from_a, in_pair_b)], b.at[(*from_c, in_pair)], dev_b)
    move("cA", cx.at[0], ctx.at[x], ctx.at[x_a], dev_a)
    move("cB", cx.at[0], ctx.at[x], ctx.at[x_b], dev_b)
    lo, hi = pl.ds(0, LOW), pl.ds(LOW, ROWS - LOW)
    move("cC0", ctx.at[x_a, lo], ctx.at[x_a, lo], ctx.at[x_c, lo], dev_b)
    move("cC1", ctx.at[x_b, hi], ctx.at[x_b, hi], ctx.at[x_c, hi], dev_a)
    for k in range(4):
        move("rsA%d" % k, partb.at[k, pair_of(x_a)], got_a.at[k], got_a.at[k], dev_a)
        move("rsB%d" % k, sumb.at[k], got_b.at[k], got_b.at[k], dev_b)

    def move_out(n, src, dst, start, size, where):
        rows = pl.ds(start, size)
        hop = stage.at[where, pl.ds(0, size)]
        to_a, to_b, to_c = (block(xx, start, size) for xx in (x_a, x_b, x_c))
        move(n + "1", src.at[(*to_c, own_full)], hop, hop, dev_b)
        move(n + "A", src.at[to_a], dst.at[0, rows, own_slab], dst.at[0, rows, slab_of(x_a)], dev_a)
        move(n + "B", src.at[(*to_b, own_full)], dst.at[0, rows, full_of(x)], dst.at[0, rows, full_of(x_b)], dev_b)
        move(n + "C", hop, dst.at[0, rows, full_of(x_b)], dst.at[0, rows, full_of(x_c)], dev_a)

    move_out("dk", dkb, gk, 0, ROWS, 0)
    move_out("dv", dvb, gv, 0, ROWS, 1)
    move_out("dqe", dqb, gq, m128(PIECE * z), PIECE, 2)
    move_out("dql", dqb, gq, m128(PIECE * zp), PIECE, 3)

    def outgoing(tag):
        i, src, there, _, dev = moves[tag]
        return pltpu.make_async_remote_copy(src, there, send.at[i], recv.at[i], device_id=dev, device_id_type=MESH)

    def arriving(tag):
        i, _, _, here, dev = moves[tag]
        return pltpu.make_async_remote_copy(here, here, send.at[i], recv.at[i], device_id=dev, device_id_type=MESH)

    def entry_kept(q):
        return pltpu.make_async_copy(bg.at[0, pl.ds(CHUNK * q, CHUNK)], slot(y, z, q), esem.at[q])

    loads = []
    for src, dst in (
        (ks.at[0, :, own_slab], k2.at[(*block(x), in_pair)]),
        (qs.at[0, :, own_slab], q2.at[(*block(x), in_pair)]),
        (vs.at[0, :, own_slab], v2.at[(*block(x), in_pair)]),
        (cx.at[0], ctx.at[x]),
        (wo.at[0], wv),
    ):
        loads.append(pltpu.make_async_copy(src, dst, lsem.at[len(loads)]))

    def emit_send(tag):
        if tag[0] == "E":
            h = int(tag[1])

            @pl.when(has_prev)
            def _():
                outgoing(tag).start()

            @pl.when(jnp.logical_not(has_next))
            def _():
                entry_kept(h).start()
        else:
            outgoing(tag).start()

    def emit_wait(tag):
        if tag[0] == "E":
            h = int(tag[1])

            @pl.when(has_next)
            def _():
                arriving(tag).wait_recv()

            @pl.when(jnp.logical_not(has_next))
            def _():
                entry_kept(h).wait()
        elif tag[0] == "@":
            loads[int(tag[1])].wait()
        else:
            arriving(tag).wait_recv()

    def group_rows(g):
        zz, p = g
        return p, zz, pl.ds(m128(PIECE * zz), PIECE), pl.ds(m128(ROWS + PIECE * zz), PIECE)

    def partial_grad(k):
        zz, p = groups[k]
        tokens = pl.ds(pl.multiple_of(ROWS * p, ROWS), ROWS)
        r = dot(wv[...], inc[zz, tokens], 1, 1)
        part[k] = r
        partb[k] = r.astype(BF16)

    def pass_on(k):
        r = part[k, slab_of(x_b)] + got_a[k, in_pair_b].astype(F32)
        sumb[k] = r.astype(BF16)

    heads = [pl.ds(HEAD * h, HEAD) for h in range(2)]
    pheads = [pl.ds(m128(HEAD * (par + h)), HEAD) for h in range(2)]

    def softmax(k):
        p, zz, rows0, rows1 = group_rows(groups[k])
        row = lax.broadcasted_iota(jnp.int32, (KEYS, ROWS), 0)
        lane = lax.broadcasted_iota(jnp.int32, (KEYS, ROWS), 1)
        ahead = jnp.where(lane < PIECE, lane, lane + PIECE) - row
        if k == 0:
            for j in range(2):
                for h in range(2):
                    kt[j, heads[h]] = k2[j, :, pheads[h]].T
        for h in range(2):
            qg[k, 0:PIECE, heads[h]] = q2[p, rows0, pheads[h]]
            qg[k, PIECE:ROWS, heads[h]] = q2[p, rows1, pheads[h]]

        def scores(j, tops):
            result = []
            ok = ahead >= KEYS * (j - p) - PIECE * zz
            for h in range(2):
                sc = dot(k2[j, :, pheads[h]], qg[k, :, heads[h]], 1, 1) * SCALE
                sc = jnp.where(ok, sc, -jnp.inf)
                pt[h, k, j] = sc
                result.append(jnp.maximum(tops[h], jnp.max(sc, axis=0, keepdims=True)))
            return tuple(result)

        low = jnp.full((1, ROWS), -jnp.inf, F32)
        tops = lax.fori_loop(0, p + 1, scores, (low, low))

        def weights(j, sums):
            result = []
            for h in range(2):
                e = jnp.exp(pt[h, k, j] - tops[h])
                pt[h, k, j] = e
                result.append(sums[h] + jnp.sum(e, axis=0, keepdims=True))
            return tuple(result)

        none = jnp.zeros((1, ROWS), F32)
        sums = lax.fori_loop(0, p + 1, weights, (none, none))
        for h in range(2):
            linv[k, h : h + 1] = 1.0 / sums[h]

    def turn(k):
        p, _, rows, _ = group_rows(groups[k])
        ctxt[k // 2, :, pl.ds(m128(ROWS * p), PIECE)] = ctx[2 * p, rows].T
        ctxt[k // 2, :, pl.ds(m128(ROWS * p + PIECE), PIECE)] = ctx[2 * p + 1, rows].T

    def weight_grad(i, half):
        zz = (z, zp)[i]

        @pl.loop(0, FEAT // TILE // 2)
        def _(n):
            cols = pl.ds(pl.multiple_of(half * (FEAT // 2) + n * TILE, TILE), TILE)
            r = dot(ctxt[i], inc[zz, :, cols], 1, 0)
            if i == 0:
                acc[:, cols] = r
            else:
                gw[0, :, cols] = (r + acc[:, cols]).astype(BF16)

    def attend(k):
        p, _, rows0, rows1 = group_rows(groups[k])
        if k == 0:
            dka[...] = jnp.zeros_like(dka)
            dva[...] = jnp.zeros_like(dva)
        grad = part[k, own_slab] + got_a[k, in_pair].astype(F32) + got_b[k].astype(F32)
        gb = grad.astype(BF16)
        dout[...] = gb
        tokens = pl.ds(pl.multiple_of(ROWS * p, ROWS), ROWS)
        prod = gb.astype(F32) * ctxt[k // 2, own_slab, tokens].astype(F32)
        deltas = [jnp.sum(prod[HEAD * h : HEAD * (h + 1)], axis=0, keepdims=True) for h in range(2)]
        inv = [linv[k, h : h + 1] for h in range(2)]
        dqa[...] = jnp.zeros_like(dqa)

        @pl.loop(0, p + 1)
        def _(j):
            for h in range(2):
                gh = dout[heads[h]]
                w = pt[h, k, j] * inv[h]
                dp = dot(v2[j, :, pheads[h]], gh, 1, 0)
                ds = (w * (dp - deltas[h])).astype(BF16)
                dva[j, :, heads[h]] += dot(w.astype(BF16), gh, 1, 1)
                dka[j, :, heads[h]] += dot(ds, qg[k, :, heads[h]], 1, 0)
                dqa[heads[h]] += dot(kt[j, heads[h]], ds, 1, 0)

        dq = (dqa[...] * SCALE).astype(BF16).T
        dqb[p, rows0] = dq[0:PIECE]
        dqb[p, rows1] = dq[PIECE:ROWS]

    def cast_keys():
        dkb[...] = (dka[...] * SCALE).astype(BF16)

    def cast_values():
        dvb[...] = dva[...].astype(BF16)

    table = {
        "cA": ([], None, ["cA"]),
        "cB": ([], None, ["cB"]),
        "cfA": (["cA"], None, ["cC0"]),
        "cfB": (["cB"], None, ["cC1"]),
        "dq": ([], None, ["dqe1", "dqeA", "dqeB"]),
        "dqf": (["dqe1"], None, ["dqeC"]),
        "dk": ([], cast_keys, ["dk1", "dkA", "dkB"]),
        "dv": ([], cast_values, ["dv1", "dvA", "dvB"]),
        "dql": ([], None, ["dql1", "dqlA", "dqlB"]),
        "gA": ([], lambda: weight_grad(0, 0), []),
        "gB": ([], lambda: weight_grad(0, 1), []),
        "gC": ([], lambda: weight_grad(1, 0), []),
        "gD": ([], lambda: weight_grad(1, 1), []),
    }
    for n in "kqv":
        table[n] = ([], None, [n + "A", n + "B"])
        table[n + "f"] = ([n + "A"], None, [n + "C"])
    own, near, far, near_z, far_z = [], [], [], [], []
    for q in range(CHUNKS):
        i = str(q)
        first = q < CHUNKS // 2
        table["E" + i] = ([], None, ["E" + i])
        table["r" + i] = (["E" + i], None, ["l_own" + i])
        table["l" + i] = (["E" + i], None, ["r_own" + i])
        table["z" + i] = (["E" + i], None, ["z" + i])
        table["R" + i] = (["z" + i], None, ["l_oth" + i])
        table["L" + i] = (["z" + i], None, ["r_oth" + i])
        table["f" + i] = (["l_own" + i] if first else ["r_own" + i], None, ["o_own" + i])
        table["F" + i] = (["o_own" + i] if first else ["r_oth" + i], None, ["o_oth" + i])
        own += ["E" + i]
        near += ["l_own" + i, "r_own" + i]
        far += ["o_own" + i]
        near_z += ["z" + i, "l_oth" + i, "r_oth" + i]
        far_z += ["o_oth" + i]
    for k, need in enumerate((["@4"] + own + near, far, near_z, far_z)):
        table["p%d" % k] = (need, lambda k=k: partial_grad(k), ["rsA%d" % k])
        table["s%d" % k] = (["rsA%d" % k], lambda k=k: pass_on(k), ["rsB%d" % k])
        table["P%d" % k] = (["@0", "@1", "kA", "kB", "kC", "qA", "qB", "qC"], lambda k=k: softmax(k), [])
        table["t%d" % k] = (["@3", "cA", "cB", "cC0", "cC1"], lambda k=k: turn(k), [])
        table["a%d" % k] = (["@2", "vA", "vB", "vC", "rsB%d" % k], lambda k=k: attend(k), [])

    def perform(order):
        seen = set()
        for name in order:
            waits, work, sends = table[name]
            for tag in waits:
                if tag not in seen:
                    seen.add(tag)
                    emit_wait(tag)
            if work is not None:
                work()
            for tag in sends:
                emit_send(tag)
        for n, (b, g) in enumerate(((dqb, gq), (dkb, gk), (dvb, gv))):
            pltpu.make_async_copy(b.at[block(x)], g.at[0, :, own_slab], osem.at[n]).start()
        for n in ("dk", "dv", "dql"):
            emit_wait(n + "1")
            emit_send(n + "C")

    for copy in loads:
        copy.start()
    for n, order in enumerate((ORDER0, ORDER1)):
        pl.when(core == n)(lambda order=order: perform(order))

    for n in ("dqe", "dk", "dv", "dql"):
        for tail in "ABC":
            emit_wait(n + tail)
    for n, (b, g) in enumerate(((dqb, gq), (dkb, gk), (dvb, gv))):
        pltpu.make_async_copy(b.at[block(x)], g.at[0, :, own_slab], osem.at[n]).wait()
    for tag in moves:
        if tag[0] == "E":

            @pl.when(has_prev)
            def _():
                outgoing(tag).wait_send()
        else:
            outgoing(tag).wait_send()


N_MOVES = 8 * CHUNKS + 9 + 4 + 8 + 16


def write_out(gw, gq, gk, gv, gw_out, gq_out, gk_out, gv_out, sems):
    copies = []
    for n in range(6):
        rows = pl.ds(n * (WIDTH // 6), WIDTH // 6)
        copies.append(pltpu.make_async_copy(gw.at[0, rows], gw_out.at[0, rows], sems.at[n]))
    for n, (src, dst) in enumerate(((gq, gq_out), (gk, gk_out), (gv, gv_out))):
        copies.append(pltpu.make_async_copy(src, dst, sems.at[6 + n]))
    for copy in copies:
        copy.start()
    for copy in copies:
        copy.wait()


def local(boundary_grad, w_out, context, queries, keys, values):
    any_spec = pl.BlockSpec(memory_space=pl.ANY)
    vmem_spec = pl.BlockSpec(memory_space=pltpu.VMEM)
    shapes = [(1, WIDTH, FEAT), (1, ROWS, WIDTH), (1, ROWS, WIDTH), (1, ROWS, WIDTH)]
    grads = pl.pallas_call(
        kernel,
        out_shape=[pltpu.VMEM(shape, BF16) for shape in shapes],
        in_specs=[any_spec] * 6,
        out_specs=[vmem_spec] * 4,
        scratch_shapes=[
            pltpu.VMEM((2, KEYS, FEAT), BF16),
            pltpu.VMEM((WIDTH, FEAT), BF16),
            pltpu.VMEM((4, ROWS, WIDTH), BF16),
            pltpu.VMEM((2, WIDTH, KEYS), BF16),
            pltpu.VMEM((WIDTH, FEAT), F32),
            pltpu.VMEM((2, KEYS, PAIR), BF16),
            pltpu.VMEM((2, KEYS, PAIR), BF16),
            pltpu.VMEM((2, KEYS, PAIR), BF16),
            pltpu.VMEM((4, ROWS, SLAB), BF16),
            pltpu.VMEM((4, WIDTH, ROWS), F32),
            pltpu.VMEM((4, WIDTH, ROWS), BF16),
            pltpu.VMEM((4, PAIR, ROWS), BF16),
            pltpu.VMEM((4, SLAB, ROWS), BF16),
            pltpu.VMEM((4, SLAB, ROWS), BF16),
            pltpu.VMEM((2, SLAB, KEYS), BF16),
            pltpu.VMEM((2, 4, 2, KEYS, ROWS), F32),
            pltpu.VMEM((4, 8, ROWS), F32),
            pltpu.VMEM((ROWS, SLAB), BF16),
            pltpu.VMEM((ROWS, SLAB), F32),
            pltpu.VMEM((2, KEYS, SLAB), F32),
            pltpu.VMEM((2, KEYS, SLAB), F32),
            pltpu.VMEM((2, KEYS, SLAB), BF16),
            pltpu.VMEM((2, KEYS, SLAB), BF16),
            pltpu.VMEM((2, KEYS, SLAB), BF16),
            pltpu.VMEM((4, ROWS, HEAD), BF16),
            pltpu.SemaphoreType.DMA((N_MOVES,)),
            pltpu.SemaphoreType.DMA((N_MOVES,)),
            pltpu.SemaphoreType.DMA((5,)),
            pltpu.SemaphoreType.DMA((CHUNKS,)),
            pltpu.SemaphoreType.DMA((3,)),
        ],
        compiler_params=pltpu.CompilerParams(
            collective_id=0, has_side_effects=True, vmem_limit_bytes=54 * 1024 * 1024
        ),
    )(boundary_grad, w_out, context, queries, keys, values)
    return pl.pallas_call(
        write_out,
        out_shape=[jax.ShapeDtypeStruct(shape, BF16) for shape in shapes],
        in_specs=[any_spec] * 4,
        out_specs=[any_spec] * 4,
        scratch_shapes=[pltpu.SemaphoreType.DMA((9,))],
        compiler_params=pltpu.CompilerParams(vmem_limit_bytes=1024 * 1024),
    )(*grads)


def solution(mesh):
    in_specs = (
        P("section", "col", "row"),
        P("section", "col", "row"),
        P("section", "row", "col"),
        P("section", "row", "col"),
        P("section", "row", "col"),
        P("section", "row", "col"),
    )
    out_specs = (
        P("section", "col", "row"),
        P("section", "row", "col"),
        P("section", "row", "col"),
        P("section", "row", "col"),
    )
    return jax.shard_map(local, mesh=mesh, in_specs=in_specs, out_specs=out_specs, check_vma=False)
```

```python
import jax
import jax.numpy as jnp
from jax import lax
from jax.experimental import pallas as pl
from jax.experimental.pallas import tpu as pltpu
from jax.sharding import PartitionSpec as P

HEAD = 128
SCALE = HEAD ** (-0.5)
MESH = pl.DeviceIdType.MESH
BF16 = jnp.bfloat16
F32 = jnp.float32

ROWS = 256
PIECE = 128
CHUNKS = 2
CHUNK = PIECE // CHUNKS
LOW = 192
KEYS = 512
FEAT = 3072
WIDTH = 768
PAIR = 384
SLAB = 256
TILE = 512

ORDER0 = [
    "E1", "q", "r0", "k", "l0", "l1", "f0", "cB", "E0", "kf", "cA", "r1", "cfA", "f1", "z1", "cfB", "v", "z0", "p0",
    "F0", "R1", "L1", "p1", "L0", "t0", "R0", "qf", "s0", "t1", "vf", "t2", "gA", "F1", "P0", "a0", "P1", "p2",
    "s1", "P2", "p3", "gB", "s2", "P3", "a1", "dq", "s3", "a2", "dqf", "t3", "gC", "a3", "dql", "gD", "dk", "dqlf",
    "dkf", "dv", "dvf",
]
ORDER1 = [
    "cB", "E0", "q", "k", "E1", "qf", "r1", "cfB", "cA", "kf", "l1", "r0", "l0", "cfA", "P0", "t0", "f0", "v", "t1",
    "f1", "z0", "p0", "vf", "z1", "t2", "P1", "L0", "F0", "p1", "s0", "R0", "P2", "t3", "R1", "L1", "s1", "gA",
    "P3", "a0", "F1", "a1", "dq", "p2", "p3", "s2", "gB", "s3", "a2", "dqf", "a3", "dql", "dk", "gC", "dv", "dkf",
    "dqlf", "gD", "dvf",
]


def dot(a, b, ca, cb):
    return lax.dot_general(a, b, (((ca,), (cb,)), ((), ())), preferred_element_type=F32)


def kernel(
    bg, wo, cx, qs, ks, vs,
    gw, gq, gk, gv,
    inc, wv, ctx, ctxt, acc, q2, k2, v2, qg, part, partb, got_a, got_b, sumb, kt, pt, linv, dout,
    dqa, dka, dva, dqb, dkb, dvb, stage,
    send, recv, lsem, esem, osem,
):
    s = lax.axis_index("section")
    x = lax.axis_index("row")
    c = lax.axis_index("col")
    y = c // 2
    z = c - 2 * y
    core = s - 2 * (s // 2)
    y_r = lax.rem(y + 1 + 2 * core, 4)
    y_l = lax.rem(y + 3 + 2 * core, 4)
    y_o = lax.rem(y + 2, 4)
    zp = 1 - z
    pair = x // 2
    par = x - 2 * pair
    par_b = 1 - par
    x_a = 3 - x
    x_b = 2 * pair + par_b
    x_c = lax.rem(x + 2, 4)
    dev_r = (s, x, 2 * y_r + z)
    dev_l = (s, x, 2 * y_l + z)
    dev_z = (s, x, 2 * y + zp)
    dev_a = (s, x_a, c)
    dev_b = (s, x_b, c)
    has_prev = s > 0
    has_next = s < 7
    dev_prev = (jnp.maximum(s - 1, 0), x, c)
    dev_next = (jnp.minimum(s + 1, 7), x, c)

    def m128(v):
        return pl.multiple_of(v, 128)

    def slab_of(xx):
        p = xx // 2
        return pl.ds(m128(PAIR * p + HEAD * (xx - 2 * p)), SLAB)

    def full_of(xx):
        p = xx // 2
        return pl.ds(m128(PAIR * p + 2 * HEAD * (xx - 2 * p)), HEAD)

    def pair_of(xx):
        return pl.ds(m128(PAIR * (xx // 2)), PAIR)

    own_slab = slab_of(x)
    in_pair = pl.ds(m128(HEAD * par), SLAB)
    in_pair_b = pl.ds(m128(HEAD * par_b), SLAB)
    own_full = pl.ds(m128(HEAD * par), HEAD)

    def block(xx, start=0, size=ROWS):
        half = xx // 2
        return half, pl.ds(m128(ROWS * (xx - 2 * half) + start), size)

    loads = []
    for src, dst in (
        (ks.at[0, :, own_slab], k2.at[(*block(x), in_pair)]),
        (qs.at[0, :, own_slab], q2.at[(*block(x), in_pair)]),
        (vs.at[0, :, own_slab], v2.at[(*block(x), in_pair)]),
        (cx.at[0], ctx.at[x]),
        (wo.at[0], wv),
    ):
        loads.append(pltpu.make_async_copy(src, dst, lsem.at[len(loads)]))
    for copy in loads:
        copy.start()

    barrier = pltpu.get_barrier_semaphore()
    for dev in (dev_r, dev_l, dev_z, dev_a, dev_b):
        pl.semaphore_signal(barrier, inc=1, device_id=dev, device_id_type=MESH)

    @pl.when(has_prev)
    def _():
        pl.semaphore_signal(barrier, inc=1, device_id=dev_prev, device_id_type=MESH)

    @pl.when(has_next)
    def _():
        pl.semaphore_signal(barrier, inc=1, device_id=dev_next, device_id_type=MESH)

    pl.semaphore_wait(barrier, 5 + has_prev.astype(jnp.int32) + has_next.astype(jnp.int32))

    def slot(yy, zz, q):
        return inc.at[zz, pl.ds(pl.multiple_of(PIECE * yy + CHUNK * q, CHUNK), CHUNK)]

    groups = [(z, y // 2), (z, 1 - y // 2), (zp, y // 2), (zp, 1 - y // 2)]

    moves = {}

    def move(tag, src, there, here, dev):
        moves[tag] = (len(moves), src, there, here, dev)

    for q in range(CHUNKS):
        move("E%d" % q, bg.at[0, pl.ds(CHUNK * q, CHUNK)], slot(y, z, q), slot(y, z, q), dev_prev)
        move("z%d" % q, slot(y, z, q), slot(y, z, q), slot(y, zp, q), dev_z)
        move("l_own%d" % q, slot(y, z, q), slot(y, z, q), slot(y_l, z, q), dev_r)
        move("r_own%d" % q, slot(y, z, q), slot(y, z, q), slot(y_r, z, q), dev_l)
        move("l_oth%d" % q, slot(y, zp, q), slot(y, zp, q), slot(y_l, zp, q), dev_r)
        move("r_oth%d" % q, slot(y, zp, q), slot(y, zp, q), slot(y_r, zp, q), dev_l)
        if q < CHUNKS // 2:
            move("o_own%d" % q, slot(y_l, z, q), slot(y_l, z, q), slot(y_o, z, q), dev_r)
            move("o_oth%d" % q, slot(y_o, z, q), slot(y_o, z, q), slot(y_o, zp, q), dev_z)
        else:
            move("o_own%d" % q, slot(y_r, z, q), slot(y_r, z, q), slot(y_o, z, q), dev_l)
            move("o_oth%d" % q, slot(y_r, zp, q), slot(y_r, zp, q), slot(y_o, zp, q), dev_l)

    for n, a, b in (("k", ks, k2), ("q", qs, q2), ("v", vs, v2)):
        to, from_a, from_b, from_c = block(x), block(x_a), block(x_b), block(x_c)
        move(n + "A", a.at[0, :, pair_of(x_a)], b.at[to], b.at[from_a], dev_a)
        move(n + "B", a.at[0, :, slab_of(x_b)], b.at[(*to, in_pair_b)], b.at[(*from_b, in_pair)], dev_b)
        move(n + "C", b.at[(*from_a, in_pair_b)], b.at[(*from_a, in_pair_b)], b.at[(*from_c, in_pair)], dev_b)
    move("cA", cx.at[0], ctx.at[x], ctx.at[x_a], dev_a)
    move("cB", cx.at[0], ctx.at[x], ctx.at[x_b], dev_b)
    lo, hi = pl.ds(0, LOW), pl.ds(LOW, ROWS - LOW)
    move("cC0", ctx.at[x_a, lo], ctx.at[x_a, lo], ctx.at[x_c, lo], dev_b)
    move("cC1", ctx.at[x_b, hi], ctx.at[x_b, hi], ctx.at[x_c, hi], dev_a)
    for k in range(4):
        move("rsA%d" % k, partb.at[k, pair_of(x_a)], got_a.at[k], got_a.at[k], dev_a)
        move("rsB%d" % k, sumb.at[k], got_b.at[k], got_b.at[k], dev_b)

    def move_out(n, src, dst, start, size, where):
        rows = pl.ds(start, size)
        hop = stage.at[where, pl.ds(0, size)]
        to_a, to_b, to_c = (block(xx, start, size) for xx in (x_a, x_b, x_c))
        move(n + "1", src.at[(*to_c, own_full)], hop, hop, dev_b)
        move(n + "A", src.at[to_a], dst.at[0, rows, own_slab], dst.at[0, rows, slab_of(x_a)], dev_a)
        move(n + "B", src.at[(*to_b, own_full)], dst.at[0, rows, full_of(x)], dst.at[0, rows, full_of(x_b)], dev_b)
        move(n + "C", hop, dst.at[0, rows, full_of(x_b)], dst.at[0, rows, full_of(x_c)], dev_a)

    move_out("dk", dkb, gk, 0, ROWS, 0)
    move_out("dv", dvb, gv, 0, ROWS, 1)
    move_out("dqe", dqb, gq, m128(PIECE * z), PIECE, 2)
    move_out("dql", dqb, gq, m128(PIECE * zp), PIECE, 3)

    def outgoing(tag):
        i, src, there, _, dev = moves[tag]
        return pltpu.make_async_remote_copy(src, there, send.at[i], recv.at[i], device_id=dev, device_id_type=MESH)

    def arriving(tag):
        i, _, _, here, dev = moves[tag]
        return pltpu.make_async_remote_copy(here, here, send.at[i], recv.at[i], device_id=dev, device_id_type=MESH)

    def entry_kept(q):
        return pltpu.make_async_copy(bg.at[0, pl.ds(CHUNK * q, CHUNK)], slot(y, z, q), esem.at[q])

    def emit_send(tag):
        if tag[0] == "E":
            h = int(tag[1])

            @pl.when(has_prev)
            def _():
                outgoing(tag).start()

            @pl.when(jnp.logical_not(has_next))
            def _():
                entry_kept(h).start()
        else:
            outgoing(tag).start()

    def emit_wait(tag):
        if tag[0] == "E":
            h = int(tag[1])

            @pl.when(has_next)
            def _():
                arriving(tag).wait_recv()

            @pl.when(jnp.logical_not(has_next))
            def _():
                entry_kept(h).wait()
        elif tag[0] == "@":
            loads[int(tag[1])].wait()
        else:
            arriving(tag).wait_recv()

    def group_rows(g):
        zz, p = g
        return p, zz, pl.ds(m128(PIECE * zz), PIECE), pl.ds(m128(ROWS + PIECE * zz), PIECE)

    def partial_grad(k):
        zz, p = groups[k]
        tokens = pl.ds(pl.multiple_of(ROWS * p, ROWS), ROWS)
        r = dot(wv[...], inc[zz, tokens], 1, 1)
        part[k] = r
        partb[k] = r.astype(BF16)

    def pass_on(k):
        r = part[k, slab_of(x_b)] + got_a[k, in_pair_b].astype(F32)
        sumb[k] = r.astype(BF16)

    heads = [pl.ds(HEAD * h, HEAD) for h in range(2)]
    pheads = [pl.ds(m128(HEAD * (par + h)), HEAD) for h in range(2)]

    def softmax(k):
        p, zz, rows0, rows1 = group_rows(groups[k])
        row = lax.broadcasted_iota(jnp.int32, (KEYS, ROWS), 0)
        lane = lax.broadcasted_iota(jnp.int32, (KEYS, ROWS), 1)
        ahead = jnp.where(lane < PIECE, lane, lane + PIECE) - row
        if k == 0:
            for j in range(2):
                for h in range(2):
                    kt[j, heads[h]] = k2[j, :, pheads[h]].T
        for h in range(2):
            qg[k, 0:PIECE, heads[h]] = q2[p, rows0, pheads[h]]
            qg[k, PIECE:ROWS, heads[h]] = q2[p, rows1, pheads[h]]

        def scores(j, tops):
            result = []
            ok = ahead >= KEYS * (j - p) - PIECE * zz
            for h in range(2):
                sc = dot(k2[j, :, pheads[h]], qg[k, :, heads[h]], 1, 1) * SCALE
                sc = jnp.where(ok, sc, -jnp.inf)
                pt[h, k, j] = sc
                result.append(jnp.maximum(tops[h], jnp.max(sc, axis=0, keepdims=True)))
            return tuple(result)

        low = jnp.full((1, ROWS), -jnp.inf, F32)
        tops = lax.fori_loop(0, p + 1, scores, (low, low))

        def weights(j, sums):
            result = []
            for h in range(2):
                e = jnp.exp(pt[h, k, j] - tops[h])
                pt[h, k, j] = e
                result.append(sums[h] + jnp.sum(e, axis=0, keepdims=True))
            return tuple(result)

        none = jnp.zeros((1, ROWS), F32)
        sums = lax.fori_loop(0, p + 1, weights, (none, none))
        for h in range(2):
            linv[k, h : h + 1] = 1.0 / sums[h]

    def turn(k):
        p, _, rows, _ = group_rows(groups[k])
        ctxt[k // 2, :, pl.ds(m128(ROWS * p), PIECE)] = ctx[2 * p, rows].T
        ctxt[k // 2, :, pl.ds(m128(ROWS * p + PIECE), PIECE)] = ctx[2 * p + 1, rows].T

    def weight_grad(i, half):
        zz = (z, zp)[i]

        @pl.loop(0, FEAT // TILE // 2)
        def _(n):
            cols = pl.ds(pl.multiple_of(half * (FEAT // 2) + n * TILE, TILE), TILE)
            r = dot(ctxt[i], inc[zz, :, cols], 1, 0)
            if i == 0:
                acc[:, cols] = r
            else:
                gw[0, :, cols] = (r + acc[:, cols]).astype(BF16)

    def attend(k):
        p, _, rows0, rows1 = group_rows(groups[k])
        if k == 0:
            dka[...] = jnp.zeros_like(dka)
            dva[...] = jnp.zeros_like(dva)
        grad = part[k, own_slab] + got_a[k, in_pair].astype(F32) + got_b[k].astype(F32)
        gb = grad.astype(BF16)
        dout[...] = gb
        tokens = pl.ds(pl.multiple_of(ROWS * p, ROWS), ROWS)
        prod = gb.astype(F32) * ctxt[k // 2, own_slab, tokens].astype(F32)
        deltas = [jnp.sum(prod[HEAD * h : HEAD * (h + 1)], axis=0, keepdims=True) for h in range(2)]
        inv = [linv[k, h : h + 1] for h in range(2)]
        dqa[...] = jnp.zeros_like(dqa)

        @pl.loop(0, p + 1)
        def _(j):
            for h in range(2):
                gh = dout[heads[h]]
                w = pt[h, k, j] * inv[h]
                dp = dot(v2[j, :, pheads[h]], gh, 1, 0)
                ds = (w * (dp - deltas[h])).astype(BF16)
                dva[j, :, heads[h]] += dot(w.astype(BF16), gh, 1, 1)
                dka[j, :, heads[h]] += dot(ds, qg[k, :, heads[h]], 1, 0)
                dqa[heads[h]] += dot(kt[j, heads[h]], ds, 1, 0)

        dq = (dqa[...] * SCALE).astype(BF16).T
        dqb[p, rows0] = dq[0:PIECE]
        dqb[p, rows1] = dq[PIECE:ROWS]

    def cast_keys():
        dkb[...] = (dka[...] * SCALE).astype(BF16)

    def cast_values():
        dvb[...] = dva[...].astype(BF16)

    table = {
        "cA": ([], None, ["cA"]),
        "cB": ([], None, ["cB"]),
        "cfA": (["cA"], None, ["cC0"]),
        "cfB": (["cB"], None, ["cC1"]),
        "dq": ([], None, ["dqe1", "dqeA", "dqeB"]),
        "dqf": (["dqe1"], None, ["dqeC"]),
        "dk": ([], cast_keys, ["dk1", "dkA", "dkB"]),
        "dv": ([], cast_values, ["dv1", "dvA", "dvB"]),
        "dql": ([], None, ["dql1", "dqlA", "dqlB"]),
        "dkf": (["dk1"], None, ["dkC"]),
        "dvf": (["dv1"], None, ["dvC"]),
        "dqlf": (["dql1"], None, ["dqlC"]),
        "gA": ([], lambda: weight_grad(0, 0), []),
        "gB": ([], lambda: weight_grad(0, 1), []),
        "gC": ([], lambda: weight_grad(1, 0), []),
        "gD": ([], lambda: weight_grad(1, 1), []),
    }
    for n in "kqv":
        table[n] = ([], None, [n + "A", n + "B"])
        table[n + "f"] = ([n + "A"], None, [n + "C"])
    own, near, far, near_z, far_z = [], [], [], [], []
    for q in range(CHUNKS):
        i = str(q)
        first = q < CHUNKS // 2
        table["E" + i] = ([], None, ["E" + i])
        table["r" + i] = (["E" + i], None, ["l_own" + i])
        table["l" + i] = (["E" + i], None, ["r_own" + i])
        table["z" + i] = (["E" + i], None, ["z" + i])
        table["R" + i] = (["z" + i], None, ["l_oth" + i])
        table["L" + i] = (["z" + i], None, ["r_oth" + i])
        table["f" + i] = (["l_own" + i] if first else ["r_own" + i], None, ["o_own" + i])
        table["F" + i] = (["o_own" + i] if first else ["r_oth" + i], None, ["o_oth" + i])
        own += ["E" + i]
        near += ["l_own" + i, "r_own" + i]
        far += ["o_own" + i]
        near_z += ["z" + i, "l_oth" + i, "r_oth" + i]
        far_z += ["o_oth" + i]
    for k, need in enumerate((["@4"] + own + near, far, near_z, far_z)):
        table["p%d" % k] = (need, lambda k=k: partial_grad(k), ["rsA%d" % k])
        table["s%d" % k] = (["rsA%d" % k], lambda k=k: pass_on(k), ["rsB%d" % k])
        table["P%d" % k] = (["@0", "@1", "kA", "kB", "kC", "qA", "qB", "qC"], lambda k=k: softmax(k), [])
        table["t%d" % k] = (["@3", "cA", "cB", "cC0", "cC1"], lambda k=k: turn(k), [])
        table["a%d" % k] = (["@2", "vA", "vB", "vC", "rsB%d" % k], lambda k=k: attend(k), [])

    def perform(order):
        seen = set()
        for name in order:
            waits, work, sends = table[name]
            for tag in waits:
                if tag not in seen:
                    seen.add(tag)
                    emit_wait(tag)
            if work is not None:
                work()
            for tag in sends:
                emit_send(tag)
        for n, (b, g) in enumerate(((dqb, gq), (dkb, gk), (dvb, gv))):
            pltpu.make_async_copy(b.at[block(x)], g.at[0, :, own_slab], osem.at[n]).start()

    for n, order in enumerate((ORDER0, ORDER1)):
        pl.when(core == n)(lambda order=order: perform(order))

    for n in ("dqe", "dk", "dv", "dql"):
        for tail in "ABC":
            emit_wait(n + tail)
    for n, (b, g) in enumerate(((dqb, gq), (dkb, gk), (dvb, gv))):
        pltpu.make_async_copy(b.at[block(x)], g.at[0, :, own_slab], osem.at[n]).wait()
    for tag in moves:
        if tag[0] == "E":

            @pl.when(has_prev)
            def _():
                outgoing(tag).wait_send()
        else:
            outgoing(tag).wait_send()


N_MOVES = 8 * CHUNKS + 9 + 4 + 8 + 16


def write_out(gw, gq, gk, gv, gw_out, gq_out, gk_out, gv_out, sems):
    copies = []
    for n in range(6):
        rows = pl.ds(n * (WIDTH // 6), WIDTH // 6)
        copies.append(pltpu.make_async_copy(gw.at[0, rows], gw_out.at[0, rows], sems.at[n]))
    for n, (src, dst) in enumerate(((gq, gq_out), (gk, gk_out), (gv, gv_out))):
        copies.append(pltpu.make_async_copy(src, dst, sems.at[6 + n]))
    for copy in copies:
        copy.start()
    for copy in copies:
        copy.wait()


def local(boundary_grad, w_out, context, queries, keys, values):
    any_spec = pl.BlockSpec(memory_space=pl.ANY)
    vmem_spec = pl.BlockSpec(memory_space=pltpu.VMEM)
    shapes = [(1, WIDTH, FEAT), (1, ROWS, WIDTH), (1, ROWS, WIDTH), (1, ROWS, WIDTH)]
    grads = pl.pallas_call(
        kernel,
        out_shape=[pltpu.VMEM(shape, BF16) for shape in shapes],
        in_specs=[any_spec] * 6,
        out_specs=[vmem_spec] * 4,
        scratch_shapes=[
            pltpu.VMEM((2, KEYS, FEAT), BF16),
            pltpu.VMEM((WIDTH, FEAT), BF16),
            pltpu.VMEM((4, ROWS, WIDTH), BF16),
            pltpu.VMEM((2, WIDTH, KEYS), BF16),
            pltpu.VMEM((WIDTH, FEAT), F32),
            pltpu.VMEM((2, KEYS, PAIR), BF16),
            pltpu.VMEM((2, KEYS, PAIR), BF16),
            pltpu.VMEM((2, KEYS, PAIR), BF16),
            pltpu.VMEM((4, ROWS, SLAB), BF16),
            pltpu.VMEM((4, WIDTH, ROWS), F32),
            pltpu.VMEM((4, WIDTH, ROWS), BF16),
            pltpu.VMEM((4, PAIR, ROWS), BF16),
            pltpu.VMEM((4, SLAB, ROWS), BF16),
            pltpu.VMEM((4, SLAB, ROWS), BF16),
            pltpu.VMEM((2, SLAB, KEYS), BF16),
            pltpu.VMEM((2, 4, 2, KEYS, ROWS), F32),
            pltpu.VMEM((4, 8, ROWS), F32),
            pltpu.VMEM((ROWS, SLAB), BF16),
            pltpu.VMEM((ROWS, SLAB), F32),
            pltpu.VMEM((2, KEYS, SLAB), F32),
            pltpu.VMEM((2, KEYS, SLAB), F32),
            pltpu.VMEM((2, KEYS, SLAB), BF16),
            pltpu.VMEM((2, KEYS, SLAB), BF16),
            pltpu.VMEM((2, KEYS, SLAB), BF16),
            pltpu.VMEM((4, ROWS, HEAD), BF16),
            pltpu.SemaphoreType.DMA((N_MOVES,)),
            pltpu.SemaphoreType.DMA((N_MOVES,)),
            pltpu.SemaphoreType.DMA((5,)),
            pltpu.SemaphoreType.DMA((CHUNKS,)),
            pltpu.SemaphoreType.DMA((3,)),
        ],
        compiler_params=pltpu.CompilerParams(
            collective_id=0, has_side_effects=True, vmem_limit_bytes=54 * 1024 * 1024
        ),
    )(boundary_grad, w_out, context, queries, keys, values)
    return pl.pallas_call(
        write_out,
        out_shape=[jax.ShapeDtypeStruct(shape, BF16) for shape in shapes],
        in_specs=[any_spec] * 4,
        out_specs=[any_spec] * 4,
        scratch_shapes=[pltpu.SemaphoreType.DMA((9,))],
        compiler_params=pltpu.CompilerParams(vmem_limit_bytes=1024 * 1024),
    )(*grads)


def solution(mesh):
    in_specs = (
        P("section", "col", "row"),
        P("section", "col", "row"),
        P("section", "row", "col"),
        P("section", "row", "col"),
        P("section", "row", "col"),
        P("section", "row", "col"),
    )
    out_specs = (
        P("section", "col", "row"),
        P("section", "row", "col"),
        P("section", "row", "col"),
        P("section", "row", "col"),
    )
    return jax.shard_map(local, mesh=mesh, in_specs=in_specs, out_specs=out_specs, check_vma=False)
```

```python
import jax
import jax.numpy as jnp
from jax import lax
from jax.experimental import pallas as pl
from jax.experimental.pallas import tpu as pltpu
from jax.sharding import PartitionSpec as P

HEAD = 128
SCALE = HEAD ** (-0.5)
MESH = pl.DeviceIdType.MESH
BF16 = jnp.bfloat16
F32 = jnp.float32

ROWS = 256
PIECE = 128
CHUNKS = 2
CHUNK = PIECE // CHUNKS
LOW = 192
KEYS = 512
FEAT = 3072
WIDTH = 768
PAIR = 384
SLAB = 256
TILE = 512

ORDER0 = [
    "E0", "l0", "r0", "q", "cA", "l1", "f0", "E1", "qf", "k", "f1", "cB", "r1", "z1", "kf", "F0", "R1", "z0", "cfB",
    "L1", "p0", "cfA", "v", "p1", "R0", "L0", "P0", "s0", "t0", "P1", "t1", "F1", "t2", "P2", "vf", "P3", "gA",
    "s1", "p2", "gB", "a0", "p3", "p4", "s2", "a1", "t3", "dq", "s3", "s4", "gC", "a2", "dqf", "a3", "dk", "dv",
    "dql", "gD", "dkf", "dvf", "dqlf",
]
ORDER1 = [
    "E0", "cB", "k", "q", "cA", "E1", "cfB", "qf", "v", "l0", "r0", "f0", "cfA", "kf", "l1", "r1", "t0", "f1", "t1",
    "z1", "P0", "vf", "P1", "p0", "t2", "L1", "z0", "P2", "s0", "R1", "F0", "p1", "gA", "R0", "L0", "t3", "gB",
    "s1", "F1", "P3", "a0", "a1", "dq", "p2", "p3", "p4", "s2", "gC", "dqf", "s3", "s4", "gD", "a2", "a3", "dk",
    "dv", "dql", "dkf", "dvf", "dqlf",
]


def dot(a, b, ca, cb):
    return lax.dot_general(a, b, (((ca,), (cb,)), ((), ())), preferred_element_type=F32)


def kernel(
    bg, wo, cx, qs, ks, vs,
    gw, gq, gk, gv,
    inc, wv, ctx, ctxt, acc, q2, k2, v2, qg, part, partb, got_a, got_b, sumb, part1, partb1, got_a1, got_b1, sumb1, kt, pt, linv, dout,
    dqa, dka, dva, dqb, dkb, dvb, stage,
    send, recv, lsem, esem, osem,
):
    s = lax.axis_index("section")
    x = lax.axis_index("row")
    c = lax.axis_index("col")
    y = c // 2
    z = c - 2 * y
    core = s - 2 * (s // 2)
    y_r = lax.rem(y + 1 + 2 * core, 4)
    y_l = lax.rem(y + 3 + 2 * core, 4)
    y_o = lax.rem(y + 2, 4)
    y_n = y_o + 1 - 2 * lax.rem(y_o, 2)
    zp = 1 - z
    pair = x // 2
    par = x - 2 * pair
    par_b = 1 - par
    x_a = 3 - x
    x_b = 2 * pair + par_b
    x_c = lax.rem(x + 2, 4)
    dev_r = (s, x, 2 * y_r + z)
    dev_l = (s, x, 2 * y_l + z)
    dev_z = (s, x, 2 * y + zp)
    dev_a = (s, x_a, c)
    dev_b = (s, x_b, c)
    has_prev = s > 0
    has_next = s < 7
    dev_prev = (jnp.maximum(s - 1, 0), x, c)
    dev_next = (jnp.minimum(s + 1, 7), x, c)

    def m128(v):
        return pl.multiple_of(v, 128)

    def slab_of(xx):
        p = xx // 2
        return pl.ds(m128(PAIR * p + HEAD * (xx - 2 * p)), SLAB)

    def full_of(xx):
        p = xx // 2
        return pl.ds(m128(PAIR * p + 2 * HEAD * (xx - 2 * p)), HEAD)

    def pair_of(xx):
        return pl.ds(m128(PAIR * (xx // 2)), PAIR)

    own_slab = slab_of(x)
    in_pair = pl.ds(m128(HEAD * par), SLAB)
    in_pair_b = pl.ds(m128(HEAD * par_b), SLAB)
    own_full = pl.ds(m128(HEAD * par), HEAD)

    def block(xx, start=0, size=ROWS):
        half = xx // 2
        return half, pl.ds(m128(ROWS * (xx - 2 * half) + start), size)

    loads = []
    for src, dst in (
        (ks.at[0, :, own_slab], k2.at[(*block(x), in_pair)]),
        (qs.at[0, :, own_slab], q2.at[(*block(x), in_pair)]),
        (vs.at[0, :, own_slab], v2.at[(*block(x), in_pair)]),
        (cx.at[0], ctx.at[x]),
        (wo.at[0], wv),
    ):
        loads.append(pltpu.make_async_copy(src, dst, lsem.at[len(loads)]))
    for copy in loads:
        copy.start()

    barrier = pltpu.get_barrier_semaphore()
    for dev in (dev_r, dev_l, dev_z, dev_a, dev_b):
        pl.semaphore_signal(barrier, inc=1, device_id=dev, device_id_type=MESH)

    @pl.when(has_prev)
    def _():
        pl.semaphore_signal(barrier, inc=1, device_id=dev_prev, device_id_type=MESH)

    @pl.when(has_next)
    def _():
        pl.semaphore_signal(barrier, inc=1, device_id=dev_next, device_id_type=MESH)

    pl.semaphore_wait(barrier, 5 + has_prev.astype(jnp.int32) + has_next.astype(jnp.int32))

    def slot(yy, zz, q):
        return inc.at[zz, pl.ds(pl.multiple_of(PIECE * yy + CHUNK * q, CHUNK), CHUNK)]

    groups = [(z, y // 2), (z, 1 - y // 2), (zp, y // 2), (zp, 1 - y // 2)]

    moves = {}

    def move(tag, src, there, here, dev):
        moves[tag] = (len(moves), src, there, here, dev)

    def sums_of(k):
        return (partb, got_a, sumb, got_b) if k < 3 else (partb1, got_a1, sumb1, got_b1)

    for q in range(CHUNKS):
        move("E%d" % q, bg.at[0, pl.ds(CHUNK * q, CHUNK)], slot(y, z, q), slot(y, z, q), dev_prev)
        move("z%d" % q, slot(y, z, q), slot(y, z, q), slot(y, zp, q), dev_z)
        move("l_own%d" % q, slot(y, z, q), slot(y, z, q), slot(y_l, z, q), dev_r)
        move("r_own%d" % q, slot(y, z, q), slot(y, z, q), slot(y_r, z, q), dev_l)
        move("l_oth%d" % q, slot(y, zp, q), slot(y, zp, q), slot(y_l, zp, q), dev_r)
        move("r_oth%d" % q, slot(y, zp, q), slot(y, zp, q), slot(y_r, zp, q), dev_l)
        if q < CHUNKS // 2:
            move("o_own%d" % q, slot(y_l, z, q), slot(y_l, z, q), slot(y_o, z, q), dev_r)
            move("o_oth%d" % q, slot(y_o, z, q), slot(y_o, z, q), slot(y_o, zp, q), dev_z)
        else:
            move("o_own%d" % q, slot(y_r, z, q), slot(y_r, z, q), slot(y_o, z, q), dev_l)
            move("o_oth%d" % q, slot(y_r, zp, q), slot(y_r, zp, q), slot(y_o, zp, q), dev_l)

    for n, a, b in (("k", ks, k2), ("q", qs, q2), ("v", vs, v2)):
        to, from_a, from_b, from_c = block(x), block(x_a), block(x_b), block(x_c)
        move(n + "A", a.at[0, :, pair_of(x_a)], b.at[to], b.at[from_a], dev_a)
        move(n + "B", a.at[0, :, slab_of(x_b)], b.at[(*to, in_pair_b)], b.at[(*from_b, in_pair)], dev_b)
        move(n + "C", b.at[(*from_a, in_pair_b)], b.at[(*from_a, in_pair_b)], b.at[(*from_c, in_pair)], dev_b)
    move("cA", cx.at[0], ctx.at[x], ctx.at[x_a], dev_a)
    move("cB", cx.at[0], ctx.at[x], ctx.at[x_b], dev_b)
    lo, hi = pl.ds(0, LOW), pl.ds(LOW, ROWS - LOW)
    move("cC0", ctx.at[x_a, lo], ctx.at[x_a, lo], ctx.at[x_c, lo], dev_b)
    move("cC1", ctx.at[x_b, hi], ctx.at[x_b, hi], ctx.at[x_c, hi], dev_a)
    for k in range(5):
        src, first, total, second = (r.at[k] if k < 3 else r.at[k - 3] for r in (sums_of(k)))
        move("rsA%d" % k, src.at[pair_of(x_a)], first, first, dev_a)
        move("rsB%d" % k, total, second, second, dev_b)

    def move_out(n, src, dst, start, size, where):
        rows = pl.ds(start, size)
        hop = stage.at[where, pl.ds(0, size)]
        to_a, to_b, to_c = (block(xx, start, size) for xx in (x_a, x_b, x_c))
        move(n + "1", src.at[(*to_c, own_full)], hop, hop, dev_b)
        move(n + "A", src.at[to_a], dst.at[0, rows, own_slab], dst.at[0, rows, slab_of(x_a)], dev_a)
        move(n + "B", src.at[(*to_b, own_full)], dst.at[0, rows, full_of(x)], dst.at[0, rows, full_of(x_b)], dev_b)
        move(n + "C", hop, dst.at[0, rows, full_of(x_b)], dst.at[0, rows, full_of(x_c)], dev_a)

    move_out("dk", dkb, gk, 0, ROWS, 0)
    move_out("dv", dvb, gv, 0, ROWS, 1)
    move_out("dqe", dqb, gq, m128(PIECE * z), PIECE, 2)
    move_out("dql", dqb, gq, m128(PIECE * zp), PIECE, 3)

    def outgoing(tag):
        i, src, there, _, dev = moves[tag]
        return pltpu.make_async_remote_copy(src, there, send.at[i], recv.at[i], device_id=dev, device_id_type=MESH)

    def arriving(tag):
        i, _, _, here, dev = moves[tag]
        return pltpu.make_async_remote_copy(here, here, send.at[i], recv.at[i], device_id=dev, device_id_type=MESH)

    def entry_kept(q):
        return pltpu.make_async_copy(bg.at[0, pl.ds(CHUNK * q, CHUNK)], slot(y, z, q), esem.at[q])

    def emit_send(tag):
        if tag[0] == "E":
            h = int(tag[1])

            @pl.when(has_prev)
            def _():
                outgoing(tag).start()

            @pl.when(jnp.logical_not(has_next))
            def _():
                entry_kept(h).start()
        else:
            outgoing(tag).start()

    def emit_wait(tag):
        if tag[0] == "E":
            h = int(tag[1])

            @pl.when(has_next)
            def _():
                arriving(tag).wait_recv()

            @pl.when(jnp.logical_not(has_next))
            def _():
                entry_kept(h).wait()
        elif tag[0] == "@":
            loads[int(tag[1])].wait()
        else:
            arriving(tag).wait_recv()

    def group_rows(g):
        zz, p = g
        return p, zz, pl.ds(m128(PIECE * zz), PIECE), pl.ds(m128(ROWS + PIECE * zz), PIECE)

    def partial_grad(k):
        if k < 3:
            zz, p = groups[k]
            r = dot(wv[...], inc[zz, pl.ds(pl.multiple_of(ROWS * p, ROWS), ROWS)], 1, 1)
            part[k] = r
            partb[k] = r.astype(BF16)
        else:
            yy = (y_n, y_o)[k - 3]
            r = dot(wv[...], inc[zp, pl.ds(m128(PIECE * yy), PIECE)], 1, 1)
            part1[k - 3] = r
            partb1[k - 3] = r.astype(BF16)

    def pass_on(k):
        if k < 3:
            sumb[k] = (part[k, slab_of(x_b)] + got_a[k, in_pair_b].astype(F32)).astype(BF16)
        else:
            i = k - 3
            sumb1[i] = (part1[i, slab_of(x_b)] + got_a1[i, in_pair_b].astype(F32)).astype(BF16)

    heads = [pl.ds(HEAD * h, HEAD) for h in range(2)]
    pheads = [pl.ds(m128(HEAD * (par + h)), HEAD) for h in range(2)]

    def softmax(k):
        p, zz, rows0, rows1 = group_rows(groups[k])
        row = lax.broadcasted_iota(jnp.int32, (KEYS, ROWS), 0)
        lane = lax.broadcasted_iota(jnp.int32, (KEYS, ROWS), 1)
        ahead = jnp.where(lane < PIECE, lane, lane + PIECE) - row
        if k == 0:
            for j in range(2):
                for h in range(2):
                    kt[j, heads[h]] = k2[j, :, pheads[h]].T
        for h in range(2):
            qg[k, 0:PIECE, heads[h]] = q2[p, rows0, pheads[h]]
            qg[k, PIECE:ROWS, heads[h]] = q2[p, rows1, pheads[h]]

        def scores(j, tops):
            result = []
            ok = ahead >= KEYS * (j - p) - PIECE * zz
            for h in range(2):
                sc = dot(k2[j, :, pheads[h]], qg[k, :, heads[h]], 1, 1) * SCALE
                sc = jnp.where(ok, sc, -jnp.inf)
                pt[h, k, j] = sc
                result.append(jnp.maximum(tops[h], jnp.max(sc, axis=0, keepdims=True)))
            return tuple(result)

        low = jnp.full((1, ROWS), -jnp.inf, F32)
        tops = lax.fori_loop(0, p + 1, scores, (low, low))

        def weights(j, sums):
            result = []
            for h in range(2):
                e = jnp.exp(pt[h, k, j] - tops[h])
                pt[h, k, j] = e
                result.append(sums[h] + jnp.sum(e, axis=0, keepdims=True))
            return tuple(result)

        none = jnp.zeros((1, ROWS), F32)
        sums = lax.fori_loop(0, p + 1, weights, (none, none))
        for h in range(2):
            linv[k, h : h + 1] = 1.0 / sums[h]

    def turn(k):
        p, _, rows, _ = group_rows(groups[k])
        ctxt[k // 2, :, pl.ds(m128(ROWS * p), PIECE)] = ctx[2 * p, rows].T
        ctxt[k // 2, :, pl.ds(m128(ROWS * p + PIECE), PIECE)] = ctx[2 * p + 1, rows].T

    def weight_grad(i, half):
        zz = (z, zp)[i]

        @pl.loop(0, FEAT // TILE // 2)
        def _(n):
            cols = pl.ds(pl.multiple_of(half * (FEAT // 2) + n * TILE, TILE), TILE)
            r = dot(ctxt[i], inc[zz, :, cols], 1, 0)
            if i == 0:
                acc[:, cols] = r
            else:
                gw[0, :, cols] = (r + acc[:, cols]).astype(BF16)

    def attend(k):
        p, _, rows0, rows1 = group_rows(groups[k])
        if k == 0:
            dka[...] = jnp.zeros_like(dka)
            dva[...] = jnp.zeros_like(dva)
        if k < 3:
            dout[...] = (part[k, own_slab] + got_a[k, in_pair].astype(F32) + got_b[k].astype(F32)).astype(BF16)
        else:
            for i, yy in enumerate((y_n, y_o)):
                r = part1[i, own_slab] + got_a1[i, in_pair].astype(F32) + got_b1[i].astype(F32)
                dout[:, pl.ds(m128(PIECE * lax.rem(yy, 2)), PIECE)] = r.astype(BF16)
        tokens = pl.ds(pl.multiple_of(ROWS * p, ROWS), ROWS)
        prod = dout[...].astype(F32) * ctxt[k // 2, own_slab, tokens].astype(F32)
        deltas = [jnp.sum(prod[HEAD * h : HEAD * (h + 1)], axis=0, keepdims=True) for h in range(2)]
        inv = [linv[k, h : h + 1] for h in range(2)]
        dqa[...] = jnp.zeros_like(dqa)

        @pl.loop(0, p + 1)
        def _(j):
            for h in range(2):
                gh = dout[heads[h]]
                w = pt[h, k, j] * inv[h]
                dp = dot(v2[j, :, pheads[h]], gh, 1, 0)
                ds = (w * (dp - deltas[h])).astype(BF16)
                dva[j, :, heads[h]] += dot(w.astype(BF16), gh, 1, 1)
                dka[j, :, heads[h]] += dot(ds, qg[k, :, heads[h]], 1, 0)
                dqa[heads[h]] += dot(kt[j, heads[h]], ds, 1, 0)

        dq = (dqa[...] * SCALE).astype(BF16).T
        dqb[p, rows0] = dq[0:PIECE]
        dqb[p, rows1] = dq[PIECE:ROWS]

    def cast_keys():
        dkb[...] = (dka[...] * SCALE).astype(BF16)

    def cast_values():
        dvb[...] = dva[...].astype(BF16)

    table = {
        "cA": ([], None, ["cA"]),
        "cB": ([], None, ["cB"]),
        "cfA": (["cA"], None, ["cC0"]),
        "cfB": (["cB"], None, ["cC1"]),
        "dq": ([], None, ["dqe1", "dqeA", "dqeB"]),
        "dqf": (["dqe1"], None, ["dqeC"]),
        "dk": ([], cast_keys, ["dk1", "dkA", "dkB"]),
        "dv": ([], cast_values, ["dv1", "dvA", "dvB"]),
        "dql": ([], None, ["dql1", "dqlA", "dqlB"]),
        "dkf": (["dk1"], None, ["dkC"]),
        "dvf": (["dv1"], None, ["dvC"]),
        "dqlf": (["dql1"], None, ["dqlC"]),
        "gA": ([], lambda: weight_grad(0, 0), []),
        "gB": ([], lambda: weight_grad(0, 1), []),
        "gC": ([], lambda: weight_grad(1, 0), []),
        "gD": ([], lambda: weight_grad(1, 1), []),
    }
    for n in "kqv":
        table[n] = ([], None, [n + "A", n + "B"])
        table[n + "f"] = ([n + "A"], None, [n + "C"])
    own, near, far, near_z, far_z = [], [], [], [], []
    for q in range(CHUNKS):
        i = str(q)
        first = q < CHUNKS // 2
        table["E" + i] = ([], None, ["E" + i])
        table["r" + i] = (["E" + i], None, ["l_own" + i])
        table["l" + i] = (["E" + i], None, ["r_own" + i])
        table["z" + i] = (["E" + i], None, ["z" + i])
        table["R" + i] = (["z" + i], None, ["l_oth" + i])
        table["L" + i] = (["z" + i], None, ["r_oth" + i])
        table["f" + i] = (["l_own" + i] if first else ["r_own" + i], None, ["o_own" + i])
        table["F" + i] = (["o_own" + i] if first else ["r_oth" + i], None, ["o_oth" + i])
        own += ["E" + i]
        near += ["l_own" + i, "r_own" + i]
        far += ["o_own" + i]
        near_z += ["z" + i, "l_oth" + i, "r_oth" + i]
        far_z += ["o_oth" + i]
    for k, need in enumerate((["@4"] + own + near, far, near_z, near_z, far_z)):
        table["p%d" % k] = (need, lambda k=k: partial_grad(k), ["rsA%d" % k])
        table["s%d" % k] = (["rsA%d" % k], lambda k=k: pass_on(k), ["rsB%d" % k])
    for k in range(4):
        sums = ["rsB%d" % k] if k < 3 else ["rsB3", "rsB4"]
        table["P%d" % k] = (["@0", "@1", "kA", "kB", "kC", "qA", "qB", "qC"], lambda k=k: softmax(k), [])
        table["t%d" % k] = (["@3", "cA", "cB", "cC0", "cC1"], lambda k=k: turn(k), [])
        table["a%d" % k] = (["@2", "vA", "vB", "vC"] + sums, lambda k=k: attend(k), [])

    def perform(order):
        seen = set()
        for name in order:
            waits, work, sends = table[name]
            for tag in waits:
                if tag not in seen:
                    seen.add(tag)
                    emit_wait(tag)
            if work is not None:
                work()
            for tag in sends:
                emit_send(tag)
        for n, (b, g) in enumerate(((dqb, gq), (dkb, gk), (dvb, gv))):
            pltpu.make_async_copy(b.at[block(x)], g.at[0, :, own_slab], osem.at[n]).start()

    for n, order in enumerate((ORDER0, ORDER1)):
        pl.when(core == n)(lambda order=order: perform(order))

    for n in ("dqe", "dk", "dv", "dql"):
        for tail in "ABC":
            emit_wait(n + tail)
    for n, (b, g) in enumerate(((dqb, gq), (dkb, gk), (dvb, gv))):
        pltpu.make_async_copy(b.at[block(x)], g.at[0, :, own_slab], osem.at[n]).wait()
    for tag in moves:
        if tag[0] == "E":

            @pl.when(has_prev)
            def _():
                outgoing(tag).wait_send()
        else:
            outgoing(tag).wait_send()


N_MOVES = 8 * CHUNKS + 9 + 4 + 10 + 16


def write_out(gw, gq, gk, gv, gw_out, gq_out, gk_out, gv_out, sems):
    copies = []
    for n in range(6):
        rows = pl.ds(n * (WIDTH // 6), WIDTH // 6)
        copies.append(pltpu.make_async_copy(gw.at[0, rows], gw_out.at[0, rows], sems.at[n]))
    for n, (src, dst) in enumerate(((gq, gq_out), (gk, gk_out), (gv, gv_out))):
        copies.append(pltpu.make_async_copy(src, dst, sems.at[6 + n]))
    for copy in copies:
        copy.start()
    for copy in copies:
        copy.wait()


def local(boundary_grad, w_out, context, queries, keys, values):
    any_spec = pl.BlockSpec(memory_space=pl.ANY)
    vmem_spec = pl.BlockSpec(memory_space=pltpu.VMEM)
    shapes = [(1, WIDTH, FEAT), (1, ROWS, WIDTH), (1, ROWS, WIDTH), (1, ROWS, WIDTH)]
    grads = pl.pallas_call(
        kernel,
        out_shape=[pltpu.VMEM(shape, BF16) for shape in shapes],
        in_specs=[any_spec] * 6,
        out_specs=[vmem_spec] * 4,
        scratch_shapes=[
            pltpu.VMEM((2, KEYS, FEAT), BF16),
            pltpu.VMEM((WIDTH, FEAT), BF16),
            pltpu.VMEM((4, ROWS, WIDTH), BF16),
            pltpu.VMEM((2, WIDTH, KEYS), BF16),
            pltpu.VMEM((WIDTH, FEAT), F32),
            pltpu.VMEM((2, KEYS, PAIR), BF16),
            pltpu.VMEM((2, KEYS, PAIR), BF16),
            pltpu.VMEM((2, KEYS, PAIR), BF16),
            pltpu.VMEM((4, ROWS, SLAB), BF16),
            pltpu.VMEM((3, WIDTH, ROWS), F32),
            pltpu.VMEM((3, WIDTH, ROWS), BF16),
            pltpu.VMEM((3, PAIR, ROWS), BF16),
            pltpu.VMEM((3, SLAB, ROWS), BF16),
            pltpu.VMEM((3, SLAB, ROWS), BF16),
            pltpu.VMEM((2, WIDTH, PIECE), F32),
            pltpu.VMEM((2, WIDTH, PIECE), BF16),
            pltpu.VMEM((2, PAIR, PIECE), BF16),
            pltpu.VMEM((2, SLAB, PIECE), BF16),
            pltpu.VMEM((2, SLAB, PIECE), BF16),
            pltpu.VMEM((2, SLAB, KEYS), BF16),
            pltpu.VMEM((2, 4, 2, KEYS, ROWS), F32),
            pltpu.VMEM((4, 8, ROWS), F32),
            pltpu.VMEM((ROWS, SLAB), BF16),
            pltpu.VMEM((ROWS, SLAB), F32),
            pltpu.VMEM((2, KEYS, SLAB), F32),
            pltpu.VMEM((2, KEYS, SLAB), F32),
            pltpu.VMEM((2, KEYS, SLAB), BF16),
            pltpu.VMEM((2, KEYS, SLAB), BF16),
            pltpu.VMEM((2, KEYS, SLAB), BF16),
            pltpu.VMEM((4, ROWS, HEAD), BF16),
            pltpu.SemaphoreType.DMA((N_MOVES,)),
            pltpu.SemaphoreType.DMA((N_MOVES,)),
            pltpu.SemaphoreType.DMA((5,)),
            pltpu.SemaphoreType.DMA((CHUNKS,)),
            pltpu.SemaphoreType.DMA((3,)),
        ],
        compiler_params=pltpu.CompilerParams(
            collective_id=0, has_side_effects=True, vmem_limit_bytes=54 * 1024 * 1024
        ),
    )(boundary_grad, w_out, context, queries, keys, values)
    return pl.pallas_call(
        write_out,
        out_shape=[jax.ShapeDtypeStruct(shape, BF16) for shape in shapes],
        in_specs=[any_spec] * 4,
        out_specs=[any_spec] * 4,
        scratch_shapes=[pltpu.SemaphoreType.DMA((9,))],
        compiler_params=pltpu.CompilerParams(vmem_limit_bytes=1024 * 1024),
    )(*grads)


def solution(mesh):
    in_specs = (
        P("section", "col", "row"),
        P("section", "col", "row"),
        P("section", "row", "col"),
        P("section", "row", "col"),
        P("section", "row", "col"),
        P("section", "row", "col"),
    )
    out_specs = (
        P("section", "col", "row"),
        P("section", "row", "col"),
        P("section", "row", "col"),
        P("section", "row", "col"),
    )
    return jax.shard_map(local, mesh=mesh, in_specs=in_specs, out_specs=out_specs, check_vma=False)
```

```python
import jax
import jax.numpy as jnp
from jax import lax
from jax.experimental import pallas as pl
from jax.experimental.pallas import tpu as pltpu
from jax.sharding import PartitionSpec as P

HEAD = 128
SCALE = HEAD ** (-0.5)
EXP_SCALE = SCALE * 1.4426950408889634
MESH = pl.DeviceIdType.MESH
BF16 = jnp.bfloat16
F32 = jnp.float32

ROWS = 256
PIECE = 128
CHUNKS = 2
CHUNK = PIECE // CHUNKS
LOW = 192
KEYS = 512
FEAT = 3072
WIDTH = 768
PAIR = 384
SLAB = 256
TILE = 512

ORDER0 = [
    "cB", "E0", "cA", "k", "l1", "r0", "r1", "l0", "E1", "f1", "f0", "v", "p0", "z1", "cfB", "cfA", "z0", "t0",
    "t1", "q", "F0", "kf", "t2", "R1", "L1", "p1", "gA", "L0", "qf", "s0", "gB", "vf", "R0", "s1", "F1", "P0", "P1",
    "P2", "p2", "t3", "P3", "p3", "p4", "a0", "s2", "s3", "s4", "a1", "a2", "dq", "a3", "dqf", "dk", "dv", "dql",
    "sent", "gC", "dkf", "dqlf", "dvf", "gD",
]
ORDER1 = [
    "E1", "q", "cB", "k", "v", "E0", "kf", "cA", "r0", "l0", "cfB", "qf", "l1", "r1", "P0", "f0", "z1", "P1", "cfA",
    "z0", "f1", "P2", "p0", "P3", "t0", "t1", "s0", "t2", "F0", "p1", "L1", "vf", "R0", "gA", "L0", "R1", "a0",
    "s1", "gB", "F1", "a1", "dq", "p2", "p3", "p4", "s2", "t3", "s3", "s4", "dqf", "a2", "a3", "dql", "dv", "dk",
    "gC", "sent", "dvf", "dqlf", "gD", "dkf",
]
LAST = ("dk", "dv", "dq")


def dot(a, b, ca, cb):
    return lax.dot_general(a, b, (((ca,), (cb,)), ((), ())), preferred_element_type=F32)


def kernel(
    bg, wo, cx, qs, ks, vs,
    gw, gq, gk, gv,
    inc, wv, ctx, ctxt, acc, q2, k2, v2, qg, part, partb, got_a, got_b, sumb, part1, partb1, got_a1, got_b1, sumb1, kt, pt, linv, dout,
    dqa, dka, dva, dqb, dkb, dvb, stage,
    send, recv, lsem, esem, osem,
):
    s = lax.axis_index("section")
    x = lax.axis_index("row")
    c = lax.axis_index("col")
    y = c // 2
    z = c - 2 * y
    core = s - 2 * (s // 2)
    y_r = lax.rem(y + 1 + 2 * core, 4)
    y_l = lax.rem(y + 3 + 2 * core, 4)
    y_o = lax.rem(y + 2, 4)
    y_n = y_o + 1 - 2 * lax.rem(y_o, 2)
    zp = 1 - z
    pair = x // 2
    par = x - 2 * pair
    par_b = 1 - par
    x_a = 3 - x
    x_b = 2 * pair + par_b
    x_c = lax.rem(x + 2, 4)
    dev_r = (s, x, 2 * y_r + z)
    dev_l = (s, x, 2 * y_l + z)
    dev_z = (s, x, 2 * y + zp)
    dev_a = (s, x_a, c)
    dev_b = (s, x_b, c)
    has_prev = s > 0
    has_next = s < 7
    dev_prev = (jnp.maximum(s - 1, 0), x, c)
    dev_next = (jnp.minimum(s + 1, 7), x, c)

    def m128(v):
        return pl.multiple_of(v, 128)

    def slab_of(xx):
        p = xx // 2
        return pl.ds(m128(PAIR * p + HEAD * (xx - 2 * p)), SLAB)

    def full_of(xx):
        p = xx // 2
        return pl.ds(m128(PAIR * p + 2 * HEAD * (xx - 2 * p)), HEAD)

    def pair_of(xx):
        return pl.ds(m128(PAIR * (xx // 2)), PAIR)

    own_slab = slab_of(x)
    in_pair = pl.ds(m128(HEAD * par), SLAB)
    in_pair_b = pl.ds(m128(HEAD * par_b), SLAB)
    own_full = pl.ds(m128(HEAD * par), HEAD)

    def block(xx, start=0, size=ROWS):
        half = xx // 2
        return half, pl.ds(m128(ROWS * (xx - 2 * half) + start), size)

    loads = []
    for src, dst in (
        (ks.at[0, :, own_slab], k2.at[(*block(x), in_pair)]),
        (qs.at[0, :, own_slab], q2.at[(*block(x), in_pair)]),
        (vs.at[0, :, own_slab], v2.at[(*block(x), in_pair)]),
        (cx.at[0], ctx.at[x]),
        (wo.at[0], wv),
    ):
        loads.append(pltpu.make_async_copy(src, dst, lsem.at[len(loads)]))
    for copy in loads:
        copy.start()

    barrier = pltpu.get_barrier_semaphore()
    for dev in (dev_r, dev_l, dev_z, dev_a, dev_b):
        pl.semaphore_signal(barrier, inc=1, device_id=dev, device_id_type=MESH)

    @pl.when(has_prev)
    def _():
        pl.semaphore_signal(barrier, inc=1, device_id=dev_prev, device_id_type=MESH)

    @pl.when(has_next)
    def _():
        pl.semaphore_signal(barrier, inc=1, device_id=dev_next, device_id_type=MESH)

    pl.semaphore_wait(barrier, 5 + has_prev.astype(jnp.int32) + has_next.astype(jnp.int32))

    def slot(yy, zz, q):
        return inc.at[zz, pl.ds(pl.multiple_of(PIECE * yy + CHUNK * q, CHUNK), CHUNK)]

    groups = [(z, y // 2), (z, 1 - y // 2), (zp, y // 2), (zp, 1 - y // 2)]

    moves = {}

    def move(tag, src, there, here, dev):
        moves[tag] = (len(moves), src, there, here, dev)

    def sums_of(k):
        return (partb, got_a, sumb, got_b) if k < 3 else (partb1, got_a1, sumb1, got_b1)

    for q in range(CHUNKS):
        move("E%d" % q, bg.at[0, pl.ds(CHUNK * q, CHUNK)], slot(y, z, q), slot(y, z, q), dev_prev)
        move("z%d" % q, slot(y, z, q), slot(y, z, q), slot(y, zp, q), dev_z)
        move("l_own%d" % q, slot(y, z, q), slot(y, z, q), slot(y_l, z, q), dev_r)
        move("r_own%d" % q, slot(y, z, q), slot(y, z, q), slot(y_r, z, q), dev_l)
        move("l_oth%d" % q, slot(y, zp, q), slot(y, zp, q), slot(y_l, zp, q), dev_r)
        move("r_oth%d" % q, slot(y, zp, q), slot(y, zp, q), slot(y_r, zp, q), dev_l)
        if q < CHUNKS // 2:
            move("o_own%d" % q, slot(y_l, z, q), slot(y_l, z, q), slot(y_o, z, q), dev_r)
            move("o_oth%d" % q, slot(y_o, z, q), slot(y_o, z, q), slot(y_o, zp, q), dev_z)
        else:
            move("o_own%d" % q, slot(y_r, z, q), slot(y_r, z, q), slot(y_o, z, q), dev_l)
            move("o_oth%d" % q, slot(y_r, zp, q), slot(y_r, zp, q), slot(y_o, zp, q), dev_l)

    for n, a, b in (("k", ks, k2), ("q", qs, q2), ("v", vs, v2)):
        to, from_a, from_b, from_c = block(x), block(x_a), block(x_b), block(x_c)
        move(n + "A", a.at[0, :, pair_of(x_a)], b.at[to], b.at[from_a], dev_a)
        move(n + "B", a.at[0, :, slab_of(x_b)], b.at[(*to, in_pair_b)], b.at[(*from_b, in_pair)], dev_b)
        move(n + "C", b.at[(*from_a, in_pair_b)], b.at[(*from_a, in_pair_b)], b.at[(*from_c, in_pair)], dev_b)
    move("cA", cx.at[0], ctx.at[x], ctx.at[x_a], dev_a)
    move("cB", cx.at[0], ctx.at[x], ctx.at[x_b], dev_b)
    lo, hi = pl.ds(0, LOW), pl.ds(LOW, ROWS - LOW)
    move("cC0", ctx.at[x_a, lo], ctx.at[x_a, lo], ctx.at[x_c, lo], dev_b)
    move("cC1", ctx.at[x_b, hi], ctx.at[x_b, hi], ctx.at[x_c, hi], dev_a)
    for k in range(5):
        src, first, total, second = (r.at[k] if k < 3 else r.at[k - 3] for r in (sums_of(k)))
        move("rsA%d" % k, src.at[pair_of(x_a)], first, first, dev_a)
        move("rsB%d" % k, total, second, second, dev_b)

    def move_out(n, src, dst, start, size, where):
        rows = pl.ds(start, size)
        hop = stage.at[where, pl.ds(0, size)]
        to_a, to_b, to_c = (block(xx, start, size) for xx in (x_a, x_b, x_c))
        move(n + "1", src.at[(*to_c, own_full)], hop, hop, dev_b)
        move(n + "A", src.at[to_a], dst.at[0, rows, own_slab], dst.at[0, rows, slab_of(x_a)], dev_a)
        move(n + "B", src.at[(*to_b, own_full)], dst.at[0, rows, full_of(x)], dst.at[0, rows, full_of(x_b)], dev_b)
        move(n + "C", hop, dst.at[0, rows, full_of(x_b)], dst.at[0, rows, full_of(x_c)], dev_a)

    move_out("dk", dkb, gk, 0, ROWS, 0)
    move_out("dv", dvb, gv, 0, ROWS, 1)
    move_out("dqe", dqb, gq, m128(PIECE * z), PIECE, 2)
    move_out("dql", dqb, gq, m128(PIECE * zp), PIECE, 3)

    def outgoing(tag):
        i, src, there, _, dev = moves[tag]
        return pltpu.make_async_remote_copy(src, there, send.at[i], recv.at[i], device_id=dev, device_id_type=MESH)

    def arriving(tag):
        i, _, _, here, dev = moves[tag]
        return pltpu.make_async_remote_copy(here, here, send.at[i], recv.at[i], device_id=dev, device_id_type=MESH)

    def entry_kept(q):
        return pltpu.make_async_copy(bg.at[0, pl.ds(CHUNK * q, CHUNK)], slot(y, z, q), esem.at[q])

    def emit_send(tag):
        if tag[0] == "E":
            h = int(tag[1])

            @pl.when(has_prev)
            def _():
                outgoing(tag).start()

            @pl.when(jnp.logical_not(has_next))
            def _():
                entry_kept(h).start()
        else:
            outgoing(tag).start()

    def emit_wait(tag):
        if tag[0] == "E":
            h = int(tag[1])

            @pl.when(has_next)
            def _():
                arriving(tag).wait_recv()

            @pl.when(jnp.logical_not(has_next))
            def _():
                entry_kept(h).wait()
        elif tag[0] == "@":
            loads[int(tag[1])].wait()
        else:
            arriving(tag).wait_recv()

    def group_rows(g):
        zz, p = g
        return p, zz, pl.ds(m128(PIECE * zz), PIECE), pl.ds(m128(ROWS + PIECE * zz), PIECE)

    def partial_grad(k):
        if k < 3:
            zz, p = groups[k]
            r = dot(wv[...], inc[zz, pl.ds(pl.multiple_of(ROWS * p, ROWS), ROWS)], 1, 1)
            part[k] = r
            partb[k] = r.astype(BF16)
        else:
            yy = (y_n, y_o)[k - 3]
            r = dot(wv[...], inc[zp, pl.ds(m128(PIECE * yy), PIECE)], 1, 1)
            part1[k - 3] = r
            partb1[k - 3] = r.astype(BF16)

    def pass_on(k):
        if k < 3:
            sumb[k] = (part[k, slab_of(x_b)] + got_a[k, in_pair_b].astype(F32)).astype(BF16)
        else:
            i = k - 3
            sumb1[i] = (part1[i, slab_of(x_b)] + got_a1[i, in_pair_b].astype(F32)).astype(BF16)

    heads = [pl.ds(HEAD * h, HEAD) for h in range(2)]
    pheads = [pl.ds(m128(HEAD * (par + h)), HEAD) for h in range(2)]

    def softmax(k):
        p, zz, rows0, rows1 = group_rows(groups[k])
        row = lax.broadcasted_iota(jnp.int32, (KEYS, ROWS), 0)
        lane = lax.broadcasted_iota(jnp.int32, (KEYS, ROWS), 1)
        ahead = jnp.where(lane < PIECE, lane, lane + PIECE) - row
        if k == 0:
            for j in range(2):
                for h in range(2):
                    kt[j, heads[h]] = k2[j, :, pheads[h]].T
        for h in range(2):
            qg[k, 0:PIECE, heads[h]] = q2[p, rows0, pheads[h]]
            qg[k, PIECE:ROWS, heads[h]] = q2[p, rows1, pheads[h]]

        def scores(j, tops):
            result = []
            ok = ahead >= KEYS * (j - p) - PIECE * zz
            for h in range(2):
                sc = dot(k2[j, :, pheads[h]], qg[k, :, heads[h]], 1, 1)
                sc = jnp.where(ok, sc, -jnp.inf)
                pt[h, k, j] = sc
                result.append(jnp.maximum(tops[h], jnp.max(sc, axis=0, keepdims=True)))
            return tuple(result)

        low = jnp.full((1, ROWS), -jnp.inf, F32)
        tops = lax.fori_loop(0, p + 1, scores, (low, low))

        def weights(j, sums):
            result = []
            for h in range(2):
                e = jnp.exp2((pt[h, k, j] - tops[h]) * EXP_SCALE)
                pt[h, k, j] = e
                result.append(sums[h] + jnp.sum(e, axis=0, keepdims=True))
            return tuple(result)

        none = jnp.zeros((1, ROWS), F32)
        sums = lax.fori_loop(0, p + 1, weights, (none, none))
        for h in range(2):
            linv[k, h : h + 1] = 1.0 / sums[h]

    def turn(k):
        p, _, rows, _ = group_rows(groups[k])
        ctxt[k // 2, :, pl.ds(m128(ROWS * p), PIECE)] = ctx[2 * p, rows].T
        ctxt[k // 2, :, pl.ds(m128(ROWS * p + PIECE), PIECE)] = ctx[2 * p + 1, rows].T

    def weight_grad(i, half):
        zz = (z, zp)[i]

        @pl.loop(0, FEAT // TILE // 2)
        def _(n):
            cols = pl.ds(pl.multiple_of(half * (FEAT // 2) + n * TILE, TILE), TILE)
            r = dot(ctxt[i], inc[zz, :, cols], 1, 0)
            if i == 0:
                acc[:, cols] = r
            else:
                gw[0, :, cols] = (r + acc[:, cols]).astype(BF16)

    def attend(k):
        p, _, rows0, rows1 = group_rows(groups[k])
        if k == 0:
            dka[...] = jnp.zeros_like(dka)
            dva[...] = jnp.zeros_like(dva)
        if k < 3:
            dout[...] = (part[k, own_slab] + got_a[k, in_pair].astype(F32) + got_b[k].astype(F32)).astype(BF16)
        else:
            for i, yy in enumerate((y_n, y_o)):
                r = part1[i, own_slab] + got_a1[i, in_pair].astype(F32) + got_b1[i].astype(F32)
                dout[:, pl.ds(m128(PIECE * lax.rem(yy, 2)), PIECE)] = r.astype(BF16)
        tokens = pl.ds(pl.multiple_of(ROWS * p, ROWS), ROWS)
        prod = dout[...].astype(F32) * ctxt[k // 2, own_slab, tokens].astype(F32)
        deltas = [jnp.sum(prod[HEAD * h : HEAD * (h + 1)], axis=0, keepdims=True) for h in range(2)]
        inv = [linv[k, h : h + 1] for h in range(2)]
        dqa[...] = jnp.zeros_like(dqa)

        @pl.loop(0, p + 1)
        def _(j):
            for h in range(2):
                gh = dout[heads[h]]
                w = pt[h, k, j] * inv[h]
                dp = dot(v2[j, :, pheads[h]], gh, 1, 0)
                ds = (w * (dp - deltas[h])).astype(BF16)
                dva[j, :, heads[h]] += dot(w.astype(BF16), gh, 1, 1)
                dka[j, :, heads[h]] += dot(ds, qg[k, :, heads[h]], 1, 0)
                dqa[heads[h]] += dot(kt[j, heads[h]], ds, 1, 0)

        dq = (dqa[...] * SCALE).astype(BF16).T
        dqb[p, rows0] = dq[0:PIECE]
        dqb[p, rows1] = dq[PIECE:ROWS]

    def cast_keys():
        dkb[...] = (dka[...] * SCALE).astype(BF16)

    def cast_values():
        dvb[...] = dva[...].astype(BF16)

    def early_sent():
        for tag in moves:
            if tag[0] == "E":

                @pl.when(has_prev)
                def _():
                    outgoing(tag).wait_send()
            elif tag[:2] not in LAST:
                outgoing(tag).wait_send()

    table = {
        "cA": ([], None, ["cA"]),
        "cB": ([], None, ["cB"]),
        "cfA": (["cA"], None, ["cC0"]),
        "cfB": (["cB"], None, ["cC1"]),
        "dq": ([], None, ["dqe1", "dqeA", "dqeB"]),
        "dqf": (["dqe1"], None, ["dqeC"]),
        "dk": ([], cast_keys, ["dk1", "dkA", "dkB"]),
        "dv": ([], cast_values, ["dv1", "dvA", "dvB"]),
        "dql": ([], None, ["dql1", "dqlA", "dqlB"]),
        "sent": ([], early_sent, []),
        "dkf": (["dk1"], None, ["dkC"]),
        "dvf": (["dv1"], None, ["dvC"]),
        "dqlf": (["dql1"], None, ["dqlC"]),
        "gA": ([], lambda: weight_grad(0, 0), []),
        "gB": ([], lambda: weight_grad(0, 1), []),
        "gC": ([], lambda: weight_grad(1, 0), []),
        "gD": ([], lambda: weight_grad(1, 1), []),
    }
    for n in "kqv":
        table[n] = ([], None, [n + "A", n + "B"])
        table[n + "f"] = ([n + "A"], None, [n + "C"])
    own, near, far, near_z, far_z = [], [], [], [], []
    for q in range(CHUNKS):
        i = str(q)
        first = q < CHUNKS // 2
        table["E" + i] = ([], None, ["E" + i])
        table["r" + i] = (["E" + i], None, ["l_own" + i])
        table["l" + i] = (["E" + i], None, ["r_own" + i])
        table["z" + i] = (["E" + i], None, ["z" + i])
        table["R" + i] = (["z" + i], None, ["l_oth" + i])
        table["L" + i] = (["z" + i], None, ["r_oth" + i])
        table["f" + i] = (["l_own" + i] if first else ["r_own" + i], None, ["o_own" + i])
        table["F" + i] = (["o_own" + i] if first else ["r_oth" + i], None, ["o_oth" + i])
        own += ["E" + i]
        near += ["l_own" + i, "r_own" + i]
        far += ["o_own" + i]
        near_z += ["z" + i, "l_oth" + i, "r_oth" + i]
        far_z += ["o_oth" + i]
    for k, need in enumerate((["@4"] + own + near, far, near_z, near_z, far_z)):
        table["p%d" % k] = (need, lambda k=k: partial_grad(k), ["rsA%d" % k])
        table["s%d" % k] = (["rsA%d" % k], lambda k=k: pass_on(k), ["rsB%d" % k])
    for k in range(4):
        sums = ["rsB%d" % k] if k < 3 else ["rsB3", "rsB4"]
        table["P%d" % k] = (["@0", "@1", "kA", "kB", "kC", "qA", "qB", "qC"], lambda k=k: softmax(k), [])
        table["t%d" % k] = (["@3", "cA", "cB", "cC0", "cC1"], lambda k=k: turn(k), [])
        table["a%d" % k] = (["@2", "vA", "vB", "vC"] + sums, lambda k=k: attend(k), [])

    def perform(order):
        seen = set()
        for name in order:
            waits, work, sends = table[name]
            for tag in waits:
                if tag not in seen:
                    seen.add(tag)
                    emit_wait(tag)
            if work is not None:
                work()
            for tag in sends:
                emit_send(tag)
        for n, (b, g) in enumerate(((dqb, gq), (dkb, gk), (dvb, gv))):
            pltpu.make_async_copy(b.at[block(x)], g.at[0, :, own_slab], osem.at[n]).start()

    for n, order in enumerate((ORDER0, ORDER1)):
        pl.when(core == n)(lambda order=order: perform(order))

    for n in ("dqe", "dk", "dv", "dql"):
        for tail in "ABC":
            emit_wait(n + tail)
    for n, (b, g) in enumerate(((dqb, gq), (dkb, gk), (dvb, gv))):
        pltpu.make_async_copy(b.at[block(x)], g.at[0, :, own_slab], osem.at[n]).wait()
    for tag in moves:
        if tag[:2] in LAST:
            outgoing(tag).wait_send()


N_MOVES = 8 * CHUNKS + 9 + 4 + 10 + 16


def write_out(gw, gq, gk, gv, gw_out, gq_out, gk_out, gv_out, sems):
    copies = []
    for n in range(6):
        rows = pl.ds(n * (WIDTH // 6), WIDTH // 6)
        copies.append(pltpu.make_async_copy(gw.at[0, rows], gw_out.at[0, rows], sems.at[n]))
    for n, (src, dst) in enumerate(((gq, gq_out), (gk, gk_out), (gv, gv_out))):
        copies.append(pltpu.make_async_copy(src, dst, sems.at[6 + n]))
    for copy in copies:
        copy.start()
    for copy in copies:
        copy.wait()


def local(boundary_grad, w_out, context, queries, keys, values):
    any_spec = pl.BlockSpec(memory_space=pl.ANY)
    vmem_spec = pl.BlockSpec(memory_space=pltpu.VMEM)
    shapes = [(1, WIDTH, FEAT), (1, ROWS, WIDTH), (1, ROWS, WIDTH), (1, ROWS, WIDTH)]
    grads = pl.pallas_call(
        kernel,
        out_shape=[pltpu.VMEM(shape, BF16) for shape in shapes],
        in_specs=[any_spec] * 6,
        out_specs=[vmem_spec] * 4,
        scratch_shapes=[
            pltpu.VMEM((2, KEYS, FEAT), BF16),
            pltpu.VMEM((WIDTH, FEAT), BF16),
            pltpu.VMEM((4, ROWS, WIDTH), BF16),
            pltpu.VMEM((2, WIDTH, KEYS), BF16),
            pltpu.VMEM((WIDTH, FEAT), F32),
            pltpu.VMEM((2, KEYS, PAIR), BF16),
            pltpu.VMEM((2, KEYS, PAIR), BF16),
            pltpu.VMEM((2, KEYS, PAIR), BF16),
            pltpu.VMEM((4, ROWS, SLAB), BF16),
            pltpu.VMEM((3, WIDTH, ROWS), F32),
            pltpu.VMEM((3, WIDTH, ROWS), BF16),
            pltpu.VMEM((3, PAIR, ROWS), BF16),
            pltpu.VMEM((3, SLAB, ROWS), BF16),
            pltpu.VMEM((3, SLAB, ROWS), BF16),
            pltpu.VMEM((2, WIDTH, PIECE), F32),
            pltpu.VMEM((2, WIDTH, PIECE), BF16),
            pltpu.VMEM((2, PAIR, PIECE), BF16),
            pltpu.VMEM((2, SLAB, PIECE), BF16),
            pltpu.VMEM((2, SLAB, PIECE), BF16),
            pltpu.VMEM((2, SLAB, KEYS), BF16),
            pltpu.VMEM((2, 4, 2, KEYS, ROWS), F32),
            pltpu.VMEM((4, 8, ROWS), F32),
            pltpu.VMEM((ROWS, SLAB), BF16),
            pltpu.VMEM((ROWS, SLAB), F32),
            pltpu.VMEM((2, KEYS, SLAB), F32),
            pltpu.VMEM((2, KEYS, SLAB), F32),
            pltpu.VMEM((2, KEYS, SLAB), BF16),
            pltpu.VMEM((2, KEYS, SLAB), BF16),
            pltpu.VMEM((2, KEYS, SLAB), BF16),
            pltpu.VMEM((4, ROWS, HEAD), BF16),
            pltpu.SemaphoreType.DMA((N_MOVES,)),
            pltpu.SemaphoreType.DMA((N_MOVES,)),
            pltpu.SemaphoreType.DMA((5,)),
            pltpu.SemaphoreType.DMA((CHUNKS,)),
            pltpu.SemaphoreType.DMA((3,)),
        ],
        compiler_params=pltpu.CompilerParams(
            collective_id=0, has_side_effects=True, vmem_limit_bytes=54 * 1024 * 1024
        ),
    )(boundary_grad, w_out, context, queries, keys, values)
    return pl.pallas_call(
        write_out,
        out_shape=[jax.ShapeDtypeStruct(shape, BF16) for shape in shapes],
        in_specs=[any_spec] * 4,
        out_specs=[any_spec] * 4,
        scratch_shapes=[pltpu.SemaphoreType.DMA((9,))],
        compiler_params=pltpu.CompilerParams(vmem_limit_bytes=1024 * 1024),
    )(*grads)


def solution(mesh):
    in_specs = (
        P("section", "col", "row"),
        P("section", "col", "row"),
        P("section", "row", "col"),
        P("section", "row", "col"),
        P("section", "row", "col"),
        P("section", "row", "col"),
    )
    out_specs = (
        P("section", "col", "row"),
        P("section", "row", "col"),
        P("section", "row", "col"),
        P("section", "row", "col"),
    )
    return jax.shard_map(local, mesh=mesh, in_specs=in_specs, out_specs=out_specs, check_vma=False)
```

```python
import jax
import jax.numpy as jnp
from jax import lax
from jax.experimental import pallas as pl
from jax.experimental.pallas import tpu as pltpu
from jax.sharding import PartitionSpec as P

HEAD = 128
SCALE = HEAD ** (-0.5)
EXP_SCALE = SCALE * 1.4426950408889634
MESH = pl.DeviceIdType.MESH
BF16 = jnp.bfloat16
F32 = jnp.float32

ROWS = 256
PIECE = 128
CHUNKS = 2
CHUNK = PIECE // CHUNKS
LOW = 192
KEYS = 512
FEAT = 3072
WIDTH = 768
PAIR = 384
SLAB = 256
TILE = 512

ORDER0 = [
    "cB", "E0", "cA", "k", "l1", "r0", "r1", "l0", "E1", "f1", "f0", "v", "p0", "z1", "cfB", "cfA", "z0", "t0",
    "t1", "q", "F0", "kf", "t2", "R1", "L1", "p1", "gA", "L0", "qf", "s0", "gB", "vf", "R0", "s1", "F1", "P0", "P1",
    "P2", "p2", "t3", "P3", "p3", "p4", "a0", "s2", "s3", "s4", "a1", "a2", "dq", "a3", "dqf", "dk", "dv", "dql",
    "sent", "gC", "dkf", "dqlf", "dvf", "gD",
]
ORDER1 = [
    "E1", "q", "cB", "k", "v", "E0", "kf", "cA", "r0", "l0", "cfB", "qf", "l1", "r1", "P0", "f0", "z1", "P1", "cfA",
    "z0", "f1", "P2", "p0", "P3", "t0", "t1", "s0", "t2", "F0", "p1", "L1", "vf", "R0", "gA", "L0", "R1", "a0",
    "s1", "gB", "F1", "a1", "dq", "p2", "p3", "p4", "s2", "t3", "s3", "s4", "dqf", "a2", "a3", "dql", "dv", "dk",
    "gC", "sent", "dvf", "dqlf", "gD", "dkf",
]
LAST = ("dk", "dv", "dq")


def dot(a, b, ca, cb):
    return lax.dot_general(a, b, (((ca,), (cb,)), ((), ())), preferred_element_type=F32)


def kernel(
    bg, wo, cx, qs, ks, vs,
    gw, gq, gk, gv,
    inc, wv, ctx, ctxt, acc, q2, k2, v2, qg, part, partb, got_a, got_b, sumb, part1, partb1, got_a1, got_b1, sumb1, kt, pt, linv, dout,
    dqa, dka, dva, dqb, dkb, dvb, stage,
    send, recv, lsem, esem, osem,
):
    s = lax.axis_index("section")
    x = lax.axis_index("row")
    c = lax.axis_index("col")
    y = c // 2
    z = c - 2 * y
    core = s - 2 * (s // 2)
    y_r = lax.rem(y + 1 + 2 * core, 4)
    y_l = lax.rem(y + 3 + 2 * core, 4)
    y_o = lax.rem(y + 2, 4)
    y_n = y_o + 1 - 2 * lax.rem(y_o, 2)
    zp = 1 - z
    pair = x // 2
    par = x - 2 * pair
    par_b = 1 - par
    x_a = 3 - x
    x_b = 2 * pair + par_b
    x_c = lax.rem(x + 2, 4)
    dev_r = (s, x, 2 * y_r + z)
    dev_l = (s, x, 2 * y_l + z)
    dev_z = (s, x, 2 * y + zp)
    dev_a = (s, x_a, c)
    dev_b = (s, x_b, c)
    has_prev = s > 0
    has_next = s < 7
    dev_prev = (jnp.maximum(s - 1, 0), x, c)
    dev_next = (jnp.minimum(s + 1, 7), x, c)

    def m128(v):
        return pl.multiple_of(v, 128)

    def slab_of(xx):
        p = xx // 2
        return pl.ds(m128(PAIR * p + HEAD * (xx - 2 * p)), SLAB)

    def full_of(xx):
        p = xx // 2
        return pl.ds(m128(PAIR * p + 2 * HEAD * (xx - 2 * p)), HEAD)

    def pair_of(xx):
        return pl.ds(m128(PAIR * (xx // 2)), PAIR)

    own_slab = slab_of(x)
    in_pair = pl.ds(m128(HEAD * par), SLAB)
    in_pair_b = pl.ds(m128(HEAD * par_b), SLAB)
    own_full = pl.ds(m128(HEAD * par), HEAD)

    def block(xx, start=0, size=ROWS):
        half = xx // 2
        return half, pl.ds(m128(ROWS * (xx - 2 * half) + start), size)

    loads = []
    for src, dst in (
        (ks.at[0, :, own_slab], k2.at[(*block(x), in_pair)]),
        (qs.at[0, :, own_slab], q2.at[(*block(x), in_pair)]),
        (vs.at[0, :, own_slab], v2.at[(*block(x), in_pair)]),
        (cx.at[0], ctx.at[x]),
        (wo.at[0], wv),
    ):
        loads.append(pltpu.make_async_copy(src, dst, lsem.at[len(loads)]))
    for copy in loads:
        copy.start()

    barrier = pltpu.get_barrier_semaphore()
    for dev in (dev_r, dev_l, dev_z, dev_a, dev_b):
        pl.semaphore_signal(barrier, inc=1, device_id=dev, device_id_type=MESH)

    @pl.when(has_next)
    def _():
        pl.semaphore_signal(barrier, inc=1, device_id=dev_next, device_id_type=MESH)

    dka[...] = jnp.zeros_like(dka)
    dva[...] = jnp.zeros_like(dva)
    pl.semaphore_wait(barrier, 5 + has_prev.astype(jnp.int32))

    def slot(yy, zz, q):
        return inc.at[zz, pl.ds(pl.multiple_of(PIECE * yy + CHUNK * q, CHUNK), CHUNK)]

    groups = [(z, y // 2), (z, 1 - y // 2), (zp, y // 2), (zp, 1 - y // 2)]

    moves = {}

    def move(tag, src, there, here, dev):
        moves[tag] = (len(moves), src, there, here, dev)

    def sums_of(k):
        return (partb, got_a, sumb, got_b) if k < 3 else (partb1, got_a1, sumb1, got_b1)

    for q in range(CHUNKS):
        move("E%d" % q, bg.at[0, pl.ds(CHUNK * q, CHUNK)], slot(y, z, q), slot(y, z, q), dev_prev)
        move("z%d" % q, slot(y, z, q), slot(y, z, q), slot(y, zp, q), dev_z)
        move("l_own%d" % q, slot(y, z, q), slot(y, z, q), slot(y_l, z, q), dev_r)
        move("r_own%d" % q, slot(y, z, q), slot(y, z, q), slot(y_r, z, q), dev_l)
        move("l_oth%d" % q, slot(y, zp, q), slot(y, zp, q), slot(y_l, zp, q), dev_r)
        move("r_oth%d" % q, slot(y, zp, q), slot(y, zp, q), slot(y_r, zp, q), dev_l)
        if q < CHUNKS // 2:
            move("o_own%d" % q, slot(y_l, z, q), slot(y_l, z, q), slot(y_o, z, q), dev_r)
            move("o_oth%d" % q, slot(y_o, z, q), slot(y_o, z, q), slot(y_o, zp, q), dev_z)
        else:
            move("o_own%d" % q, slot(y_r, z, q), slot(y_r, z, q), slot(y_o, z, q), dev_l)
            move("o_oth%d" % q, slot(y_r, zp, q), slot(y_r, zp, q), slot(y_o, zp, q), dev_l)

    for n, a, b in (("k", ks, k2), ("q", qs, q2), ("v", vs, v2)):
        to, from_a, from_b, from_c = block(x), block(x_a), block(x_b), block(x_c)
        move(n + "A", a.at[0, :, pair_of(x_a)], b.at[to], b.at[from_a], dev_a)
        move(n + "B", a.at[0, :, slab_of(x_b)], b.at[(*to, in_pair_b)], b.at[(*from_b, in_pair)], dev_b)
        move(n + "C", b.at[(*from_a, in_pair_b)], b.at[(*from_a, in_pair_b)], b.at[(*from_c, in_pair)], dev_b)
    move("cA", cx.at[0], ctx.at[x], ctx.at[x_a], dev_a)
    move("cB", cx.at[0], ctx.at[x], ctx.at[x_b], dev_b)
    lo, hi = pl.ds(0, LOW), pl.ds(LOW, ROWS - LOW)
    move("cC0", ctx.at[x_a, lo], ctx.at[x_a, lo], ctx.at[x_c, lo], dev_b)
    move("cC1", ctx.at[x_b, hi], ctx.at[x_b, hi], ctx.at[x_c, hi], dev_a)
    for k in range(5):
        src, first, total, second = (r.at[k] if k < 3 else r.at[k - 3] for r in (sums_of(k)))
        move("rsA%d" % k, src.at[pair_of(x_a)], first, first, dev_a)
        move("rsB%d" % k, total, second, second, dev_b)

    def move_out(n, src, dst, start, size, where):
        rows = pl.ds(start, size)
        hop = stage.at[where, pl.ds(0, size)]
        to_a, to_b, to_c = (block(xx, start, size) for xx in (x_a, x_b, x_c))
        move(n + "1", src.at[(*to_c, own_full)], hop, hop, dev_b)
        move(n + "A", src.at[to_a], dst.at[0, rows, own_slab], dst.at[0, rows, slab_of(x_a)], dev_a)
        move(n + "B", src.at[(*to_b, own_full)], dst.at[0, rows, full_of(x)], dst.at[0, rows, full_of(x_b)], dev_b)
        move(n + "C", hop, dst.at[0, rows, full_of(x_b)], dst.at[0, rows, full_of(x_c)], dev_a)

    move_out("dk", dkb, gk, 0, ROWS, 0)
    move_out("dv", dvb, gv, 0, ROWS, 1)
    move_out("dqe", dqb, gq, m128(PIECE * z), PIECE, 2)
    move_out("dql", dqb, gq, m128(PIECE * zp), PIECE, 3)

    def outgoing(tag):
        i, src, there, _, dev = moves[tag]
        return pltpu.make_async_remote_copy(src, there, send.at[i], recv.at[i], device_id=dev, device_id_type=MESH)

    def arriving(tag):
        i, _, _, here, dev = moves[tag]
        return pltpu.make_async_remote_copy(here, here, send.at[i], recv.at[i], device_id=dev, device_id_type=MESH)

    def entry_kept(q):
        return pltpu.make_async_copy(bg.at[0, pl.ds(CHUNK * q, CHUNK)], slot(y, z, q), esem.at[q])

    def emit_send(tag):
        if tag[0] == "E":
            h = int(tag[1])

            @pl.when(has_prev)
            def _():
                outgoing(tag).start()

            @pl.when(jnp.logical_not(has_next))
            def _():
                entry_kept(h).start()
        else:
            outgoing(tag).start()

    def emit_wait(tag):
        if tag[0] == "E":
            h = int(tag[1])

            @pl.when(has_next)
            def _():
                arriving(tag).wait_recv()

            @pl.when(jnp.logical_not(has_next))
            def _():
                entry_kept(h).wait()
        elif tag[0] == "@":
            loads[int(tag[1])].wait()
        else:
            arriving(tag).wait_recv()

    def group_rows(g):
        zz, p = g
        return p, zz, pl.ds(m128(PIECE * zz), PIECE), pl.ds(m128(ROWS + PIECE * zz), PIECE)

    def partial_grad(k):
        if k < 3:
            zz, p = groups[k]
            r = dot(wv[...], inc[zz, pl.ds(pl.multiple_of(ROWS * p, ROWS), ROWS)], 1, 1)
            part[k] = r
            partb[k] = r.astype(BF16)
        else:
            yy = (y_n, y_o)[k - 3]
            r = dot(wv[...], inc[zp, pl.ds(m128(PIECE * yy), PIECE)], 1, 1)
            part1[k - 3] = r
            partb1[k - 3] = r.astype(BF16)

    def pass_on(k):
        if k < 3:
            sumb[k] = (part[k, slab_of(x_b)] + got_a[k, in_pair_b].astype(F32)).astype(BF16)
        else:
            i = k - 3
            sumb1[i] = (part1[i, slab_of(x_b)] + got_a1[i, in_pair_b].astype(F32)).astype(BF16)

    heads = [pl.ds(HEAD * h, HEAD) for h in range(2)]
    pheads = [pl.ds(m128(HEAD * (par + h)), HEAD) for h in range(2)]

    def softmax(k):
        p, zz, rows0, rows1 = group_rows(groups[k])
        row = lax.broadcasted_iota(jnp.int32, (KEYS, ROWS), 0)
        lane = lax.broadcasted_iota(jnp.int32, (KEYS, ROWS), 1)
        ahead = jnp.where(lane < PIECE, lane, lane + PIECE) - row
        if k == 0:
            for j in range(2):
                for h in range(2):
                    kt[j, heads[h]] = k2[j, :, pheads[h]].T
        for h in range(2):
            qg[k, 0:PIECE, heads[h]] = q2[p, rows0, pheads[h]]
            qg[k, PIECE:ROWS, heads[h]] = q2[p, rows1, pheads[h]]

        def scores(j, tops):
            result = []
            ok = ahead >= KEYS * (j - p) - PIECE * zz
            for h in range(2):
                sc = dot(k2[j, :, pheads[h]], qg[k, :, heads[h]], 1, 1)
                sc = jnp.where(ok, sc, -jnp.inf)
                pt[h, k, j] = sc
                result.append(jnp.maximum(tops[h], jnp.max(sc, axis=0, keepdims=True)))
            return tuple(result)

        low = jnp.full((1, ROWS), -jnp.inf, F32)
        tops = lax.fori_loop(0, p + 1, scores, (low, low))

        def weights(j, sums):
            result = []
            for h in range(2):
                e = jnp.exp2((pt[h, k, j] - tops[h]) * EXP_SCALE)
                pt[h, k, j] = e
                result.append(sums[h] + jnp.sum(e, axis=0, keepdims=True))
            return tuple(result)

        none = jnp.zeros((1, ROWS), F32)
        sums = lax.fori_loop(0, p + 1, weights, (none, none))
        for h in range(2):
            linv[k, h : h + 1] = 1.0 / sums[h]

    def turn(k):
        p, _, rows, _ = group_rows(groups[k])
        ctxt[k // 2, :, pl.ds(m128(ROWS * p), PIECE)] = ctx[2 * p, rows].T
        ctxt[k // 2, :, pl.ds(m128(ROWS * p + PIECE), PIECE)] = ctx[2 * p + 1, rows].T

    def weight_grad(i, half):
        zz = (z, zp)[i]

        @pl.loop(0, FEAT // TILE // 2)
        def _(n):
            cols = pl.ds(pl.multiple_of(half * (FEAT // 2) + n * TILE, TILE), TILE)
            r = dot(ctxt[i], inc[zz, :, cols], 1, 0)
            if i == 0:
                acc[:, cols] = r
            else:
                gw[0, :, cols] = (r + acc[:, cols]).astype(BF16)

    def attend(k):
        p, _, rows0, rows1 = group_rows(groups[k])
        if k < 3:
            dout[...] = (part[k, own_slab] + got_a[k, in_pair].astype(F32) + got_b[k].astype(F32)).astype(BF16)
        else:
            for i, yy in enumerate((y_n, y_o)):
                r = part1[i, own_slab] + got_a1[i, in_pair].astype(F32) + got_b1[i].astype(F32)
                dout[:, pl.ds(m128(PIECE * lax.rem(yy, 2)), PIECE)] = r.astype(BF16)
        tokens = pl.ds(pl.multiple_of(ROWS * p, ROWS), ROWS)
        prod = dout[...].astype(F32) * ctxt[k // 2, own_slab, tokens].astype(F32)
        deltas = [jnp.sum(prod[HEAD * h : HEAD * (h + 1)], axis=0, keepdims=True) for h in range(2)]
        inv = [linv[k, h : h + 1] for h in range(2)]
        dqa[...] = jnp.zeros_like(dqa)

        @pl.loop(0, p + 1)
        def _(j):
            for h in range(2):
                gh = dout[heads[h]]
                w = pt[h, k, j] * inv[h]
                dp = dot(v2[j, :, pheads[h]], gh, 1, 0)
                ds = (w * (dp - deltas[h])).astype(BF16)
                dva[j, :, heads[h]] += dot(w.astype(BF16), gh, 1, 1)
                dka[j, :, heads[h]] += dot(ds, qg[k, :, heads[h]], 1, 0)
                dqa[heads[h]] += dot(kt[j, heads[h]], ds, 1, 0)

        dq = (dqa[...] * SCALE).astype(BF16).T
        dqb[p, rows0] = dq[0:PIECE]
        dqb[p, rows1] = dq[PIECE:ROWS]

    def cast_keys():
        dkb[...] = (dka[...] * SCALE).astype(BF16)

    def cast_values():
        dvb[...] = dva[...].astype(BF16)

    def early_sent():
        for tag in moves:
            if tag[0] == "E":

                @pl.when(has_prev)
                def _():
                    outgoing(tag).wait_send()
            elif tag[:2] not in LAST:
                outgoing(tag).wait_send()

    table = {
        "cA": ([], None, ["cA"]),
        "cB": ([], None, ["cB"]),
        "cfA": (["cA"], None, ["cC0"]),
        "cfB": (["cB"], None, ["cC1"]),
        "dq": ([], None, ["dqe1", "dqeA", "dqeB"]),
        "dqf": (["dqe1"], None, ["dqeC"]),
        "dk": ([], cast_keys, ["dk1", "dkA", "dkB"]),
        "dv": ([], cast_values, ["dv1", "dvA", "dvB"]),
        "dql": ([], None, ["dql1", "dqlA", "dqlB"]),
        "sent": ([], early_sent, []),
        "dkf": (["dk1"], None, ["dkC"]),
        "dvf": (["dv1"], None, ["dvC"]),
        "dqlf": (["dql1"], None, ["dqlC"]),
        "gA": ([], lambda: weight_grad(0, 0), []),
        "gB": ([], lambda: weight_grad(0, 1), []),
        "gC": ([], lambda: weight_grad(1, 0), []),
        "gD": ([], lambda: weight_grad(1, 1), []),
    }
    for n in "kqv":
        table[n] = ([], None, [n + "A", n + "B"])
        table[n + "f"] = ([n + "A"], None, [n + "C"])
    own, near, far, near_z, far_z = [], [], [], [], []
    for q in range(CHUNKS):
        i = str(q)
        first = q < CHUNKS // 2
        table["E" + i] = ([], None, ["E" + i])
        table["r" + i] = (["E" + i], None, ["l_own" + i])
        table["l" + i] = (["E" + i], None, ["r_own" + i])
        table["z" + i] = (["E" + i], None, ["z" + i])
        table["R" + i] = (["z" + i], None, ["l_oth" + i])
        table["L" + i] = (["z" + i], None, ["r_oth" + i])
        table["f" + i] = (["l_own" + i] if first else ["r_own" + i], None, ["o_own" + i])
        table["F" + i] = (["o_own" + i] if first else ["r_oth" + i], None, ["o_oth" + i])
        own += ["E" + i]
        near += ["l_own" + i, "r_own" + i]
        far += ["o_own" + i]
        near_z += ["z" + i, "l_oth" + i, "r_oth" + i]
        far_z += ["o_oth" + i]
    for k, need in enumerate((["@4"] + own + near, far, near_z, near_z, far_z)):
        table["p%d" % k] = (need, lambda k=k: partial_grad(k), ["rsA%d" % k])
        table["s%d" % k] = (["rsA%d" % k], lambda k=k: pass_on(k), ["rsB%d" % k])
    for k in range(4):
        sums = ["rsB%d" % k] if k < 3 else ["rsB3", "rsB4"]
        table["P%d" % k] = (["@0", "@1", "kA", "kB", "kC", "qA", "qB", "qC"], lambda k=k: softmax(k), [])
        table["t%d" % k] = (["@3", "cA", "cB", "cC0", "cC1"], lambda k=k: turn(k), [])
        table["a%d" % k] = (["@2", "vA", "vB", "vC"] + sums, lambda k=k: attend(k), [])

    def perform(order):
        seen = set()
        for name in order:
            waits, work, sends = table[name]
            for tag in waits:
                if tag not in seen:
                    seen.add(tag)
                    emit_wait(tag)
            if work is not None:
                work()
            for tag in sends:
                emit_send(tag)
        for n, (b, g) in enumerate(((dqb, gq), (dkb, gk), (dvb, gv))):
            pltpu.make_async_copy(b.at[block(x)], g.at[0, :, own_slab], osem.at[n]).start()

    for n, order in enumerate((ORDER0, ORDER1)):
        pl.when(core == n)(lambda order=order: perform(order))

    for n in ("dqe", "dk", "dv", "dql"):
        for tail in "ABC":
            emit_wait(n + tail)
    for n, (b, g) in enumerate(((dqb, gq), (dkb, gk), (dvb, gv))):
        pltpu.make_async_copy(b.at[block(x)], g.at[0, :, own_slab], osem.at[n]).wait()
    for tag in moves:
        if tag[:2] in LAST:
            outgoing(tag).wait_send()


N_MOVES = 8 * CHUNKS + 9 + 4 + 10 + 16


def write_out(gw, gq, gk, gv, gw_out, gq_out, gk_out, gv_out, sems):
    copies = []
    for n in range(6):
        rows = pl.ds(n * (WIDTH // 6), WIDTH // 6)
        copies.append(pltpu.make_async_copy(gw.at[0, rows], gw_out.at[0, rows], sems.at[n]))
    for n, (src, dst) in enumerate(((gq, gq_out), (gk, gk_out), (gv, gv_out))):
        copies.append(pltpu.make_async_copy(src, dst, sems.at[6 + n]))
    for copy in copies:
        copy.start()
    for copy in copies:
        copy.wait()


def local(boundary_grad, w_out, context, queries, keys, values):
    any_spec = pl.BlockSpec(memory_space=pl.ANY)
    vmem_spec = pl.BlockSpec(memory_space=pltpu.VMEM)
    shapes = [(1, WIDTH, FEAT), (1, ROWS, WIDTH), (1, ROWS, WIDTH), (1, ROWS, WIDTH)]
    grads = pl.pallas_call(
        kernel,
        out_shape=[pltpu.VMEM(shape, BF16) for shape in shapes],
        in_specs=[any_spec] * 6,
        out_specs=[vmem_spec] * 4,
        scratch_shapes=[
            pltpu.VMEM((2, KEYS, FEAT), BF16),
            pltpu.VMEM((WIDTH, FEAT), BF16),
            pltpu.VMEM((4, ROWS, WIDTH), BF16),
            pltpu.VMEM((2, WIDTH, KEYS), BF16),
            pltpu.VMEM((WIDTH, FEAT), F32),
            pltpu.VMEM((2, KEYS, PAIR), BF16),
            pltpu.VMEM((2, KEYS, PAIR), BF16),
            pltpu.VMEM((2, KEYS, PAIR), BF16),
            pltpu.VMEM((4, ROWS, SLAB), BF16),
            pltpu.VMEM((3, WIDTH, ROWS), F32),
            pltpu.VMEM((3, WIDTH, ROWS), BF16),
            pltpu.VMEM((3, PAIR, ROWS), BF16),
            pltpu.VMEM((3, SLAB, ROWS), BF16),
            pltpu.VMEM((3, SLAB, ROWS), BF16),
            pltpu.VMEM((2, WIDTH, PIECE), F32),
            pltpu.VMEM((2, WIDTH, PIECE), BF16),
            pltpu.VMEM((2, PAIR, PIECE), BF16),
            pltpu.VMEM((2, SLAB, PIECE), BF16),
            pltpu.VMEM((2, SLAB, PIECE), BF16),
            pltpu.VMEM((2, SLAB, KEYS), BF16),
            pltpu.VMEM((2, 4, 2, KEYS, ROWS), F32),
            pltpu.VMEM((4, 8, ROWS), F32),
            pltpu.VMEM((ROWS, SLAB), BF16),
            pltpu.VMEM((ROWS, SLAB), F32),
            pltpu.VMEM((2, KEYS, SLAB), F32),
            pltpu.VMEM((2, KEYS, SLAB), F32),
            pltpu.VMEM((2, KEYS, SLAB), BF16),
            pltpu.VMEM((2, KEYS, SLAB), BF16),
            pltpu.VMEM((2, KEYS, SLAB), BF16),
            pltpu.VMEM((4, ROWS, HEAD), BF16),
            pltpu.SemaphoreType.DMA((N_MOVES,)),
            pltpu.SemaphoreType.DMA((N_MOVES,)),
            pltpu.SemaphoreType.DMA((5,)),
            pltpu.SemaphoreType.DMA((CHUNKS,)),
            pltpu.SemaphoreType.DMA((3,)),
        ],
        compiler_params=pltpu.CompilerParams(
            collective_id=0, has_side_effects=True, vmem_limit_bytes=54 * 1024 * 1024
        ),
    )(boundary_grad, w_out, context, queries, keys, values)
    return pl.pallas_call(
        write_out,
        out_shape=[jax.ShapeDtypeStruct(shape, BF16) for shape in shapes],
        in_specs=[any_spec] * 4,
        out_specs=[any_spec] * 4,
        scratch_shapes=[pltpu.SemaphoreType.DMA((9,))],
        compiler_params=pltpu.CompilerParams(vmem_limit_bytes=1024 * 1024),
    )(*grads)


def solution(mesh):
    in_specs = (
        P("section", "col", "row"),
        P("section", "col", "row"),
        P("section", "row", "col"),
        P("section", "row", "col"),
        P("section", "row", "col"),
        P("section", "row", "col"),
    )
    out_specs = (
        P("section", "col", "row"),
        P("section", "row", "col"),
        P("section", "row", "col"),
        P("section", "row", "col"),
    )
    return jax.shard_map(local, mesh=mesh, in_specs=in_specs, out_specs=out_specs, check_vma=False)
```

```python
import jax
import jax.numpy as jnp
from jax import lax
from jax.experimental import pallas as pl
from jax.experimental.pallas import tpu as pltpu
from jax.sharding import PartitionSpec as P

HEAD = 128
SCALE = HEAD ** (-0.5)
EXP_SCALE = SCALE * 1.4426950408889634
MESH = pl.DeviceIdType.MESH
BF16 = jnp.bfloat16
F32 = jnp.float32

ROWS = 256
PIECE = 128
CHUNKS = 2
CHUNK = PIECE // CHUNKS
LOW = 192
KEYS = 512
FEAT = 3072
WIDTH = 768
PAIR = 384
SLAB = 256
TILE = 512

ORDER0 = [
    "cB", "E0", "cA", "k", "l1", "r0", "r1", "l0", "E1", "f1", "f0", "v", "p0", "z1", "cfB", "cfA", "z0", "t0",
    "t1", "q", "F0", "kf", "t2", "R1", "L1", "p1", "gA", "L0", "qf", "s0", "gB", "vf", "R0", "s1", "F1", "P0", "P1",
    "P2", "p2", "t3", "P3", "p3", "p4", "a0", "s2", "s3", "s4", "a1", "a2", "dq", "a3", "dk", "dv", "dql",
    "sent", "gC", "gD",
]
ORDER1 = [
    "E1", "q", "cB", "k", "v", "E0", "kf", "cA", "r0", "l0", "cfB", "qf", "l1", "r1", "P0", "f0", "z1", "P1", "cfA",
    "z0", "f1", "P2", "p0", "P3", "t0", "t1", "s0", "t2", "F0", "p1", "L1", "vf", "R0", "gA", "L0", "R1", "a0",
    "s1", "gB", "F1", "a1", "dq", "p2", "p3", "p4", "s2", "t3", "s3", "s4", "a2", "a3", "dql", "dv", "dk",
    "gC", "sent", "gD",
]
LAST = ("dk", "dv", "dq")


def dot(a, b, ca, cb):
    return lax.dot_general(a, b, (((ca,), (cb,)), ((), ())), preferred_element_type=F32)


def kernel(
    bg, wo, cx, qs, ks, vs,
    gw, gq, gk, gv,
    inc, wv, ctx, ctxt, acc, q2, k2, v2, qg, part, partb, got_a, got_b, sumb, part1, partb1, got_a1, got_b1, sumb1, kt, pt, linv, dout,
    dqa, dka, dva, dqb, dkb, dvb,
    send, recv, lsem, esem, osem,
):
    s = lax.axis_index("section")
    x = lax.axis_index("row")
    c = lax.axis_index("col")
    y = c // 2
    z = c - 2 * y
    core = s - 2 * (s // 2)
    y_r = lax.rem(y + 1 + 2 * core, 4)
    y_l = lax.rem(y + 3 + 2 * core, 4)
    y_o = lax.rem(y + 2, 4)
    y_n = y_o + 1 - 2 * lax.rem(y_o, 2)
    zp = 1 - z
    pair = x // 2
    par = x - 2 * pair
    par_b = 1 - par
    x_a = 3 - x
    x_b = 2 * pair + par_b
    x_c = lax.rem(x + 2, 4)
    dev_r = (s, x, 2 * y_r + z)
    dev_l = (s, x, 2 * y_l + z)
    dev_z = (s, x, 2 * y + zp)
    dev_a = (s, x_a, c)
    dev_b = (s, x_b, c)
    dev_c = (s, x_c, c)
    has_prev = s > 0
    has_next = s < 7
    dev_prev = (jnp.maximum(s - 1, 0), x, c)
    dev_next = (jnp.minimum(s + 1, 7), x, c)

    def m128(v):
        return pl.multiple_of(v, 128)

    def slab_of(xx):
        p = xx // 2
        return pl.ds(m128(PAIR * p + HEAD * (xx - 2 * p)), SLAB)

    def full_of(xx):
        p = xx // 2
        return pl.ds(m128(PAIR * p + 2 * HEAD * (xx - 2 * p)), HEAD)

    def pair_of(xx):
        return pl.ds(m128(PAIR * (xx // 2)), PAIR)

    own_slab = slab_of(x)
    in_pair = pl.ds(m128(HEAD * par), SLAB)
    in_pair_b = pl.ds(m128(HEAD * par_b), SLAB)
    own_full = pl.ds(m128(HEAD * par), HEAD)

    def block(xx, start=0, size=ROWS):
        half = xx // 2
        return half, pl.ds(m128(ROWS * (xx - 2 * half) + start), size)

    loads = []
    for src, dst in (
        (ks.at[0, :, own_slab], k2.at[(*block(x), in_pair)]),
        (qs.at[0, :, own_slab], q2.at[(*block(x), in_pair)]),
        (vs.at[0, :, own_slab], v2.at[(*block(x), in_pair)]),
        (cx.at[0], ctx.at[x]),
        (wo.at[0], wv),
    ):
        loads.append(pltpu.make_async_copy(src, dst, lsem.at[len(loads)]))
    for copy in loads:
        copy.start()

    barrier = pltpu.get_barrier_semaphore()
    for dev in (dev_r, dev_l, dev_z, dev_a, dev_b, dev_c):
        pl.semaphore_signal(barrier, inc=1, device_id=dev, device_id_type=MESH)

    @pl.when(has_next)
    def _():
        pl.semaphore_signal(barrier, inc=1, device_id=dev_next, device_id_type=MESH)

    dka[...] = jnp.zeros_like(dka)
    dva[...] = jnp.zeros_like(dva)
    pl.semaphore_wait(barrier, 6 + has_prev.astype(jnp.int32))

    def slot(yy, zz, q):
        return inc.at[zz, pl.ds(pl.multiple_of(PIECE * yy + CHUNK * q, CHUNK), CHUNK)]

    groups = [(z, y // 2), (z, 1 - y // 2), (zp, y // 2), (zp, 1 - y // 2)]

    moves = {}

    def move(tag, src, there, here, dev):
        moves[tag] = (len(moves), src, there, here, dev)

    def sums_of(k):
        return (partb, got_a, sumb, got_b) if k < 3 else (partb1, got_a1, sumb1, got_b1)

    for q in range(CHUNKS):
        move("E%d" % q, bg.at[0, pl.ds(CHUNK * q, CHUNK)], slot(y, z, q), slot(y, z, q), dev_prev)
        move("z%d" % q, slot(y, z, q), slot(y, z, q), slot(y, zp, q), dev_z)
        move("l_own%d" % q, slot(y, z, q), slot(y, z, q), slot(y_l, z, q), dev_r)
        move("r_own%d" % q, slot(y, z, q), slot(y, z, q), slot(y_r, z, q), dev_l)
        move("l_oth%d" % q, slot(y, zp, q), slot(y, zp, q), slot(y_l, zp, q), dev_r)
        move("r_oth%d" % q, slot(y, zp, q), slot(y, zp, q), slot(y_r, zp, q), dev_l)
        if q < CHUNKS // 2:
            move("o_own%d" % q, slot(y_l, z, q), slot(y_l, z, q), slot(y_o, z, q), dev_r)
            move("o_oth%d" % q, slot(y_o, z, q), slot(y_o, z, q), slot(y_o, zp, q), dev_z)
        else:
            move("o_own%d" % q, slot(y_r, z, q), slot(y_r, z, q), slot(y_o, z, q), dev_l)
            move("o_oth%d" % q, slot(y_r, zp, q), slot(y_r, zp, q), slot(y_o, zp, q), dev_l)

    for n, a, b in (("k", ks, k2), ("q", qs, q2), ("v", vs, v2)):
        to, from_a, from_b, from_c = block(x), block(x_a), block(x_b), block(x_c)
        move(n + "A", a.at[0, :, pair_of(x_a)], b.at[to], b.at[from_a], dev_a)
        move(n + "B", a.at[0, :, slab_of(x_b)], b.at[(*to, in_pair_b)], b.at[(*from_b, in_pair)], dev_b)
        move(n + "C", b.at[(*from_a, in_pair_b)], b.at[(*from_a, in_pair_b)], b.at[(*from_c, in_pair)], dev_b)
    move("cA", cx.at[0], ctx.at[x], ctx.at[x_a], dev_a)
    move("cB", cx.at[0], ctx.at[x], ctx.at[x_b], dev_b)
    lo, hi = pl.ds(0, LOW), pl.ds(LOW, ROWS - LOW)
    move("cC0", ctx.at[x_a, lo], ctx.at[x_a, lo], ctx.at[x_c, lo], dev_b)
    move("cC1", ctx.at[x_b, hi], ctx.at[x_b, hi], ctx.at[x_c, hi], dev_a)
    for k in range(5):
        src, first, total, second = (r.at[k] if k < 3 else r.at[k - 3] for r in (sums_of(k)))
        move("rsA%d" % k, src.at[pair_of(x_a)], first, first, dev_a)
        move("rsB%d" % k, total, second, second, dev_b)

    def move_out(n, src, dst, start, size):
        rows = pl.ds(start, size)
        to_a, to_b, to_c = (block(xx, start, size) for xx in (x_a, x_b, x_c))
        move(n + "A", src.at[to_a], dst.at[0, rows, own_slab], dst.at[0, rows, slab_of(x_a)], dev_a)
        move(n + "B", src.at[(*to_b, own_full)], dst.at[0, rows, full_of(x)], dst.at[0, rows, full_of(x_b)], dev_b)
        move(n + "C", src.at[(*to_c, own_full)], dst.at[0, rows, full_of(x)], dst.at[0, rows, full_of(x_c)], dev_c)

    move_out("dk", dkb, gk, 0, ROWS)
    move_out("dv", dvb, gv, 0, ROWS)
    move_out("dqe", dqb, gq, m128(PIECE * z), PIECE)
    move_out("dql", dqb, gq, m128(PIECE * zp), PIECE)

    def outgoing(tag):
        i, src, there, _, dev = moves[tag]
        return pltpu.make_async_remote_copy(src, there, send.at[i], recv.at[i], device_id=dev, device_id_type=MESH)

    def arriving(tag):
        i, _, _, here, dev = moves[tag]
        return pltpu.make_async_remote_copy(here, here, send.at[i], recv.at[i], device_id=dev, device_id_type=MESH)

    def entry_kept(q):
        return pltpu.make_async_copy(bg.at[0, pl.ds(CHUNK * q, CHUNK)], slot(y, z, q), esem.at[q])

    def emit_send(tag):
        if tag[0] == "E":
            h = int(tag[1])

            @pl.when(has_prev)
            def _():
                outgoing(tag).start()

            @pl.when(jnp.logical_not(has_next))
            def _():
                entry_kept(h).start()
        else:
            outgoing(tag).start()

    def emit_wait(tag):
        if tag[0] == "E":
            h = int(tag[1])

            @pl.when(has_next)
            def _():
                arriving(tag).wait_recv()

            @pl.when(jnp.logical_not(has_next))
            def _():
                entry_kept(h).wait()
        elif tag[0] == "@":
            loads[int(tag[1])].wait()
        else:
            arriving(tag).wait_recv()

    def group_rows(g):
        zz, p = g
        return p, zz, pl.ds(m128(PIECE * zz), PIECE), pl.ds(m128(ROWS + PIECE * zz), PIECE)

    def partial_grad(k):
        if k < 3:
            zz, p = groups[k]
            r = dot(wv[...], inc[zz, pl.ds(pl.multiple_of(ROWS * p, ROWS), ROWS)], 1, 1)
            part[k] = r
            partb[k] = r.astype(BF16)
        else:
            yy = (y_n, y_o)[k - 3]
            r = dot(wv[...], inc[zp, pl.ds(m128(PIECE * yy), PIECE)], 1, 1)
            part1[k - 3] = r
            partb1[k - 3] = r.astype(BF16)

    def pass_on(k):
        if k < 3:
            sumb[k] = (part[k, slab_of(x_b)] + got_a[k, in_pair_b].astype(F32)).astype(BF16)
        else:
            i = k - 3
            sumb1[i] = (part1[i, slab_of(x_b)] + got_a1[i, in_pair_b].astype(F32)).astype(BF16)

    heads = [pl.ds(HEAD * h, HEAD) for h in range(2)]
    pheads = [pl.ds(m128(HEAD * (par + h)), HEAD) for h in range(2)]

    def softmax(k):
        p, zz, rows0, rows1 = group_rows(groups[k])
        row = lax.broadcasted_iota(jnp.int32, (KEYS, ROWS), 0)
        lane = lax.broadcasted_iota(jnp.int32, (KEYS, ROWS), 1)
        ahead = jnp.where(lane < PIECE, lane, lane + PIECE) - row
        if k == 0:
            for j in range(2):
                for h in range(2):
                    kt[j, heads[h]] = k2[j, :, pheads[h]].T
        for h in range(2):
            qg[k, 0:PIECE, heads[h]] = q2[p, rows0, pheads[h]]
            qg[k, PIECE:ROWS, heads[h]] = q2[p, rows1, pheads[h]]

        def scores(j, tops):
            result = []
            ok = ahead >= KEYS * (j - p) - PIECE * zz
            for h in range(2):
                sc = dot(k2[j, :, pheads[h]], qg[k, :, heads[h]], 1, 1)
                sc = jnp.where(ok, sc, -jnp.inf)
                pt[h, k, j] = sc
                result.append(jnp.maximum(tops[h], jnp.max(sc, axis=0, keepdims=True)))
            return tuple(result)

        low = jnp.full((1, ROWS), -jnp.inf, F32)
        tops = lax.fori_loop(0, p + 1, scores, (low, low))

        def weights(j, sums):
            result = []
            for h in range(2):
                e = jnp.exp2((pt[h, k, j] - tops[h]) * EXP_SCALE)
                pt[h, k, j] = e
                result.append(sums[h] + jnp.sum(e, axis=0, keepdims=True))
            return tuple(result)

        none = jnp.zeros((1, ROWS), F32)
        sums = lax.fori_loop(0, p + 1, weights, (none, none))
        for h in range(2):
            linv[k, h : h + 1] = 1.0 / sums[h]

    def turn(k):
        p, _, rows, _ = group_rows(groups[k])
        ctxt[k // 2, :, pl.ds(m128(ROWS * p), PIECE)] = ctx[2 * p, rows].T
        ctxt[k // 2, :, pl.ds(m128(ROWS * p + PIECE), PIECE)] = ctx[2 * p + 1, rows].T

    def weight_grad(i, half):
        zz = (z, zp)[i]

        @pl.loop(0, FEAT // TILE // 2)
        def _(n):
            cols = pl.ds(pl.multiple_of(half * (FEAT // 2) + n * TILE, TILE), TILE)
            r = dot(ctxt[i], inc[zz, :, cols], 1, 0)
            if i == 0:
                acc[:, cols] = r
            else:
                gw[0, :, cols] = (r + acc[:, cols]).astype(BF16)

    def attend(k):
        p, _, rows0, rows1 = group_rows(groups[k])
        if k < 3:
            dout[...] = (part[k, own_slab] + got_a[k, in_pair].astype(F32) + got_b[k].astype(F32)).astype(BF16)
        else:
            for i, yy in enumerate((y_n, y_o)):
                r = part1[i, own_slab] + got_a1[i, in_pair].astype(F32) + got_b1[i].astype(F32)
                dout[:, pl.ds(m128(PIECE * lax.rem(yy, 2)), PIECE)] = r.astype(BF16)
        tokens = pl.ds(pl.multiple_of(ROWS * p, ROWS), ROWS)
        prod = dout[...].astype(F32) * ctxt[k // 2, own_slab, tokens].astype(F32)
        deltas = [jnp.sum(prod[HEAD * h : HEAD * (h + 1)], axis=0, keepdims=True) for h in range(2)]
        inv = [linv[k, h : h + 1] for h in range(2)]
        dqa[...] = jnp.zeros_like(dqa)

        @pl.loop(0, p + 1)
        def _(j):
            for h in range(2):
                gh = dout[heads[h]]
                w = pt[h, k, j] * inv[h]
                dp = dot(v2[j, :, pheads[h]], gh, 1, 0)
                ds = (w * (dp - deltas[h])).astype(BF16)
                dva[j, :, heads[h]] += dot(w.astype(BF16), gh, 1, 1)
                dka[j, :, heads[h]] += dot(ds, qg[k, :, heads[h]], 1, 0)
                dqa[heads[h]] += dot(kt[j, heads[h]], ds, 1, 0)

        dq = (dqa[...] * SCALE).astype(BF16).T
        dqb[p, rows0] = dq[0:PIECE]
        dqb[p, rows1] = dq[PIECE:ROWS]

    def cast_keys():
        dkb[...] = (dka[...] * SCALE).astype(BF16)

    def cast_values():
        dvb[...] = dva[...].astype(BF16)

    def early_sent():
        for tag in moves:
            if tag[0] == "E":

                @pl.when(has_prev)
                def _():
                    outgoing(tag).wait_send()
            elif tag[:2] not in LAST:
                outgoing(tag).wait_send()

    table = {
        "cA": ([], None, ["cA"]),
        "cB": ([], None, ["cB"]),
        "cfA": (["cA"], None, ["cC0"]),
        "cfB": (["cB"], None, ["cC1"]),
        "dq": ([], None, ["dqeC", "dqeA", "dqeB"]),
        "dk": ([], cast_keys, ["dkC", "dkA", "dkB"]),
        "dv": ([], cast_values, ["dvC", "dvA", "dvB"]),
        "dql": ([], None, ["dqlC", "dqlA", "dqlB"]),
        "sent": ([], early_sent, []),
        "gA": ([], lambda: weight_grad(0, 0), []),
        "gB": ([], lambda: weight_grad(0, 1), []),
        "gC": ([], lambda: weight_grad(1, 0), []),
        "gD": ([], lambda: weight_grad(1, 1), []),
    }
    for n in "kqv":
        table[n] = ([], None, [n + "A", n + "B"])
        table[n + "f"] = ([n + "A"], None, [n + "C"])
    own, near, far, near_z, far_z = [], [], [], [], []
    for q in range(CHUNKS):
        i = str(q)
        first = q < CHUNKS // 2
        table["E" + i] = ([], None, ["E" + i])
        table["r" + i] = (["E" + i], None, ["l_own" + i])
        table["l" + i] = (["E" + i], None, ["r_own" + i])
        table["z" + i] = (["E" + i], None, ["z" + i])
        table["R" + i] = (["z" + i], None, ["l_oth" + i])
        table["L" + i] = (["z" + i], None, ["r_oth" + i])
        table["f" + i] = (["l_own" + i] if first else ["r_own" + i], None, ["o_own" + i])
        table["F" + i] = (["o_own" + i] if first else ["r_oth" + i], None, ["o_oth" + i])
        own += ["E" + i]
        near += ["l_own" + i, "r_own" + i]
        far += ["o_own" + i]
        near_z += ["z" + i, "l_oth" + i, "r_oth" + i]
        far_z += ["o_oth" + i]
    for k, need in enumerate((["@4"] + own + near, far, near_z, near_z, far_z)):
        table["p%d" % k] = (need, lambda k=k: partial_grad(k), ["rsA%d" % k])
        table["s%d" % k] = (["rsA%d" % k], lambda k=k: pass_on(k), ["rsB%d" % k])
    for k in range(4):
        sums = ["rsB%d" % k] if k < 3 else ["rsB3", "rsB4"]
        table["P%d" % k] = (["@0", "@1", "kA", "kB", "kC", "qA", "qB", "qC"], lambda k=k: softmax(k), [])
        table["t%d" % k] = (["@3", "cA", "cB", "cC0", "cC1"], lambda k=k: turn(k), [])
        table["a%d" % k] = (["@2", "vA", "vB", "vC"] + sums, lambda k=k: attend(k), [])

    def perform(order):
        seen = set()
        for name in order:
            waits, work, sends = table[name]
            for tag in waits:
                if tag not in seen:
                    seen.add(tag)
                    emit_wait(tag)
            if work is not None:
                work()
            for tag in sends:
                emit_send(tag)
        for n, (b, g) in enumerate(((dqb, gq), (dkb, gk), (dvb, gv))):
            pltpu.make_async_copy(b.at[block(x)], g.at[0, :, own_slab], osem.at[n]).start()

    for n, order in enumerate((ORDER0, ORDER1)):
        pl.when(core == n)(lambda order=order: perform(order))

    for n in ("dqe", "dk", "dv", "dql"):
        for tail in "ABC":
            emit_wait(n + tail)
    for n, (b, g) in enumerate(((dqb, gq), (dkb, gk), (dvb, gv))):
        pltpu.make_async_copy(b.at[block(x)], g.at[0, :, own_slab], osem.at[n]).wait()
    for tag in moves:
        if tag[:2] in LAST:
            outgoing(tag).wait_send()


N_MOVES = 8 * CHUNKS + 9 + 4 + 10 + 12


def write_out(gw, gq, gk, gv, gw_out, gq_out, gk_out, gv_out, sems):
    copies = []
    for n in range(6):
        rows = pl.ds(n * (WIDTH // 6), WIDTH // 6)
        copies.append(pltpu.make_async_copy(gw.at[0, rows], gw_out.at[0, rows], sems.at[n]))
    for n, (src, dst) in enumerate(((gq, gq_out), (gk, gk_out), (gv, gv_out))):
        copies.append(pltpu.make_async_copy(src, dst, sems.at[6 + n]))
    for copy in copies:
        copy.start()
    for copy in copies:
        copy.wait()


def local(boundary_grad, w_out, context, queries, keys, values):
    any_spec = pl.BlockSpec(memory_space=pl.ANY)
    vmem_spec = pl.BlockSpec(memory_space=pltpu.VMEM)
    shapes = [(1, WIDTH, FEAT), (1, ROWS, WIDTH), (1, ROWS, WIDTH), (1, ROWS, WIDTH)]
    grads = pl.pallas_call(
        kernel,
        out_shape=[pltpu.VMEM(shape, BF16) for shape in shapes],
        in_specs=[any_spec] * 6,
        out_specs=[vmem_spec] * 4,
        scratch_shapes=[
            pltpu.VMEM((2, KEYS, FEAT), BF16),
            pltpu.VMEM((WIDTH, FEAT), BF16),
            pltpu.VMEM((4, ROWS, WIDTH), BF16),
            pltpu.VMEM((2, WIDTH, KEYS), BF16),
            pltpu.VMEM((WIDTH, FEAT), F32),
            pltpu.VMEM((2, KEYS, PAIR), BF16),
            pltpu.VMEM((2, KEYS, PAIR), BF16),
            pltpu.VMEM((2, KEYS, PAIR), BF16),
            pltpu.VMEM((4, ROWS, SLAB), BF16),
            pltpu.VMEM((3, WIDTH, ROWS), F32),
            pltpu.VMEM((3, WIDTH, ROWS), BF16),
            pltpu.VMEM((3, PAIR, ROWS), BF16),
            pltpu.VMEM((3, SLAB, ROWS), BF16),
            pltpu.VMEM((3, SLAB, ROWS), BF16),
            pltpu.VMEM((2, WIDTH, PIECE), F32),
            pltpu.VMEM((2, WIDTH, PIECE), BF16),
            pltpu.VMEM((2, PAIR, PIECE), BF16),
            pltpu.VMEM((2, SLAB, PIECE), BF16),
            pltpu.VMEM((2, SLAB, PIECE), BF16),
            pltpu.VMEM((2, SLAB, KEYS), BF16),
            pltpu.VMEM((2, 4, 2, KEYS, ROWS), F32),
            pltpu.VMEM((4, 8, ROWS), F32),
            pltpu.VMEM((ROWS, SLAB), BF16),
            pltpu.VMEM((ROWS, SLAB), F32),
            pltpu.VMEM((2, KEYS, SLAB), F32),
            pltpu.VMEM((2, KEYS, SLAB), F32),
            pltpu.VMEM((2, KEYS, SLAB), BF16),
            pltpu.VMEM((2, KEYS, SLAB), BF16),
            pltpu.VMEM((2, KEYS, SLAB), BF16),
            pltpu.SemaphoreType.DMA((N_MOVES,)),
            pltpu.SemaphoreType.DMA((N_MOVES,)),
            pltpu.SemaphoreType.DMA((5,)),
            pltpu.SemaphoreType.DMA((CHUNKS,)),
            pltpu.SemaphoreType.DMA((3,)),
        ],
        compiler_params=pltpu.CompilerParams(
            collective_id=0, has_side_effects=True, vmem_limit_bytes=54 * 1024 * 1024
        ),
    )(boundary_grad, w_out, context, queries, keys, values)
    return pl.pallas_call(
        write_out,
        out_shape=[jax.ShapeDtypeStruct(shape, BF16) for shape in shapes],
        in_specs=[any_spec] * 4,
        out_specs=[any_spec] * 4,
        scratch_shapes=[pltpu.SemaphoreType.DMA((9,))],
        compiler_params=pltpu.CompilerParams(vmem_limit_bytes=1024 * 1024),
    )(*grads)


def solution(mesh):
    in_specs = (
        P("section", "col", "row"),
        P("section", "col", "row"),
        P("section", "row", "col"),
        P("section", "row", "col"),
        P("section", "row", "col"),
        P("section", "row", "col"),
    )
    out_specs = (
        P("section", "col", "row"),
        P("section", "row", "col"),
        P("section", "row", "col"),
        P("section", "row", "col"),
    )
    return jax.shard_map(local, mesh=mesh, in_specs=in_specs, out_specs=out_specs, check_vma=False)
```
